32 devices in a mesh: dp: 8 (over y, x, core), seq: 4 (over z).
Axes of the slice: x: 2, y: 2, z: 4, core: 2. Of those that a mesh axis runs over, the one named last changes fastest.
Arguments:
- enc_input: bfloat16 [32, 1024, 512], P('dp', 'seq'), may hold values from -6 to 6
- dec_input: bfloat16 [32, 100, 512], P('dp', 'seq'), may hold values from -6 to 6
- targets: float32 [32, 100, 14], P('dp', 'seq'), may hold values from -6 to 6
- lengths: int32 [32], P('dp'), may hold values from 1 to 100, as said below
- attention_mats: float32 [12, 512, 512], P(None, ('dp', 'seq')), may hold values from -1.8856181 to 1.8856181
- expand_mats: float32 [2, 512, 3200], P(None, ('dp', 'seq')), may hold values from -0.25 to 0.25
- reduce_mats: float32 [2, 3200, 512], P(None, None, ('dp', 'seq')), may hold values from -0.109375 to 0.109375
- action_head: float32 [512, 14], P(('dp', 'seq')), may hold values from -0.25 to 0.25
- query_pos: float32 [100, 512], P(None, ('dp', 'seq')), may hold values from -3 to 3
- vectors: float32 [21, 512], P(None, ('dp', 'seq')), may hold values from -1.2 to 1.4, as said below
- expand_bias: float32 [6400], P(('dp', 'seq')), may hold values from -1 to 1
- first_attention: float32 [12, 512, 512], P(None, ('dp', 'seq')), may hold values from -0.875 to 0.875
- first_expand: float32 [2, 512, 3200], P(None, ('dp', 'seq')), may hold values from -0.875 to 0.875
- first_reduce: float32 [2, 3200, 512], P(None, None, ('dp', 'seq')), may hold values from -0.875 to 0.875
- first_head: float32 [512, 14], P(('dp', 'seq')), may hold values from -3.5 to 3.5
- first_query: float32 [100, 512], P(None, ('dp', 'seq')), may hold values from -0.01953125 to 0.01953125
- first_vectors: float32 [21, 512], P(None, ('dp', 'seq')), may hold values from -1.75 to 1.75
- first_bias: float32 [6400], P(('dp', 'seq')), may hold values from -0.4375 to 0.4375
- second_attention: float32 [12, 512, 512], P(None, ('dp', 'seq')), may hold values from 0.00016 to 0.00256
- second_expand: float32 [2, 512, 3200], P(None, ('dp', 'seq')), may hold values from 0.00016 to 0.00256
- second_reduce: float32 [2, 3200, 512], P(None, None, ('dp', 'seq')), may hold values from 0.00016 to 0.00256
- second_head: float32 [512, 14], P(('dp', 'seq')), may hold values from 0.00256 to 0.04096
- second_query: float32 [100, 512], P(None, ('dp', 'seq')), may hold values from 6.4e-08 to 1.024e-06
- second_vectors: float32 [21, 512], P(None, ('dp', 'seq')), may hold values from 0.00064 to 0.01024
- second_bias: float32 [6400], P(('dp', 'seq')), may hold values from 4e-05 to 0.00064
Outputs:
- enc_input_grad: bfloat16 [32, 1024, 512], P('dp', 'seq')
- dec_input_grad: bfloat16 [32, 100, 512], P('dp', 'seq')
- first_attention_new: float32 [12, 512, 512], P(None, ('dp', 'seq'))
- second_attention_new: float32 [12, 512, 512], P(None, ('dp', 'seq'))
- attention_master: float32 [12, 512, 512], P(None, ('dp', 'seq'))
- attention_half: bfloat16 [12, 512, 512], P(None, ('dp', 'seq'))
- first_expand_new: float32 [2, 512, 3200], P(None, ('dp', 'seq'))
- second_expand_new: float32 [2, 512, 3200], P(None, ('dp', 'seq'))
- expand_master: float32 [2, 512, 3200], P(None, ('dp', 'seq'))
- expand_half: bfloat16 [2, 512, 3200], P(None, ('dp', 'seq'))
- first_reduce_new: float32 [2, 3200, 512], P(None, None, ('dp', 'seq'))
- second_reduce_new: float32 [2, 3200, 512], P(None, None, ('dp', 'seq'))
- reduce_master: float32 [2, 3200, 512], P(None, None, ('dp', 'seq'))
- reduce_half: bfloat16 [2, 3200, 512], P(None, None, ('dp', 'seq'))
- first_head_new: float32 [512, 14], P(('dp', 'seq'))
- second_head_new: float32 [512, 14], P(('dp', 'seq'))
- head_master: float32 [512, 14], P(('dp', 'seq'))
- head_half: bfloat16 [512, 14], P(('dp', 'seq'))
- first_query_new: float32 [100, 512], P(None, ('dp', 'seq'))
- second_query_new: float32 [100, 512], P(None, ('dp', 'seq'))
- query_master: float32 [100, 512], P(None, ('dp', 'seq'))
- query_half: bfloat16 [100, 512], P(None, ('dp', 'seq'))
- first_vectors_new: float32 [21, 512], P(None, ('dp', 'seq'))
- second_vectors_new: float32 [21, 512], P(None, ('dp', 'seq'))
- vectors_master: float32 [21, 512], P(None, ('dp', 'seq'))
- vectors_half: bfloat16 [21, 512], P(None, ('dp', 'seq'))
- first_bias_new: float32 [6400], P(('dp', 'seq'))
- second_bias_new: float32 [6400], P(('dp', 'seq'))
- bias_master: float32 [6400], P(('dp', 'seq'))
- bias_half: bfloat16 [6400], P(('dp', 'seq'))
The draws below stay inside these ranges and needn't reach their ends.
Inputs may be any that keep to these rules, and one draw needn't show every extreme that they name: `lengths`: in each aligned group of 4 items one item has all 100 steps valid. `vectors`: rows 3, 6, 11, 16 and 19 are LayerNorm gains, the other rows biases and shifts.
All inputs are finite; a program needn't handle non-finite values.
Results may differ from the reference program's by a relative error of at most 0.02.
Values may be sent and summed in bfloat16 or wider, within the bound.
No kernel may reach another device: no remote copies, remote signals or barrier semaphores. Data moves between devices by JAX's collectives and lax.ppermute only.
A program may use at most 256 MiB of HBM per device.

```python
import math
import jax
import jax.numpy as jnp
from jax import lax

D = 512
FF = 3200
HEADS = 8
HDIM = 64
QLEN = 100
A = 14
STEP = 10
IT_DEV = 4
ITEMS = 32
S_ENC = 1024


def draw_lengths(key, part):
    key = jax.random.fold_in(key, 11)
    drawn = jax.random.randint(key, (ITEMS,), 1, QLEN + 1)
    chosen = jax.random.randint(jax.random.fold_in(key, 1), (ITEMS // IT_DEV,), 0, IT_DEV)
    filled = jnp.arange(ITEMS) % IT_DEV == jnp.repeat(chosen, IT_DEV, total_repeat_length=ITEMS)
    return jnp.where(filled, QLEN, drawn).astype(jnp.int32)


def draw_attention_mats(key, part):
    key = jax.random.fold_in(key, 5)
    entries = jax.random.truncated_normal(key, -4.0, 4.0, (12, D, D), jnp.float32) * D ** (-0.5)
    index_row = jnp.arange(12)
    wide_scale = max(1.0, S_ENC ** 0.5 / 3.0)
    short_scale = max(1.0, QLEN ** 0.5 / 3.0)
    scale = jnp.where((index_row == 3) | (index_row == 11), wide_scale, 1.0)
    scale = jnp.where(index_row == 7, short_scale, scale)
    return (entries * scale[:, None, None]).astype(jnp.float32)


def draw_vectors(key, part):
    key = jax.random.fold_in(key, 7)
    index_row = jnp.arange(21)
    gain_rows = (index_row == 3) | (index_row == 6) | (index_row == 11) | (index_row == 16) | (index_row == 19)
    gains = jax.random.uniform(key, (21, D), jnp.float32, 0.6, 1.4)
    shifts = jax.random.truncated_normal(jax.random.fold_in(key, 1), -4.0, 4.0, (21, D), jnp.float32) * 0.3
    return jnp.where(gain_rows[:, None], gains, shifts).astype(jnp.float32)


def shard_levels(key, shape, pieces, low, high):
    def one(dim, shards_of):
        heights = jax.random.uniform(jax.random.fold_in(jax.random.fold_in(key, 6), dim), (shards_of,), jnp.float32, low / len(pieces), high / len(pieces))
        return jnp.repeat(jnp.exp(heights), shape[dim] // shards_of).reshape((-1,) + (1,) * (len(shape) - dim - 1))

    level = one(*pieces[0])
    for cut in pieces[1:]:
        level = level * one(*cut)
    return level


def gaussian(own_key, dims, scale, reach, cuts=(), kind=jnp.bfloat16):
    values = scale * jax.random.normal(own_key, dims, jnp.float32)
    if cuts:
        values = values * shard_levels(own_key, dims, cuts, -0.22, 0.18)
    return jnp.clip(values, -reach, reach).astype(kind)


def setup_inputs(seed: int = 0) -> dict:
    streams_of = jax.random.split(jax.random.key(seed), 26)
    enc_input = gaussian(streams_of[0], (ITEMS, S_ENC, D), 1.0, 6.0, ((0, 8), (1, 4)))
    dec_input = gaussian(streams_of[1], (ITEMS, QLEN, D), 1.0, 6.0, ((0, 8), (1, 4)))
    targets = gaussian(streams_of[2], (ITEMS, QLEN, A), 1.0, 6.0, ((0, 8), (1, 4)), jnp.float32)
    lengths = draw_lengths(jax.random.fold_in(streams_of[25], 71), 0)
    attention_mats = draw_attention_mats(jax.random.fold_in(streams_of[25], 71), 0)
    expand_mats = gaussian(streams_of[5], (2, D, FF), D ** -0.5, 0.25, ((1, 32),), jnp.float32)
    reduce_mats = gaussian(streams_of[6], (2, FF, D), FF ** -0.5, 0.109375, ((2, 32),), jnp.float32)
    action_head = gaussian(streams_of[7], (D, A), D ** -0.5, 0.25, ((0, 32),), jnp.float32)
    query_pos = gaussian(streams_of[8], (QLEN, D), 0.5, 3.0, ((1, 32),), jnp.float32)
    vectors = draw_vectors(jax.random.fold_in(streams_of[25], 71), 0)
    expand_bias = gaussian(streams_of[10], (2 * FF,), 0.2, 1.0, ((0, 32),), jnp.float32)
    first_attention = gaussian(streams_of[11], (12, D, D), (0.0011 * (ITEMS * QLEN) ** 0.5), 0.875, ((1, 32),), jnp.float32)
    first_expand = gaussian(streams_of[12], (2, D, FF), (0.0011 * (ITEMS * QLEN) ** 0.5), 0.875, ((1, 32),), jnp.float32)
    first_reduce = gaussian(streams_of[13], (2, FF, D), (0.0011 * (ITEMS * QLEN) ** 0.5), 0.875, ((2, 32),), jnp.float32)
    first_head = gaussian(streams_of[14], (D, A), (0.0044 * (ITEMS * QLEN) ** 0.5), 3.5, ((0, 32),), jnp.float32)
    first_query = gaussian(streams_of[15], (QLEN, D), (0.00022 * ITEMS ** 0.5), 0.01953125, ((1, 32),), jnp.float32)
    first_vectors = gaussian(streams_of[16], (21, D), (0.0022 * (ITEMS * QLEN) ** 0.5), 1.75, ((1, 32),), jnp.float32)
    first_bias = gaussian(streams_of[17], (2 * FF,), (0.00055 * (ITEMS * QLEN) ** 0.5), 0.4375, ((0, 32),), jnp.float32)
    second_attention = jnp.clip(jnp.exp(math.log(0.00256) - 2.7725887 * jax.random.uniform(streams_of[18], (12, D, D), jnp.float32) ** shard_levels(streams_of[18], (12, D, D), ((1, 32),), -0.2, 0.2)), 0.00016, 0.00256)
    second_expand = jnp.clip(jnp.exp(math.log(0.00256) - 2.7725887 * jax.random.uniform(streams_of[19], (2, D, FF), jnp.float32) ** shard_levels(streams_of[19], (2, D, FF), ((1, 32),), -0.2, 0.2)), 0.00016, 0.00256)
    second_reduce = jnp.clip(jnp.exp(math.log(0.00256) - 2.7725887 * jax.random.uniform(streams_of[20], (2, FF, D), jnp.float32) ** shard_levels(streams_of[20], (2, FF, D), ((2, 32),), -0.2, 0.2)), 0.00016, 0.00256)
    second_head = jnp.clip(jnp.exp(math.log(0.04096) - 2.7725887 * jax.random.uniform(streams_of[21], (D, A), jnp.float32) ** shard_levels(streams_of[21], (D, A), ((0, 32),), -0.2, 0.2)), 0.00256, 0.04096)
    second_query = jnp.clip(jnp.exp(math.log(1.0239999710393022e-06) - 2.7725887 * jax.random.uniform(streams_of[22], (QLEN, D), jnp.float32) ** shard_levels(streams_of[22], (QLEN, D), ((1, 32),), -0.2, 0.2)), 6.399999818995639e-08, 1.0239999710393022e-06)
    second_vectors = jnp.clip(jnp.exp(math.log(0.01024) - 2.7725887 * jax.random.uniform(streams_of[23], (21, D), jnp.float32) ** shard_levels(streams_of[23], (21, D), ((1, 32),), -0.2, 0.2)), 0.00064, 0.01024)
    second_bias = jnp.clip(jnp.exp(math.log(0.00064) - 2.7725887 * jax.random.uniform(streams_of[24], (2 * FF,), jnp.float32) ** shard_levels(streams_of[24], (2 * FF,), ((0, 32),), -0.2, 0.2)), 3.9999998989515007e-05, 0.00064)
    return {"enc_input": enc_input, "dec_input": dec_input, "targets": targets, "lengths": lengths, "attention_mats": attention_mats, "expand_mats": expand_mats, "reduce_mats": reduce_mats, "action_head": action_head, "query_pos": query_pos, "vectors": vectors, "expand_bias": expand_bias, "first_attention": first_attention, "first_expand": first_expand, "first_reduce": first_reduce, "first_head": first_head, "first_query": first_query, "first_vectors": first_vectors, "first_bias": first_bias, "second_attention": second_attention, "second_expand": second_expand, "second_reduce": second_reduce, "second_head": second_head, "second_query": second_query, "second_vectors": second_vectors, "second_bias": second_bias}


@jax.custom_vjp
def low(v):
    return lax.optimization_barrier(v.astype(jnp.bfloat16)).astype(jnp.float32)

@jax.custom_vjp
def low_back(v):
    return v

def low_keep(v):
    return (low(v), None)

def low_pass(kept, grad):
    return (grad,)

def back_keep(v):
    return (v, None)

def back_low(kept, grad):
    return (low(grad),)
low.defvjp(low_keep, low_pass)
low_back.defvjp(back_keep, back_low)
beta_first = 0.9
beta_second = 0.999
epsilon = 1e-08
decay_rate = 0.1
rate_matrix = 0.08
rate_vector = 0.2

def highest(left, right):
    return jnp.matmul(left, right, precision=lax.Precision.HIGHEST)

def layer_norm(values, gain, shift):
    center = values - lax.optimization_barrier(jnp.mean(values, axis=-1, keepdims=True))
    spread = lax.optimization_barrier(jnp.mean(center * center, axis=-1, keepdims=True))
    return center * lax.rsqrt(spread + 1e-05) * gain + shift

def sine_table(places, width):
    halves = jnp.arange(width // 2).astype(jnp.float32)
    frequency = jnp.exp(halves * (-2.0 * math.log(10000.0) / width))
    angles = places[:, None] * frequency[None, :]
    return jnp.stack([jnp.sin(angles), jnp.cos(angles)], axis=-1).reshape(places.shape[0], width)

def attention(query, keys, values):
    query_heads = query.reshape(query.shape[0], HEADS, HDIM)
    key_heads = keys.reshape(keys.shape[0], HEADS, HDIM)
    value_heads = values.reshape(values.shape[0], HEADS, HDIM)
    raw = low_back(jnp.einsum('qhd,khd->hqk', query_heads, key_heads, precision=lax.Precision.HIGHEST))
    probs = low(jax.nn.softmax(raw * HDIM ** (-0.5), axis=-1))
    mixed = jnp.einsum('hqk,khd->qhd', probs, value_heads, precision=lax.Precision.HIGHEST)
    return low(low_back(mixed.reshape(query.shape[0], HEADS * HDIM)))

def forward(params, enc_item, dec_item, target_item, length):
    mats = low(params[0])
    expand_low = low(params[1])
    reduce_low = low(params[2])
    head_low = low(params[3])
    query_low = low(params[4])
    vector_low = low(params[5])
    bias_low = low(params[6])
    positions = sine_table(jnp.arange(S_ENC).astype(jnp.float32), D)
    enc_in = low(enc_item + positions)
    enc_query = low(low_back(highest(enc_in, mats[0]) + vector_low[0]))
    enc_keys = low(low_back(highest(enc_in, mats[1])))
    enc_values = low(low_back(highest(enc_item, mats[2]) + vector_low[1]))
    enc_sum = enc_item + low_back(highest(attention(enc_query, enc_keys, enc_values), mats[3])) + vector_low[2]
    hidden = layer_norm(enc_sum, vector_low[3], vector_low[4])
    inner = low_back(highest(low(hidden), expand_low[0]) + bias_low[:FF])
    enc_two = hidden + low_back(highest(low(jax.nn.gelu(inner)), reduce_low[0])) + vector_low[5]
    memory = layer_norm(enc_two, vector_low[6], vector_low[7])
    self_in = low(dec_item + query_low)
    self_query = low(low_back(highest(self_in, mats[4]) + vector_low[8]))
    self_keys = low(low_back(highest(self_in, mats[5])))
    self_values = low(low_back(highest(dec_item, mats[6]) + vector_low[9]))
    dec_one = layer_norm(dec_item + low_back(highest(attention(self_query, self_keys, self_values), mats[7])) + vector_low[10], vector_low[11], vector_low[12])
    cross_in = low(dec_one + query_low)
    cross_query = low(low_back(highest(cross_in, mats[8]) + vector_low[13]))
    cross_keys = low(low_back(highest(low(memory + positions), mats[9])))
    cross_values = low(low_back(highest(low(memory), mats[10]) + vector_low[14]))
    dec_two = layer_norm(dec_one + low_back(highest(attention(cross_query, cross_keys, cross_values), mats[11])) + vector_low[15], vector_low[16], vector_low[17])
    dec_inner = low_back(highest(low(dec_two), expand_low[1]) + bias_low[FF:])
    dec_three = layer_norm(dec_two + low_back(highest(low(jax.nn.gelu(dec_inner)), reduce_low[1])) + vector_low[18], vector_low[19], vector_low[20])
    predicted = low_back(highest(low(dec_three), head_low))
    error = predicted - target_item
    valid = (jnp.arange(QLEN) < length).astype(jnp.float32)
    return jnp.sum((jnp.sqrt(error * error + 1.0) - 1.0) * valid[:, None]) / A

def adamw(weight, gradient, moment_one, moment_two, step_rate):
    moment_one = beta_first * moment_one + (1.0 - beta_first) * gradient
    moment_two = beta_second * moment_two + (1.0 - beta_second) * gradient * gradient
    mean_hat = moment_one / (1.0 - beta_first ** STEP)
    square_hat = moment_two / (1.0 - beta_second ** STEP)
    updated = weight - step_rate * (mean_hat / (jnp.sqrt(square_hat) + epsilon) + decay_rate * weight)
    return (moment_one, moment_two, updated, updated.astype(jnp.bfloat16))

def reference(enc_input, dec_input, targets, lengths, attention_mats, expand_mats, reduce_mats, action_head, query_pos, vectors, expand_bias, first_attention, first_expand, first_reduce, first_head, first_query, first_vectors, first_bias, second_attention, second_expand, second_reduce, second_head, second_query, second_vectors, second_bias):
    weights = (attention_mats, expand_mats, reduce_mats, action_head, query_pos, vectors, expand_bias)

    def one_item(totals, item):
        enc_item, dec_item, target_item, length = item

        def item_loss(params, enc_float, dec_float):
            return forward(params, enc_float, dec_float, target_item, length)
        loss_value, pullback = jax.vjp(item_loss, weights, enc_item.astype(jnp.float32), dec_item.astype(jnp.float32))
        item_grads, enc_grad, dec_grad = pullback(jnp.ones_like(loss_value))
        totals = jax.tree.map(jnp.add, totals, item_grads)
        return (totals, (enc_grad.astype(jnp.bfloat16), dec_grad.astype(jnp.bfloat16)))
    initial = tuple((jnp.zeros_like(weight) for weight in weights))
    totals, grads_pair = lax.scan(one_item, initial, (enc_input, dec_input, targets, lengths))
    firsts = (first_attention, first_expand, first_reduce, first_head, first_query, first_vectors, first_bias)
    seconds = (second_attention, second_expand, second_reduce, second_head, second_query, second_vectors, second_bias)
    rates = (rate_matrix, rate_matrix, rate_matrix, rate_matrix, rate_vector, rate_vector, rate_vector)
    outputs = [grads_pair[0], grads_pair[1]]
    for weight, gradient, moment_one, moment_two, step_rate in zip(weights, totals, firsts, seconds, rates):
        outputs.extend(adamw(weight, gradient, moment_one, moment_two, step_rate))
    return tuple(outputs)
```

```python
import functools
import math

import jax
import jax.numpy as jnp
import numpy as np
from jax import lax
from jax.experimental import pallas as pl
from jax.experimental.pallas import tpu as pltpu
from jax.sharding import PartitionSpec as P

HEADS = 8
HDIM = 64
STEP = 10
ALL = ("dp", "seq")

beta_first = 0.9
beta_second = 0.999
epsilon = 1e-08
decay_rate = 0.1
rate_matrix = 0.08
rate_vector = 0.2

BF = jnp.bfloat16
F32 = jnp.float32
MB = 1 << 20


def to_half(values):
    return values.astype(BF)


def mm(a, b):
    return lax.dot_general(a, b, (((1,), (0,)), ((), ())), preferred_element_type=F32)


def mm_t(a, b):
    return lax.dot_general(a, b, (((1,), (1,)), ((), ())), preferred_element_type=F32)


def t_mm(a, b):
    return lax.dot_general(a, b, (((0,), (0,)), ((), ())), preferred_element_type=F32)


def column_sum(values):
    return jnp.sum(values.astype(F32), axis=0)


def layer_norm(values, gain, shift):
    center = values - jnp.mean(values, axis=-1, keepdims=True)
    spread = jnp.mean(center * center, axis=-1, keepdims=True)
    return center * lax.rsqrt(spread + 1e-05) * gain + shift


def norm_back(values, gain, gradient):
    center = values - jnp.mean(values, axis=-1, keepdims=True)
    spread = jnp.mean(center * center, axis=-1, keepdims=True)
    scale = lax.rsqrt(spread + 1e-05)
    unit = center * scale
    inner = gradient * gain
    mean_inner = jnp.mean(inner, axis=-1, keepdims=True)
    mean_cross = jnp.mean(inner * unit, axis=-1, keepdims=True)
    back = scale * (inner - mean_inner - unit * mean_cross)
    return back, jnp.sum(gradient * unit, axis=0), jnp.sum(gradient, axis=0)


def gelu_back(inner, gradient):
    unused_out, pullback = jax.vjp(jax.nn.gelu, inner)
    return pullback(gradient)[0]


def sine_table(count, width):
    halves = np.arange(width // 2, dtype=np.float64)
    frequency = np.exp(halves * (-2.0 * math.log(10000.0) / width))
    angles = np.arange(count)[:, None] * frequency[None, :]
    table = np.stack([np.sin(angles), np.cos(angles)], axis=-1).reshape(count, width)
    return table.astype(np.float32)


def attend_kernel(q_ref, k_ref, v_ref, o_ref, log_ref, *, chunk):
    keys = k_ref[...]
    values_t = v_ref[...].T
    lane = lax.broadcasted_iota(jnp.int32, (chunk, 2 * HDIM), 1)
    row = lax.broadcasted_iota(jnp.int32, (2 * HDIM, chunk), 0)

    def step(i, carry):
        at = pl.ds(i * chunk, chunk)
        query = q_ref[at, :] * BF(HDIM ** (-0.5))
        mixed = []
        for h in range(2):
            own = jnp.where((lane < HDIM) == (h == 0), query, BF(0))
            scores = mm_t(keys, own)
            peak = jnp.max(scores, axis=0, keepdims=True)
            weights = jnp.exp(scores - peak)
            total = jnp.sum(weights, axis=0, keepdims=True)
            mixed.append(mm(values_t, weights.astype(BF)) / total)
            log_ref[0, pl.ds(h, 1), at] = peak + jnp.log(total)
        both = jnp.where(row < HDIM, mixed[0], mixed[1])
        o_ref[at, :] = both.T.astype(BF)
        return carry

    lax.fori_loop(0, q_ref.shape[0] // chunk, step, 0)


def attend(query, keys, values):
    rows, width = query.shape
    pairs = width // (2 * HDIM)
    spec = pl.BlockSpec((rows, 2 * HDIM), lambda i: (0, i))
    return pl.pallas_call(
        functools.partial(attend_kernel, chunk=256),
        grid=(pairs,),
        in_specs=[spec, spec, spec],
        out_specs=[spec, pl.BlockSpec((1, 2, rows), lambda i: (i, 0, 0))],
        out_shape=[
            jax.ShapeDtypeStruct((rows, width), BF),
            jax.ShapeDtypeStruct((pairs, 2, rows), F32),
        ],
        compiler_params=pltpu.CompilerParams(vmem_limit_bytes=48 * MB),
        cost_estimate=pl.CostEstimate(
            flops=16 * rows * rows * width, bytes_accessed=8 * rows * width, transcendentals=rows * rows * 8
        ),
    )(query, keys, values)


def attend_back_kernel(
    q_ref, k_ref, v_ref, o_ref, g_ref, log_ref, dq_ref, dk_ref, dv_ref, dk_acc, dv_acc, *, chunk
):
    keys = k_ref[...]
    keys_t = keys.T
    values = v_ref[...]
    lane = lax.broadcasted_iota(jnp.int32, (chunk, 2 * HDIM), 1)
    row = lax.broadcasted_iota(jnp.int32, (2 * HDIM, chunk), 0)
    scale = HDIM ** (-0.5)
    dk_acc[...] = jnp.zeros_like(dk_acc)
    dv_acc[...] = jnp.zeros_like(dv_acc)

    def step(i, carry):
        at = pl.ds(i * chunk, chunk)
        query = q_ref[at, :] * BF(scale)
        grad = g_ref[at, :]
        cross = (grad.astype(F32) * o_ref[at, :].astype(F32)).T
        query_grads = []
        for h in range(2):
            mine = (lane < HDIM) == (h == 0)
            own = jnp.where(mine, query, BF(0))
            own_grad = jnp.where(mine, grad, BF(0))
            weighted = jnp.sum(cross[h * HDIM : (h + 1) * HDIM], axis=0, keepdims=True)
            probs = jnp.exp(mm_t(keys, own) - log_ref[0, pl.ds(h, 1), at])
            prob_grad = mm_t(values, own_grad)
            score_grad = (probs * (prob_grad - weighted)).astype(BF)
            dv_acc[...] += mm(probs.astype(BF), own_grad)
            dk_acc[...] += mm(score_grad, own)
            query_grads.append(mm(keys_t, score_grad))
        both = jnp.where(row < HDIM, query_grads[0], query_grads[1]) * scale
        dq_ref[at, :] = both.T.astype(BF)
        return carry

    lax.fori_loop(0, q_ref.shape[0] // chunk, step, 0)
    dk_ref[...] = dk_acc[...].astype(BF)
    dv_ref[...] = dv_acc[...].astype(BF)


def attend_back(query, keys, values, mixed, grad, log_total):
    rows, width = query.shape
    pairs = width // (2 * HDIM)
    spec = pl.BlockSpec((rows, 2 * HDIM), lambda i: (0, i))
    return pl.pallas_call(
        functools.partial(attend_back_kernel, chunk=256),
        grid=(pairs,),
        in_specs=[spec] * 5 + [pl.BlockSpec((1, 2, rows), lambda i: (i, 0, 0))],
        out_specs=[spec] * 3,
        out_shape=[jax.ShapeDtypeStruct((rows, width), BF)] * 3,
        scratch_shapes=[pltpu.VMEM((rows, 2 * HDIM), F32)] * 2,
        compiler_params=pltpu.CompilerParams(vmem_limit_bytes=48 * MB),
        cost_estimate=pl.CostEstimate(
            flops=40 * rows * rows * width, bytes_accessed=16 * rows * width, transcendentals=rows * rows * 8
        ),
    )(query, keys, values, mixed, grad, log_total)


def heads_of(values):
    return values.reshape(values.shape[0], HEADS, HDIM)


def small_attend(query, keys, values):
    raw = jnp.einsum("qhd,khd->hqk", heads_of(query), heads_of(keys), preferred_element_type=F32)
    scores = raw * HDIM ** (-0.5)
    peak = jnp.max(scores, axis=-1, keepdims=True)
    weights = jnp.exp(scores - peak)
    probs = weights / jnp.sum(weights, axis=-1, keepdims=True)
    mixed = jnp.einsum("hqk,khd->qhd", to_half(probs), heads_of(values), preferred_element_type=F32)
    return to_half(mixed.reshape(query.shape)), probs


def small_attend_back(query, keys, values, probs, grad):
    prob_grad = jnp.einsum("qhd,khd->hqk", heads_of(grad), heads_of(values), preferred_element_type=F32)
    weighted = jnp.sum(probs * prob_grad, axis=-1, keepdims=True)
    score_grad = to_half(probs * (prob_grad - weighted) * HDIM ** (-0.5))
    dq = jnp.einsum("hqk,khd->qhd", score_grad, heads_of(keys), preferred_element_type=F32)
    dk = jnp.einsum("hqk,qhd->khd", score_grad, heads_of(query), preferred_element_type=F32)
    dv = jnp.einsum("hqk,qhd->khd", to_half(probs), heads_of(grad), preferred_element_type=F32)
    return (
        to_half(dq.reshape(query.shape)),
        to_half(dk.reshape(keys.shape)),
        to_half(dv.reshape(values.shape)),
    )


def adamw(weight, gradient, moment_one, moment_two, step_rate):
    moment_one = beta_first * moment_one + (1.0 - beta_first) * gradient
    moment_two = beta_second * moment_two + (1.0 - beta_second) * gradient * gradient
    mean_hat = moment_one / (1.0 - beta_first**STEP)
    square_hat = moment_two / (1.0 - beta_second**STEP)
    updated = weight - step_rate * (
        mean_hat / (jnp.sqrt(square_hat) + epsilon) + decay_rate * weight
    )
    return (moment_one, moment_two, updated, updated.astype(BF))


def side_by_side(mats):
    return jnp.concatenate([mats[i] for i in range(mats.shape[0])], axis=1)


def pad_rows(values, count):
    return jnp.pad(values, ((0, count - values.shape[0]), (0, 0)))


def pad_columns(values, count):
    return jnp.pad(values, ((0, 0), (0, count - values.shape[1])))


def gather(columns):
    return lax.all_gather(columns, ALL, axis=0, tiled=True)


def scatter(columns):
    return lax.psum_scatter(columns, ALL, scatter_dimension=0, tiled=True).astype(F32)


def per_device(
    enc_input,
    dec_input,
    targets,
    lengths,
    attention_mats,
    expand_mats,
    reduce_mats,
    action_head,
    query_pos,
    vectors,
    expand_bias,
    *moments,
):
    ranks = lax.axis_size("seq")
    seq_index = lax.axis_index("seq")
    items, enc_part, width = enc_input.shape
    dec_part = dec_input.shape[1]
    joints = targets.shape[2]
    width_ff = expand_mats.shape[2]
    shard = attention_mats.shape[1]
    bias_part = expand_bias.shape[0]
    n_query, n_vec = query_pos.shape[0], vectors.shape[0]
    vec_at = (n_query + 7) // 8 * 8
    head_at = (vec_at + n_vec + 7) // 8 * 8
    n_small = (head_at + joints + 127) // 128 * 128
    devices = width // shard

    def pack_small(query, vector, head):
        return pad_columns(
            jnp.concatenate(
                [pad_columns(query, vec_at), pad_columns(vector, head_at - vec_at), head], axis=1
            ),
            n_small,
        )

    half_mats = to_half(attention_mats)
    half_expand = to_half(expand_mats)
    half_reduce = to_half(jnp.swapaxes(reduce_mats, 1, 2))
    small_local = to_half(pack_small(query_pos.T, vectors.T, action_head))
    bias_local = to_half(jnp.pad(expand_bias, (0, shard * 128 - bias_part)).reshape(shard, 128))
    enc_all = gather(
        jnp.concatenate(
            [side_by_side(half_mats[0:4]), half_expand[0], half_reduce[0], small_local, bias_local],
            axis=1,
        )
    )
    dec_all = gather(
        jnp.concatenate([side_by_side(half_mats[4:12]), half_expand[1], half_reduce[1]], axis=1)
    )

    per_rank = items // ranks
    def to_item(values):
        return lax.all_to_all(values, "seq", 0, 1, tiled=True)

    enc_items = to_item(enc_input)
    dec_items = to_item(dec_input)
    target_items = to_item(targets)
    enc_x = enc_items[0]
    dec_x = dec_items[0]
    target = target_items[0]
    length = lengths[seq_index]
    enc_rows = enc_x.shape[0]
    dec_rows = dec_x.shape[0]

    enc_mats = [enc_all[:, i * width : (i + 1) * width] for i in range(4)]
    at = 4 * width
    enc_expand = enc_all[:, at : at + width_ff]
    enc_reduce_t = enc_all[:, at + width_ff : at + 2 * width_ff]
    at += 2 * width_ff
    small = enc_all[:, at : at + n_small].T
    bias_all = (
        enc_all[:, at + n_small :].reshape(devices, shard * 128)[:, :bias_part].reshape(-1).astype(F32)
    )
    query_whole = small[:n_query].astype(F32)
    vec = small[vec_at : vec_at + n_vec].astype(F32)
    head_t = small[head_at : head_at + joints]
    dec_mats = [None] * 4 + [dec_all[:, i * width : (i + 1) * width] for i in range(8)]
    at = 8 * width
    dec_expand = dec_all[:, at : at + width_ff]
    dec_reduce_t = dec_all[:, at + width_ff : at + 2 * width_ff]

    positions = jnp.asarray(sine_table(enc_rows, width))
    enc_float = enc_x.astype(F32)
    enc_in = to_half(enc_float + positions)
    enc_query = to_half(mm(enc_in, enc_mats[0]) + vec[0])
    enc_keys = to_half(mm(enc_in, enc_mats[1]))
    enc_values = to_half(mm(enc_x, enc_mats[2]) + vec[1])
    enc_mixed, enc_log = attend(enc_query, enc_keys, enc_values)
    enc_sum_one = enc_float + mm(enc_mixed, enc_mats[3]) + vec[2]
    enc_hidden = layer_norm(enc_sum_one, vec[3], vec[4])
    enc_hidden_half = to_half(enc_hidden)
    enc_inner = mm(enc_hidden_half, enc_expand) + bias_all[:width_ff]
    enc_act = to_half(jax.nn.gelu(enc_inner))
    enc_sum_two = enc_hidden + mm_t(enc_act, enc_reduce_t) + vec[5]
    memory = layer_norm(enc_sum_two, vec[6], vec[7])

    dec_float = dec_x.astype(F32)
    self_in = to_half(dec_float + query_whole)
    self_query = to_half(mm(self_in, dec_mats[4]) + vec[8])
    self_keys = to_half(mm(self_in, dec_mats[5]))
    self_values = to_half(mm(dec_x, dec_mats[6]) + vec[9])
    self_mixed, self_probs = small_attend(self_query, self_keys, self_values)
    dec_sum_one = dec_float + mm(self_mixed, dec_mats[7]) + vec[10]
    dec_one = layer_norm(dec_sum_one, vec[11], vec[12])
    cross_in = to_half(dec_one + query_whole)
    cross_query = to_half(mm(cross_in, dec_mats[8]) + vec[13])
    memory_in = to_half(memory + positions)
    memory_half = to_half(memory)
    cross_keys = to_half(mm(memory_in, dec_mats[9]))
    cross_values = to_half(mm(memory_half, dec_mats[10]) + vec[14])
    cross_mixed, cross_probs = small_attend(cross_query, cross_keys, cross_values)
    dec_sum_two = dec_one + mm(cross_mixed, dec_mats[11]) + vec[15]
    dec_two = layer_norm(dec_sum_two, vec[16], vec[17])
    dec_two_half = to_half(dec_two)
    dec_inner = mm(dec_two_half, dec_expand) + bias_all[width_ff:]
    dec_act = to_half(jax.nn.gelu(dec_inner))
    dec_sum_three = dec_two + mm_t(dec_act, dec_reduce_t) + vec[18]
    dec_three = layer_norm(dec_sum_three, vec[19], vec[20])
    dec_three_half = to_half(dec_three)
    predicted = mm_t(dec_three_half, head_t)

    valid = (jnp.arange(dec_rows) < length).astype(F32)
    error = predicted - target
    pred_grad = to_half(error * lax.rsqrt(error * error + 1.0) * valid[:, None] / joints)
    head_grad_t = t_mm(pred_grad, dec_three_half)
    three_grad = mm(pred_grad, head_t)
    sum_three_grad, gain_three, shift_three = norm_back(dec_sum_three, vec[19], three_grad)
    reduce_out = to_half(sum_three_grad)
    dec_reduce_grad_t = t_mm(reduce_out, dec_act)
    dec_inner_half = to_half(gelu_back(dec_inner, mm(reduce_out, dec_reduce_t)))
    dec_expand_grad = t_mm(dec_two_half, dec_inner_half)
    two_grad = sum_three_grad + mm_t(dec_inner_half, dec_expand)
    sum_two_grad, gain_two, shift_two = norm_back(dec_sum_two, vec[16], two_grad)
    cross_out = to_half(sum_two_grad)
    cross_out_wgrad = t_mm(cross_mixed, cross_out)
    cross_mixed_grad = to_half(mm_t(cross_out, dec_mats[11]))
    cross_dq, cross_dk, cross_dv = small_attend_back(
        cross_query, cross_keys, cross_values, cross_probs, cross_mixed_grad
    )
    cross_in_grad = mm_t(cross_dq, dec_mats[8])
    one_grad = sum_two_grad + cross_in_grad
    sum_one_grad, gain_one, shift_one = norm_back(dec_sum_one, vec[11], one_grad)
    self_out = to_half(sum_one_grad)
    self_out_wgrad = t_mm(self_mixed, self_out)
    self_mixed_grad = to_half(mm_t(self_out, dec_mats[7]))
    self_dq, self_dk, self_dv = small_attend_back(
        self_query, self_keys, self_values, self_probs, self_mixed_grad
    )
    self_in_grad = mm_t(self_dq, dec_mats[4]) + mm_t(self_dk, dec_mats[5])
    dec_input_grad = to_half(sum_one_grad + self_in_grad + mm_t(self_dv, dec_mats[6]))
    query_grad = self_in_grad + cross_in_grad
    memory_grad = mm_t(cross_dk, dec_mats[9]) + mm_t(cross_dv, dec_mats[10])
    dec_sums = scatter(
        jnp.concatenate(
            [
                to_half(g)
                for g in (
                    t_mm(self_in, self_dq),
                    t_mm(self_in, self_dk),
                    t_mm(dec_x, self_dv),
                    self_out_wgrad,
                    t_mm(cross_in, cross_dq),
                    t_mm(memory_in, cross_dk),
                    t_mm(memory_half, cross_dv),
                    cross_out_wgrad,
                    dec_expand_grad,
                    dec_reduce_grad_t,
                )
            ],
            axis=1,
        )
    )

    enc_two_grad, enc_gain_two, enc_shift_two = norm_back(enc_sum_two, vec[6], memory_grad)
    enc_out = to_half(enc_two_grad)
    enc_reduce_grad_t = t_mm(enc_out, enc_act)
    enc_inner_half = to_half(gelu_back(enc_inner, mm(enc_out, enc_reduce_t)))
    enc_expand_grad = t_mm(enc_hidden_half, enc_inner_half)
    hidden_grad = enc_two_grad + mm_t(enc_inner_half, enc_expand)
    enc_one_grad, enc_gain_one, enc_shift_one = norm_back(enc_sum_one, vec[3], hidden_grad)
    attn_out = to_half(enc_one_grad)
    enc_out_wgrad = t_mm(enc_mixed, attn_out)
    enc_mixed_grad = to_half(mm_t(attn_out, enc_mats[3]))
    enc_dq, enc_dk, enc_dv = attend_back(
        enc_query, enc_keys, enc_values, enc_mixed, enc_mixed_grad, enc_log
    )
    enc_input_grad = to_half(
        enc_one_grad
        + mm_t(enc_dq, enc_mats[0])
        + mm_t(enc_dk, enc_mats[1])
        + mm_t(enc_dv, enc_mats[2])
    )
    vec_grads = jnp.stack(
        [
            column_sum(enc_dq),
            column_sum(enc_dv),
            column_sum(enc_one_grad),
            enc_gain_one,
            enc_shift_one,
            column_sum(enc_two_grad),
            enc_gain_two,
            enc_shift_two,
            column_sum(self_dq),
            column_sum(self_dv),
            column_sum(sum_one_grad),
            gain_one,
            shift_one,
            column_sum(cross_dq),
            column_sum(cross_dv),
            column_sum(sum_two_grad),
            gain_two,
            shift_two,
            column_sum(sum_three_grad),
            gain_three,
            shift_three,
        ]
    )
    small_grad = pad_rows(
        jnp.concatenate(
            [
                pad_rows(query_grad, vec_at),
                pad_rows(vec_grads, head_at - vec_at),
                head_grad_t,
            ]
        ),
        n_small,
    ).T
    bias_grad = jnp.concatenate([column_sum(enc_inner_half), column_sum(dec_inner_half)])
    bias_grad = pad_columns(bias_grad.reshape(devices, bias_part), shard * 128).reshape(width, 128)
    enc_sums = scatter(
        jnp.concatenate(
            [
                to_half(g)
                for g in (
                    t_mm(enc_in, enc_dq),
                    t_mm(enc_in, enc_dk),
                    t_mm(enc_x, enc_dv),
                    enc_out_wgrad,
                    enc_expand_grad,
                    enc_reduce_grad_t,
                    small_grad,
                    bias_grad,
                )
            ],
            axis=1,
        )
    )

    def to_parts(values, part):
        return lax.all_to_all(values.reshape(per_rank, ranks * part, width), "seq", 1, 0, tiled=True)

    outputs = [to_parts(enc_input_grad, enc_part), to_parts(dec_input_grad, dec_part)]

    at = 4 * width
    small_sum = enc_sums[:, at + 2 * width_ff : at + 2 * width_ff + n_small]
    bias_sum = enc_sums[:, at + 2 * width_ff + n_small :]
    gradients = (
        jnp.stack(
            [enc_sums[:, i * width : (i + 1) * width] for i in range(4)]
            + [dec_sums[:, i * width : (i + 1) * width] for i in range(8)]
        ),
        jnp.stack([enc_sums[:, at : at + width_ff], dec_sums[:, 2 * at : 2 * at + width_ff]]),
        jnp.swapaxes(
            jnp.stack(
                [enc_sums[:, at + width_ff : at + 2 * width_ff], dec_sums[:, 2 * at + width_ff :]]
            ),
            1,
            2,
        ),
        small_sum[:, head_at : head_at + joints],
        small_sum[:, :n_query].T,
        small_sum[:, vec_at : vec_at + n_vec].T,
        bias_sum.reshape(-1)[:bias_part],
    )
    weights = (
        attention_mats,
        expand_mats,
        reduce_mats,
        action_head,
        query_pos,
        vectors,
        expand_bias,
    )
    firsts, seconds = moments[:7], moments[7:]
    rates = (rate_matrix,) * 4 + (rate_vector,) * 3
    for weight, gradient, moment_one, moment_two, step_rate in zip(
        weights, gradients, firsts, seconds, rates
    ):
        outputs.extend(adamw(weight, gradient, moment_one, moment_two, step_rate))
    return tuple(outputs)


def solution(mesh):
    rows = P("dp", "seq", None)
    weight_specs = (
        P(None, ALL, None),
        P(None, ALL, None),
        P(None, None, ALL),
        P(ALL, None),
        P(None, ALL),
        P(None, ALL),
        P(ALL),
    )
    in_specs = (rows, rows, rows, P("dp")) + weight_specs * 3
    out_specs = (rows, rows) + tuple(spec for spec in weight_specs for unused in range(4))
    return jax.shard_map(
        per_device, mesh=mesh, in_specs=in_specs, out_specs=out_specs, check_vma=False
    )
```

```python
import functools
import math

import jax
import jax.numpy as jnp
import numpy as np
from jax import lax
from jax.experimental import pallas as pl
from jax.experimental.pallas import tpu as pltpu
from jax.sharding import PartitionSpec as P

HEADS = 8
HDIM = 64
PAIR = 2 * HDIM
STEP = 10
ALL = ("dp", "seq")

beta_first = 0.9
beta_second = 0.999
epsilon = 1e-08
decay_rate = 0.1
rate_matrix = 0.08
rate_vector = 0.2

BF = jnp.bfloat16
F32 = jnp.float32
MB = 1 << 20
SCALE = HDIM ** (-0.5)


def to_half(values):
    return values.astype(BF)


def mm(a, b):
    return lax.dot_general(a, b, (((1,), (0,)), ((), ())), preferred_element_type=F32)


def mm_t(a, b):
    return lax.dot_general(a, b, (((1,), (1,)), ((), ())), preferred_element_type=F32)


def column_sum(values):
    return jnp.sum(values.astype(F32), axis=0, keepdims=True)


def norm_parts(values):
    center = values - jnp.mean(values, axis=-1, keepdims=True)
    scale = lax.rsqrt(jnp.mean(center * center, axis=-1, keepdims=True) + 1e-05)
    return center * scale, scale


def layer_norm(values, gain, shift):
    return norm_parts(values)[0] * gain + shift


def norm_back(values, gain, gradient):
    unit, scale = norm_parts(values)
    inner = gradient * gain
    mean_inner = jnp.mean(inner, axis=-1, keepdims=True)
    mean_cross = jnp.mean(inner * unit, axis=-1, keepdims=True)
    back = scale * (inner - mean_inner - unit * mean_cross)
    return back, column_sum(gradient * unit), column_sum(gradient)


GELU_A = math.sqrt(2.0 / math.pi)
GELU_B = 0.044715


def gelu_parts(u):
    square = u * u
    bend = jnp.tanh(u * (GELU_A + GELU_A * GELU_B * square))
    half = 0.5 + 0.5 * bend
    slope = half + (0.5 * u) * (1.0 - bend * bend) * (GELU_A + 3.0 * GELU_A * GELU_B * square)
    return u * half, slope


def gelu(u):
    return u * (0.5 + 0.5 * jnp.tanh(u * (GELU_A + GELU_A * GELU_B * (u * u))))


def sine_table(count, width):
    halves = np.arange(width // 2, dtype=np.float64)
    frequency = np.exp(halves * (-2.0 * math.log(10000.0) / width))
    angles = np.arange(count)[:, None] * frequency[None, :]
    table = np.stack([np.sin(angles), np.cos(angles)], axis=-1).reshape(count, width)
    return table.astype(np.float32)


def own_lanes(values, h):
    lane = lax.broadcasted_iota(jnp.int32, values.shape, 1)
    return jnp.where((lane < HDIM) == (h == 0), values, jnp.zeros_like(values))


def join_rows(first, second):
    row = lax.broadcasted_iota(jnp.int32, first.shape, 0)
    return jnp.where(row < HDIM, first, second)


def attend_kernel(
    x_ref, pos_ref, wq_ref, wk_ref, wv_ref, vec_ref, q_ref, k_ref, v_ref, o_ref, log_ref, in_ref, vt_ref, *, chunk
):
    @pl.when(pl.program_id(0) == 0)
    def _():
        in_ref[...] = to_half(x_ref[...].astype(F32) + pos_ref[...])

    q_ref[...] = to_half(mm(in_ref[...], wq_ref[...]) + vec_ref[0:1, :])
    k_ref[...] = to_half(mm(in_ref[...], wk_ref[...]))
    values = to_half(mm(x_ref[...], wv_ref[...]) + vec_ref[1:2, :])
    v_ref[...] = values
    vt_ref[...] = values.T

    def step(i, carry):
        at = pl.ds(i * chunk, chunk)
        query = q_ref[at, :] * BF(SCALE)
        mixed = []
        for h in range(2):
            scores = mm_t(k_ref[...], own_lanes(query, h))
            peak = jnp.max(scores, axis=0, keepdims=True)
            weights = jnp.exp(scores - peak)
            total = jnp.sum(weights, axis=0, keepdims=True)
            mixed.append(mm(vt_ref[...], to_half(weights)) / total)
            log_ref[0, pl.ds(h, 1), at] = peak + jnp.log(total)
        o_ref[at, :] = to_half(join_rows(*mixed).T)
        return carry

    lax.fori_loop(0, q_ref.shape[0] // chunk, step, 0)


def attend(x, positions, weights, vec):
    rows, width = x.shape
    pairs = width // PAIR
    whole = pl.BlockSpec((rows, width), lambda i: (0, 0))
    own = pl.BlockSpec((rows, PAIR), lambda i: (0, i))
    mats = [pl.BlockSpec((width, PAIR), lambda i, j=j: (0, i + j * pairs)) for j in range(3)]
    half = jax.ShapeDtypeStruct((rows, width), BF)
    return pl.pallas_call(
        functools.partial(attend_kernel, chunk=256),
        grid=(pairs,),
        in_specs=[whole, whole] + mats + [pl.BlockSpec((vec.shape[0], PAIR), lambda i: (0, i))],
        out_specs=[own] * 4 + [pl.BlockSpec((1, 2, rows), lambda i: (i, 0, 0))],
        out_shape=[half] * 4 + [jax.ShapeDtypeStruct((pairs, 2, rows), F32)],
        scratch_shapes=[pltpu.VMEM((rows, width), BF), pltpu.VMEM((PAIR, rows), BF)],
        compiler_params=pltpu.CompilerParams(vmem_limit_bytes=56 * MB),
        cost_estimate=pl.CostEstimate(
            flops=16 * rows * rows * width, bytes_accessed=12 * rows * width, transcendentals=8 * rows * rows
        ),
        name="attend",
    )(x, positions, weights, weights, weights, vec)


def forward_kernel(
    mixed_ref, x_ref, out_ref, vec_ref, e_ref, r_ref, bias_ref,
    sum_one_ref, hidden_ref, u_ref, sum_two_ref, memory_ref, *, tile
):
    step = pl.program_id(0)
    count = x_ref.shape[0] // tile

    def rows_of(i):
        return pl.ds(pl.multiple_of(i * tile, tile), tile)

    @pl.when(step == 0)
    def _():
        def body(i, carry):
            at = rows_of(i)
            total = x_ref[at, :].astype(F32) + mm(mixed_ref[at, :], out_ref[...]) + vec_ref[2:3, :]
            sum_one_ref[at, :] = total
            hidden = layer_norm(total, vec_ref[3:4, :], vec_ref[4:5, :])
            hidden_ref[at, :] = to_half(hidden)
            sum_two_ref[at, :] = hidden + vec_ref[5:6, :]
            return carry

        lax.fori_loop(0, count, body, 0)

    def body(i, carry):
        at = rows_of(i)
        u = mm(hidden_ref[at, :], e_ref[...]) + bias_ref[...]
        u_ref[at, :] = u
        sum_two_ref[at, :] += mm_t(to_half(gelu(u)), r_ref[...])
        return carry

    lax.fori_loop(0, count, body, 0)

    @pl.when(step == pl.num_programs(0) - 1)
    def _():
        def body(i, carry):
            at = rows_of(i)
            memory_ref[at, :] = layer_norm(sum_two_ref[at, :], vec_ref[6:7, :], vec_ref[7:8, :])
            return carry

        lax.fori_loop(0, count, body, 0)


def feed_forward(mixed, x, enc_mats, vec, enc_ffn, bias):
    rows, width = x.shape
    width_ff = bias.shape[1]
    block = 640 if width_ff % 640 == 0 else width_ff
    steps = width_ff // block
    whole = pl.BlockSpec((rows, width), lambda i: (0, 0))
    float_rows = jax.ShapeDtypeStruct((rows, width), F32)
    return pl.pallas_call(
        functools.partial(forward_kernel, tile=256),
        grid=(steps,),
        in_specs=[
            whole,
            whole,
            pl.BlockSpec((width, width), lambda i: (0, 3)),
            pl.BlockSpec(vec.shape, lambda i: (0, 0)),
            pl.BlockSpec((width, block), lambda i: (0, i)),
            pl.BlockSpec((width, block), lambda i: (0, i + steps)),
            pl.BlockSpec((1, block), lambda i: (0, i)),
        ],
        out_specs=[whole, whole, pl.BlockSpec((rows, block), lambda i: (0, i)), whole, whole],
        out_shape=[
            float_rows,
            jax.ShapeDtypeStruct((rows, width), BF),
            jax.ShapeDtypeStruct((rows, width_ff), F32),
            float_rows,
            float_rows,
        ],
        compiler_params=pltpu.CompilerParams(vmem_limit_bytes=56 * MB),
        cost_estimate=pl.CostEstimate(
            flops=4 * rows * width * width_ff, bytes_accessed=4 * rows * width_ff, transcendentals=rows * width_ff
        ),
        name="feed_forward",
    )(mixed, x, enc_mats, vec, enc_ffn, enc_ffn, bias)


def turned(turn, values):
    return to_half(mm_t(turn, values))


def lefts_kernel(x_ref, pos_ref, mixed_ref, hidden_ref, turn_ref, in_t_ref, x_t_ref, mixed_t_ref, hidden_t_ref):
    in_t_ref[...] = turned(turn_ref[...], to_half(x_ref[...].astype(F32) + pos_ref[...]))
    x_t_ref[...] = turned(turn_ref[...], x_ref[...])
    mixed_t_ref[...] = turned(turn_ref[...], mixed_ref[...])
    hidden_t_ref[...] = turned(turn_ref[...], hidden_ref[...])


def lefts(x, positions, mixed, hidden, turn):
    rows, width = x.shape
    return pl.pallas_call(
        lefts_kernel,
        out_shape=[jax.ShapeDtypeStruct((width, rows), BF)] * 4,
        compiler_params=pltpu.CompilerParams(vmem_limit_bytes=40 * MB),
        cost_estimate=pl.CostEstimate(flops=8 * rows * width * width, bytes_accessed=20 * rows * width, transcendentals=0),
        name="lefts",
    )(x, positions, mixed, hidden, turn)


def norm_kernel(grad_ref, sum_two_ref, vec_ref, turn_ref, two_ref, half_t_ref, vec_grad_ref, half_ref, *, tile):
    vec_grad_ref[...] = jnp.zeros_like(vec_grad_ref)

    def body(i, carry):
        at = pl.ds(pl.multiple_of(i * tile, tile), tile)
        back, gain, shift = norm_back(sum_two_ref[at, :], vec_ref[6:7, :], grad_ref[at, :])
        two_ref[at, :] = back
        half_ref[at, :] = to_half(back)
        vec_grad_ref[0:1, :] += column_sum(back)
        vec_grad_ref[1:2, :] += gain
        vec_grad_ref[2:3, :] += shift
        return carry

    lax.fori_loop(0, grad_ref.shape[0] // tile, body, 0)
    half_t_ref[...] = turned(turn_ref[...], half_ref[...])


def last_norm_back(grad, sum_two, vec, turn):
    rows, width = grad.shape
    return pl.pallas_call(
        functools.partial(norm_kernel, tile=256),
        out_shape=[
            jax.ShapeDtypeStruct((rows, width), F32),
            jax.ShapeDtypeStruct((width, rows), BF),
            jax.ShapeDtypeStruct((8, width), F32),
        ],
        scratch_shapes=[pltpu.VMEM((rows, width), BF)],
        compiler_params=pltpu.CompilerParams(vmem_limit_bytes=40 * MB),
        cost_estimate=pl.CostEstimate(flops=2 * rows * width * width, bytes_accessed=14 * rows * width, transcendentals=0),
        name="last_norm_back",
    )(grad, sum_two, vec, turn)


def backward_kernel(
    grad_ref, half_t_ref, sum_one_ref, hidden_t_ref, mixed_t_ref, u_ref, e_ref, r_ref, out_ref, vec_ref,
    keep_ref, send_ref, one_ref, mixed_grad_ref, vec_grad_ref, bias_ref,
    two_ref, half_ref, act_ref, inner_ref, *, tile
):
    step = pl.program_id(0)
    rows, width = sum_one_ref.shape
    count = rows // tile
    cut = width // 2

    def rows_of(i):
        return pl.ds(pl.multiple_of(i * tile, tile), tile)

    @pl.when(step == 0)
    def _():
        two_ref[...] = grad_ref[...]
        half_ref[...] = to_half(grad_ref[...])

    bias_ref[...] = jnp.zeros_like(bias_ref)

    def body(i, carry):
        at = rows_of(i)
        act, slope = gelu_parts(u_ref[at, :])
        act_ref[at, :] = to_half(act)
        inner = to_half(mm(half_ref[at, :], r_ref[...]) * slope)
        inner_ref[at, :] = inner
        bias_ref[...] += column_sum(inner)
        two_ref[at, :] += mm_t(inner, e_ref[...])
        return carry

    lax.fori_loop(0, count, body, 0)
    block = u_ref.shape[1]
    steps = pl.num_programs(0)

    def set_grad(at, grad):
        at = pl.ds(pl.multiple_of(at, 128), grad.shape[1])
        keep_ref[:, at] = to_half(grad[:cut])
        send_ref[:, at] = to_half(grad[cut:])

    set_grad(step * block, mm(hidden_t_ref[...], inner_ref[...]))
    set_grad((step + steps) * block, mm(half_t_ref[...], act_ref[...]))

    @pl.when(step == pl.num_programs(0) - 1)
    def _():
        vec_grad_ref[...] = jnp.zeros_like(vec_grad_ref)

        def body(i, carry):
            at = rows_of(i)
            back, gain, shift = norm_back(sum_one_ref[at, :], vec_ref[3:4, :], two_ref[at, :])
            one_ref[at, :] = back
            half = to_half(back)
            half_ref[at, :] = half
            mixed_grad_ref[at, :] = to_half(mm_t(half, out_ref[...]))
            vec_grad_ref[0:1, :] += column_sum(back)
            vec_grad_ref[1:2, :] += gain
            vec_grad_ref[2:3, :] += shift
            return carry

        lax.fori_loop(0, count, body, 0)
        set_grad(2 * steps * block, mm(mixed_t_ref[...], half_ref[...]))


def feed_back(grad, half_t, sum_one, hidden_t, mixed_t, u, enc_mats, enc_ffn, vec):
    rows, width = sum_one.shape
    width_ff = u.shape[1]
    block = 640 if width_ff % 640 == 0 else width_ff
    steps = width_ff // block
    cut = width // 2
    whole = pl.BlockSpec((rows, width), lambda i: (0, 0))
    whole_t = pl.BlockSpec((width, rows), lambda i: (0, 0))
    grads = (cut, 2 * width_ff + width)
    return pl.pallas_call(
        functools.partial(backward_kernel, tile=256),
        grid=(steps,),
        in_specs=[
            whole,
            whole_t,
            whole,
            whole_t,
            whole_t,
            pl.BlockSpec((rows, block), lambda i: (0, i)),
            pl.BlockSpec((width, block), lambda i: (0, i)),
            pl.BlockSpec((width, block), lambda i: (0, i + steps)),
            pl.BlockSpec((width, width), lambda i: (0, 3)),
            pl.BlockSpec(vec.shape, lambda i: (0, 0)),
        ],
        out_specs=[pl.BlockSpec(grads, lambda i: (0, 0))] * 2
        + [
            whole,
            whole,
            pl.BlockSpec((8, width), lambda i: (0, 0)),
            pl.BlockSpec((1, block), lambda i: (0, i)),
        ],
        out_shape=[jax.ShapeDtypeStruct(grads, BF)] * 2
        + [
            jax.ShapeDtypeStruct((rows, width), F32),
            jax.ShapeDtypeStruct((rows, width), BF),
            jax.ShapeDtypeStruct((8, width), F32),
            jax.ShapeDtypeStruct((1, width_ff), F32),
        ],
        scratch_shapes=[
            pltpu.VMEM((rows, width), F32),
            pltpu.VMEM((rows, width), BF),
            pltpu.VMEM((rows, block), BF),
            pltpu.VMEM((rows, block), BF),
        ],
        compiler_params=pltpu.CompilerParams(vmem_limit_bytes=60 * MB),
        cost_estimate=pl.CostEstimate(
            flops=8 * rows * width * width_ff, bytes_accessed=6 * rows * width_ff, transcendentals=rows * width_ff
        ),
        name="feed_back",
    )(grad, half_t, sum_one, hidden_t, mixed_t, u, enc_ffn, enc_ffn, enc_mats, vec)


def attend_back_kernel(
    q_ref, k_ref, v_ref, o_ref, g_ref, log_ref, in_t_ref, x_t_ref, one_ref, wq_ref, wk_ref, wv_ref, *refs, chunk, first
):
    keep_ref, send_ref, grad_ref, vec_ref, kt_ref, dx_ref, dq_ref, dk_ref, dv_ref = refs[-9:]
    step_at = pl.program_id(0)
    width = x_t_ref.shape[0]
    cut = width // 2

    @pl.when(step_at == 0)
    def _():
        dx_ref[...] = one_ref[...]
        if first:
            keep_ref[...] = refs[0][...]
            send_ref[...] = refs[1][...]

    kt_ref[...] = k_ref[...].T
    dk_ref[...] = jnp.zeros_like(dk_ref)
    dv_ref[...] = jnp.zeros_like(dv_ref)

    def step(i, carry):
        at = pl.ds(i * chunk, chunk)
        query = q_ref[at, :] * BF(SCALE)
        grad = g_ref[at, :]
        cross = (grad.astype(F32) * o_ref[at, :].astype(F32)).T
        back = []
        for h in range(2):
            own, own_grad = own_lanes(query, h), own_lanes(grad, h)
            weighted = jnp.sum(cross[h * HDIM : (h + 1) * HDIM], axis=0, keepdims=True)
            probs = jnp.exp(mm_t(k_ref[...], own) - log_ref[0, pl.ds(h, 1), at])
            score_grad = to_half(probs * (mm_t(v_ref[...], own_grad) - weighted))
            dv_ref[...] += mm(to_half(probs), own_grad)
            dk_ref[...] += mm(score_grad, own)
            back.append(mm(kt_ref[...], score_grad))
        dq_ref[at, :] = to_half((join_rows(*back) * SCALE).T)
        return carry

    lax.fori_loop(0, q_ref.shape[0] // chunk, step, 0)
    dq = dq_ref[...]
    dk = to_half(dk_ref[...])
    dv = to_half(dv_ref[...])
    dx_ref[...] += mm_t(dq, wq_ref[...]) + mm_t(dk, wk_ref[...]) + mm_t(dv, wv_ref[...])
    for j, (left_ref, right) in enumerate(((in_t_ref, dq), (in_t_ref, dk), (x_t_ref, dv))):
        wgrad = to_half(mm(left_ref[...], right))
        at = pl.ds(pl.multiple_of(j * width + (first + step_at) * PAIR, PAIR), PAIR)
        keep_ref[:, at] = wgrad[:cut]
        send_ref[:, at] = wgrad[cut:]
    vec_ref[...] = jnp.zeros_like(vec_ref)
    vec_ref[0:1, :] = column_sum(dq)
    vec_ref[1:2, :] = column_sum(dv)

    @pl.when(step_at == pl.num_programs(0) - 1)
    def _():
        grad_ref[...] = dx_ref[...].astype(grad_ref.dtype)


def attend_back(query, keys, values, mixed, grad, log_total, in_t, x_t, so_far, enc_mats, part, parts, grads):
    rows, width = query.shape
    pairs = width // PAIR
    count = pairs // parts
    first = part * count
    cut = width // 2
    own = pl.BlockSpec((rows, PAIR), lambda i: (0, i + first))
    whole = pl.BlockSpec((rows, width), lambda i: (0, 0))
    whole_t = pl.BlockSpec((width, rows), lambda i: (0, 0))
    mats = [pl.BlockSpec((width, PAIR), lambda i, j=j: (0, i + first + j * pairs)) for j in range(3)]
    three = pl.BlockSpec((cut, 3 * width), lambda i: (0, 0))
    return pl.pallas_call(
        functools.partial(attend_back_kernel, chunk=256, first=first),
        grid=(count,),
        in_specs=[own] * 5
        + [pl.BlockSpec((1, 2, rows), lambda i: (i + first, 0, 0)), whole_t, whole_t, whole]
        + mats
        + [three] * len(grads),
        out_specs=[three, three, whole, pl.BlockSpec((8, PAIR), lambda i: (0, i))],
        out_shape=[jax.ShapeDtypeStruct((cut, 3 * width), BF)] * 2
        + [
            jax.ShapeDtypeStruct((rows, width), BF if part == parts - 1 else F32),
            jax.ShapeDtypeStruct((8, count * PAIR), F32),
        ],
        scratch_shapes=[
            pltpu.VMEM((PAIR, rows), BF),
            pltpu.VMEM((rows, width), F32),
            pltpu.VMEM((rows, PAIR), BF),
            pltpu.VMEM((rows, PAIR), F32),
            pltpu.VMEM((rows, PAIR), F32),
        ],
        compiler_params=pltpu.CompilerParams(vmem_limit_bytes=60 * MB),
        cost_estimate=pl.CostEstimate(
            flops=40 * rows * rows * width // parts, bytes_accessed=16 * rows * width, transcendentals=4 * rows * rows
        ),
        name="attend_back",
    )(query, keys, values, mixed, grad, log_total, in_t, x_t, so_far, enc_mats, enc_mats, enc_mats, *grads)


def heads_forward(query, key_ref, value_ref, prob_ref, n_keys):
    outs = []
    for pair in range(HEADS // 2):
        lanes = slice(pair * PAIR, (pair + 1) * PAIR)
        keys = key_ref[:, lanes]
        values_t = value_ref[:, lanes].T
        scaled = query[:, lanes] * BF(SCALE)
        mixed = []
        for h in range(2):
            scores = mm_t(keys, own_lanes(scaled, h))
            if n_keys < keys.shape[0]:
                row = lax.broadcasted_iota(jnp.int32, scores.shape, 0)
                scores = jnp.where(row < n_keys, scores, -jnp.inf)
            weights = jnp.exp(scores - jnp.max(scores, axis=0, keepdims=True))
            probs = weights * (1.0 / jnp.sum(weights, axis=0, keepdims=True))
            prob_ref[2 * pair + h] = probs
            mixed.append(mm(values_t, to_half(probs)))
        outs.append(to_half(join_rows(*mixed).T))
    return jnp.concatenate(outs, axis=1)


def heads_back(query, key_ref, value_ref, prob_ref, grad, dk_ref, dv_ref):
    outs = []
    for pair in range(HEADS // 2):
        lanes = slice(pair * PAIR, (pair + 1) * PAIR)
        keys_t = key_ref[:, lanes].T
        values = value_ref[:, lanes]
        scaled = query[:, lanes] * BF(SCALE)
        dk = dv = None
        back = []
        for h in range(2):
            own, own_grad = own_lanes(scaled, h), own_lanes(grad[:, lanes], h)
            probs = prob_ref[2 * pair + h]
            prob_grad = mm_t(values, own_grad)
            weighted = jnp.sum(probs * prob_grad, axis=0, keepdims=True)
            score_grad = to_half(probs * (prob_grad - weighted))
            back.append(mm(keys_t, score_grad))
            k_part, v_part = mm(score_grad, own), mm(to_half(probs), own_grad)
            dk = k_part if h == 0 else dk + k_part
            dv = v_part if h == 0 else dv + v_part
        dk_ref[:, lanes] = to_half(dk)
        dv_ref[:, lanes] = to_half(dv)
        outs.append(to_half((join_rows(*back) * SCALE).T))
    return jnp.concatenate(outs, axis=1)


def decode_kernel(
    x_ref, query_ref, target_ref, valid_ref, w_ref, head_ref, vec_ref, bias_ref, mem_ref, pos_ref, turn_ref,
    w_keep_ref, w_send_ref, f_keep_ref, f_send_ref, in_grad_ref, query_grad_ref, mem_grad_ref, vec_grad_ref, head_grad_ref, bias_grad_ref,
    mem_in, mem_half, cross_k, cross_v, cross_dk, cross_dv, cross_p,
    self_k, self_v, self_dk, self_dv, self_p, u_ref, act_ref, acc_ref, left_ref, *, n_steps, joints, block
):
    width = x_ref.shape[1]
    width_ff = u_ref.shape[1]
    blocks = width_ff // block
    first = 8 * width
    second = first + width_ff

    def mat(i):
        return w_ref[:, i * width : (i + 1) * width]

    cut = width // 2

    def left_of(values):
        return turned(turn_ref[...], values)

    def set_mat(i, left_t, right):
        grad = to_half(mm(left_t, right))
        w_keep_ref[:, i * width : (i + 1) * width] = grad[:cut]
        w_send_ref[:, i * width : (i + 1) * width] = grad[cut:]

    def set_ffn(at, left_t, right):
        grad = to_half(mm(left_t, right))
        f_keep_ref[:, at] = grad[:cut]
        f_send_ref[:, at] = grad[cut:]

    def vec(i):
        return vec_ref[i : i + 1, :]

    def set_vec(i, value):
        vec_grad_ref[i - 8 : i - 7, :] = value

    def lanes(i, start=0):
        return pl.ds(pl.multiple_of(start + i * block, 128), block)

    vec_grad_ref[...] = jnp.zeros_like(vec_grad_ref)
    x = x_ref[...]
    x_float = x.astype(F32)
    places = query_ref[...]
    self_in = to_half(x_float + places)
    self_q = to_half(mm(self_in, mat(0)) + vec(8))
    self_k[...] = to_half(mm(self_in, mat(1)))
    self_v[...] = to_half(mm(x, mat(2)) + vec(9))
    self_mixed = heads_forward(self_q, self_k, self_v, self_p, n_steps)
    sum_one = x_float + mm(self_mixed, mat(3)) + vec(10)
    one = layer_norm(sum_one, vec(11), vec(12))
    cross_in = to_half(one + places)
    cross_q = to_half(mm(cross_in, mat(4)) + vec(13))
    mem_in[...] = to_half(mem_ref[...] + pos_ref[...])
    mem_half[...] = to_half(mem_ref[...])
    cross_k[...] = to_half(mm(mem_in[...], mat(5)))
    cross_v[...] = to_half(mm(mem_half[...], mat(6)) + vec(14))
    cross_mixed = heads_forward(cross_q, cross_k, cross_v, cross_p, cross_k.shape[0])
    sum_two = one + mm(cross_mixed, mat(7)) + vec(15)
    two = layer_norm(sum_two, vec(16), vec(17))
    two_half = to_half(two)
    acc_ref[...] = two + vec(18)

    def forward(i, carry):
        u = mm(two_half, w_ref[:, lanes(i, first)]) + bias_ref[:, lanes(i)]
        u_ref[:, lanes(i)] = u
        acc_ref[...] += mm_t(to_half(gelu(u)), w_ref[:, lanes(i, second)])
        return carry

    lax.fori_loop(0, blocks, forward, 0)
    sum_three = acc_ref[...]
    three_half = to_half(layer_norm(sum_three, vec(19), vec(20)))
    error = mm_t(three_half, head_ref[...]) - target_ref[...]
    pred_grad = to_half(error * lax.rsqrt(error * error + 1.0) * valid_ref[...] / joints)
    head_grad_ref[...] = mm(pred_grad.T, three_half)
    sum_three_grad, gain, shift = norm_back(sum_three, vec(19), mm(pred_grad, head_ref[...]))
    set_vec(18, column_sum(sum_three_grad))
    set_vec(19, gain)
    set_vec(20, shift)
    out_grad = to_half(sum_three_grad)
    left_ref[0] = left_of(out_grad)
    left_ref[1] = left_of(two_half)
    acc_ref[...] = sum_three_grad

    def backward(i, carry):
        act, slope = gelu_parts(u_ref[:, lanes(i)])
        inner = to_half(mm(out_grad, w_ref[:, lanes(i, second)]) * slope)
        bias_grad_ref[:, lanes(i)] = column_sum(inner)
        acc_ref[...] += mm_t(inner, w_ref[:, lanes(i, first)])
        set_ffn(lanes(i), left_ref[1], inner)
        set_ffn(lanes(i, width_ff), left_ref[0], to_half(act))
        return carry

    lax.fori_loop(0, blocks, backward, 0)
    sum_two_grad, gain, shift = norm_back(sum_two, vec(16), acc_ref[...])
    set_vec(15, column_sum(sum_two_grad))
    set_vec(16, gain)
    set_vec(17, shift)
    out_grad = to_half(sum_two_grad)
    set_mat(7, left_of(cross_mixed), out_grad)
    mixed_grad = to_half(mm_t(out_grad, mat(7)))
    cross_dq = heads_back(cross_q, cross_k, cross_v, cross_p, mixed_grad, cross_dk, cross_dv)
    set_vec(13, column_sum(cross_dq))
    set_vec(14, column_sum(cross_dv[...]))
    mem_grad_ref[...] = mm_t(cross_dk[...], mat(5)) + mm_t(cross_dv[...], mat(6))
    set_mat(4, left_of(cross_in), cross_dq)
    set_mat(5, left_of(mem_in[...]), cross_dk[...])
    set_mat(6, left_of(mem_half[...]), cross_dv[...])
    cross_in_grad = mm_t(cross_dq, mat(4))
    sum_one_grad, gain, shift = norm_back(sum_one, vec(11), sum_two_grad + cross_in_grad)
    set_vec(10, column_sum(sum_one_grad))
    set_vec(11, gain)
    set_vec(12, shift)
    out_grad = to_half(sum_one_grad)
    set_mat(3, left_of(self_mixed), out_grad)
    mixed_grad = to_half(mm_t(out_grad, mat(3)))
    self_dq = heads_back(self_q, self_k, self_v, self_p, mixed_grad, self_dk, self_dv)
    set_vec(8, column_sum(self_dq))
    set_vec(9, column_sum(self_dv[...]))
    in_t = left_of(self_in)
    set_mat(0, in_t, self_dq)
    set_mat(1, in_t, self_dk[...])
    set_mat(2, left_of(x), self_dv[...])
    self_in_grad = mm_t(self_dq, mat(0)) + mm_t(self_dk[...], mat(1))
    in_grad_ref[...] = to_half(sum_one_grad + self_in_grad + mm_t(self_dv[...], mat(2)))
    query_grad_ref[...] = self_in_grad + cross_in_grad


def decode(x, places, target, valid, weights, head_t, vec, bias, memory, positions, turn, n_steps, joints):
    rows, width = x.shape
    mem_rows = memory.shape[0]
    width_ff = bias.shape[1]
    half = lambda n: pltpu.VMEM((n, width), BF)
    return pl.pallas_call(
        functools.partial(
            decode_kernel, n_steps=n_steps, joints=joints, block=640 if width_ff % 640 == 0 else width_ff
        ),
        out_shape=[
            jax.ShapeDtypeStruct((width // 2, 8 * width), BF),
            jax.ShapeDtypeStruct((width // 2, 8 * width), BF),
            jax.ShapeDtypeStruct((width // 2, 2 * width_ff), BF),
            jax.ShapeDtypeStruct((width // 2, 2 * width_ff), BF),
            jax.ShapeDtypeStruct((rows, width), BF),
            jax.ShapeDtypeStruct((rows, width), F32),
            jax.ShapeDtypeStruct((mem_rows, width), F32),
            jax.ShapeDtypeStruct((16, width), F32),
            jax.ShapeDtypeStruct(head_t.shape, F32),
            jax.ShapeDtypeStruct((1, width_ff), F32),
        ],
        scratch_shapes=[half(mem_rows)] * 6
        + [pltpu.VMEM((HEADS, mem_rows, rows), F32)]
        + [half(rows)] * 4
        + [
            pltpu.VMEM((HEADS, rows, rows), F32),
            pltpu.VMEM((rows, width_ff), F32),
            pltpu.VMEM((rows, width_ff), BF),
            pltpu.VMEM((rows, width), F32),
            pltpu.VMEM((2, width, rows), BF),
        ],
        compiler_params=pltpu.CompilerParams(vmem_limit_bytes=60 * MB),
        cost_estimate=pl.CostEstimate(
            flops=12 * mem_rows * width * width, bytes_accessed=4 * weights.size, transcendentals=rows * width_ff
        ),
        name="decode",
    )(x, places, target, valid, weights, head_t, vec, bias, memory, positions, turn)


def adamw(weight, gradient, moment_one, moment_two, step_rate):
    moment_one = beta_first * moment_one + (1.0 - beta_first) * gradient
    moment_two = beta_second * moment_two + (1.0 - beta_second) * gradient * gradient
    mean_hat = moment_one / (1.0 - beta_first**STEP)
    square_hat = moment_two / (1.0 - beta_second**STEP)
    updated = weight - step_rate * (
        mean_hat / (jnp.sqrt(square_hat) + epsilon) + decay_rate * weight
    )
    return (moment_one, moment_two, updated, updated.astype(BF))


def update_kernel(*refs, rates):
    count = len(rates)
    ins, outs = refs[: 4 * count], refs[4 * count :]
    for i, rate in enumerate(rates):
        values = adamw(*(ref[...] for ref in ins[4 * i : 4 * i + 4]), rate)
        for ref, value in zip(outs[4 * i : 4 * i + 4], values):
            ref[...] = value


def update(groups, rates):
    shapes = []
    for group in groups:
        shapes += [jax.ShapeDtypeStruct(group[0].shape, F32)] * 3
        shapes.append(jax.ShapeDtypeStruct(group[0].shape, BF))
    outs = pl.pallas_call(
        functools.partial(update_kernel, rates=rates),
        out_shape=shapes,
        compiler_params=pltpu.CompilerParams(vmem_limit_bytes=56 * MB),
        name="update",
    )(*(array for group in groups for array in group))
    return [outs[4 * i : 4 * i + 4] for i in range(len(groups))]


def pad_to(values, rows, columns):
    return jnp.pad(values, ((0, rows - values.shape[0]), (0, columns - values.shape[1])))


def side_by_side(mats):
    return jnp.concatenate([mats[i] for i in range(mats.shape[0])], axis=1)


def gather(columns):
    return lax.all_gather(columns, ALL, axis=0, tiled=True)


def width_bits(axis):
    return (lax.axis_size(axis) - 1).bit_length()


def bit_groups():
    low = width_bits("seq")
    others = list(range(low + width_bits("dp") - 1, low, -1))
    seq = list(range(low - 1, -1, -1))
    groups = [[low]]
    for bits in (others, seq):
        groups += [bits[i : i + 2] for i in range(0, len(bits), 2)]
    return groups


def spread(bits, place):
    return sum(((place >> k) & 1) << bit for k, bit in enumerate(reversed(bits)))


def turn_matrix(width):
    order = [bit for bits in bit_groups() for bit in bits]
    devices = 1 << len(order)
    relative = np.array([spread(order, j) for j in range(devices)], np.int32)
    shard = width // devices
    source = jnp.bitwise_xor(jnp.asarray(relative), lax.axis_index(ALL).astype(jnp.int32))
    source = (source[:, None] * shard + jnp.arange(shard, dtype=jnp.int32)[None, :]).reshape(width)
    return (source[:, None] == jnp.arange(width, dtype=jnp.int32)[None, :]).astype(BF)


def exchange(values, distance):
    low = width_bits("seq")
    axis, distance = ("dp", distance >> low) if distance >> low else ("seq", distance)
    pairs = [(i, i ^ distance) for i in range(lax.axis_size(axis))]
    return lax.ppermute(values, axis, pairs)


class Sum:
    def __init__(self, blocks):
        self.blocks = list(blocks)
        self.groups = bit_groups()
        self.arrived = None

    def start(self):
        bits = self.groups.pop(0)
        self.arrived = [exchange(block, spread(bits, j)) for j, block in enumerate(self.blocks) if j]

    def add(self):
        arrays = [self.blocks[0]] + self.arrived
        count = 1 << len(self.groups[0]) if self.groups else 1
        rows = arrays[0].shape[-2] // count
        totals = []
        for j in range(count):
            parts = [array[..., j * rows : (j + 1) * rows, :].astype(F32) for array in arrays]
            total = functools.reduce(jnp.add, parts)
            totals.append(to_half(total) if self.groups else total)
        self.blocks = totals
        self.arrived = None

    def step(self):
        self.add()
        if self.groups:
            self.start()

    def finish(self):
        while self.groups or self.arrived is not None:
            if self.arrived is None:
                self.start()
            self.step()
        return self.blocks[0]


class Swap:
    def __init__(self, pieces):
        self.pieces = list(pieces)

    def start(self):
        self.arrived = [exchange(piece, j) for j, piece in enumerate(self.pieces) if j]

    def result(self):
        return [self.pieces[0]] + self.arrived


def by_rank(pieces):
    me = lax.axis_index("seq")
    return [lax.dynamic_index_in_dim(pieces, me ^ i, 0, keepdims=False) for i in range(pieces.shape[0])]


def tie(values, *sums):
    values, arrived = lax.optimization_barrier((values, [s.arrived for s in sums]))
    for s, a in zip(sums, arrived):
        s.arrived = a
    return values


def per_device(
    enc_input,
    dec_input,
    targets,
    lengths,
    attention_mats,
    expand_mats,
    reduce_mats,
    action_head,
    query_pos,
    vectors,
    expand_bias,
    *moments,
):
    ranks = lax.axis_size("seq")
    seq_index = lax.axis_index("seq")
    items, enc_part, width = enc_input.shape
    dec_part = dec_input.shape[1]
    joints = targets.shape[2]
    width_ff = expand_mats.shape[2]
    shard = attention_mats.shape[1]
    bias_part = expand_bias.shape[0]
    n_query, n_vec = query_pos.shape[0], vectors.shape[0]
    vec_at = (n_query + 7) // 8 * 8
    head_at = (vec_at + n_vec + 7) // 8 * 8
    n_small = (head_at + joints + 127) // 128 * 128
    devices = width // shard
    dec_rows = (n_query + 127) // 128 * 128

    reduce_t = jnp.swapaxes(reduce_mats, 1, 2)
    half_mats = to_half(attention_mats)
    half_expand = to_half(expand_mats)
    half_reduce = to_half(reduce_t)
    small_local = to_half(
        jnp.concatenate(
            [
                pad_to(query_pos.T, shard, vec_at),
                pad_to(vectors.T, shard, head_at - vec_at),
                pad_to(action_head, shard, n_small - head_at),
            ],
            axis=1,
        )
    )
    bias_local = to_half(jnp.pad(expand_bias, (0, shard * 128 - bias_part)).reshape(shard, 128))
    enc_all = gather(
        jnp.concatenate(
            [side_by_side(half_mats[0:4]), small_local, bias_local, half_expand[0], half_reduce[0]],
            axis=1,
        )
    )
    dec_all = gather(
        jnp.concatenate([side_by_side(half_mats[4:12]), half_expand[1], half_reduce[1]], axis=1)
    )

    assert items == ranks

    def swapped(pieces):
        swap = Swap(by_rank(pieces))
        swap.start()
        return swap.result()

    enc_x = jnp.concatenate(swapped(enc_input))
    dec_x = jnp.concatenate(by_rank(jnp.stack(swapped(dec_input))))
    dec_x = pad_to(dec_x, dec_rows, width)
    target = jnp.concatenate(by_rank(jnp.stack(swapped(targets))))
    target = pad_to(target, dec_rows, 128)
    turn = turn_matrix(width)
    table = sine_table(ranks * enc_part, width).reshape(ranks, enc_part, width)
    positions = jnp.concatenate(by_rank(jnp.asarray(table)))
    length = lengths[seq_index]
    valid = jnp.broadcast_to((jnp.arange(dec_rows) < length).astype(F32)[:, None], (dec_rows, 128))

    at = 4 * width
    enc_att = enc_all[:, :at]
    enc_ffn = enc_all[:, at + n_small + 128 :]
    small = enc_all[:, at : at + n_small].T
    bias_all = enc_all[:, at + n_small : at + n_small + 128].reshape(devices, shard * 128)
    bias_all = bias_all[:, :bias_part].reshape(1, 2 * width_ff).astype(F32)
    query_whole = pad_to(small[:n_query].astype(F32), dec_rows, width)
    vec = pad_to(small[vec_at : vec_at + n_vec].astype(F32), (n_vec + 7) // 8 * 8, width)
    head_t = pad_to(small[head_at : head_at + joints], 128, width)
    query, keys, values, mixed, log_total = attend(enc_x, positions, enc_att, vec)
    sum_one, hidden, u, sum_two, memory = feed_forward(
        mixed, enc_x, enc_att, vec, enc_ffn, bias_all[:, :width_ff]
    )
    memory, in_t, x_t, mixed_t, hidden_t = lax.optimization_barrier(
        (memory, *lefts(enc_x, positions, mixed, hidden, turn))
    )
    (
        w_keep, w_send, f_keep, f_send,
        dec_in_grad, query_grad, memory_grad, dec_vec_grads, head_grad_t, dec_bias_grad,
    ) = decode(
        dec_x, query_whole, target, valid, dec_all, head_t, vec, bias_all[:, width_ff:], memory, positions, turn,
        n_query, joints,
    )
    dec_ffn, dec_att = Sum([f_keep, f_send]), Sum([w_keep, w_send])
    dec_ffn.start()
    dec_att.start()
    two_grad, half_t, vec_grads_c = tie(last_norm_back(memory_grad, sum_two, vec, turn), dec_ffn, dec_att)
    dec_ffn.step()
    dec_swap = Swap(by_rank(dec_in_grad[:n_query].reshape(ranks, dec_part, width)))
    keep, send, one_grad, mixed_grad, vec_grads_b, enc_bias_grad, att_held = tie(
        [
            *feed_back(two_grad, half_t, sum_one, hidden_t, mixed_t, u, enc_att, enc_ffn, vec),
            (dec_att.blocks, dec_att.arrived),
        ],
        dec_ffn,
    )
    dec_att.blocks, dec_att.arrived = att_held
    dec_swap.start()
    enc_ffn_sum = Sum([keep, send])
    enc_ffn_sum.start()
    dec_ffn.step()
    dec_att.step()

    def back(so_far, part, grads):
        return attend_back(
            query, keys, values, mixed, mixed_grad, log_total, in_t, x_t, so_far, enc_att, part, 2, grads
        )

    keep, send, so_far, vec_grads_d = tie(back(one_grad, 0, ()), dec_ffn, dec_att, enc_ffn_sum)
    dec_ffn.step()
    dec_att.step()
    enc_ffn_sum.step()
    dec_grad = jnp.stack(by_rank(jnp.stack(dec_swap.result())))
    vec_grads = jnp.concatenate([vec_grads_b[:3], vec_grads_c[:3], dec_vec_grads[: n_vec - 8]])
    small_rows = jnp.concatenate(
        [
            pad_to(query_grad[:n_query], vec_at + 2, width),
            pad_to(vec_grads, head_at - vec_at - 2, width),
            pad_to(head_grad_t[:joints], n_small - head_at, width),
        ]
    )
    bias_grad = jnp.concatenate([enc_bias_grad, dec_bias_grad], axis=1).reshape(devices, bias_part)
    bias_grad = pad_to(bias_grad, devices, shard * 128).reshape(width, 128)
    small_grad = to_half(
        jnp.concatenate([mm_t(turn, to_half(small_rows)), mm(turn, to_half(bias_grad))], axis=1)
    )
    keep, send, enc_grad, vec_grads_e, small_grad = tie([*back(so_far, 1, (keep, send)), small_grad], dec_att)
    dec_att_total = dec_att.finish()
    late_rows = jnp.concatenate([vec_grads_d[:2], vec_grads_e[:2]], axis=1)
    late_grad = to_half(mm_t(turn, to_half(pad_to(late_rows, 128, width))))
    half = width // 2
    last = Sum(
        [
            jnp.concatenate([keep, small_grad[:half], late_grad[:half]], axis=1),
            jnp.concatenate([send, small_grad[half:], late_grad[half:]], axis=1),
        ]
    )
    last.start()
    enc_grad = tie(enc_grad, enc_ffn_sum, last)
    last.step()
    enc_ffn_sum.step()
    grad_swap = Swap([enc_grad[j * enc_part : (j + 1) * enc_part] for j in range(ranks)])
    grad_swap.start()
    dec_ffn_total = tie(dec_ffn.finish(), last, enc_ffn_sum)
    last.step()
    enc_ffn_total, last_total = enc_ffn_sum.finish(), last.finish()
    outputs = [jnp.stack(by_rank(jnp.stack(grad_swap.result()))), dec_grad]

    small_total = last_total[:, 3 * width :]
    gradients = (
        jnp.stack(
            [last_total[:, i * width : (i + 1) * width] for i in range(3)]
            + [enc_ffn_total[:, 2 * width_ff :]]
            + [dec_att_total[:, i * width : (i + 1) * width] for i in range(8)]
        ),
        jnp.stack([enc_ffn_total[:, :width_ff], dec_ffn_total[:, :width_ff]]),
        jnp.stack([enc_ffn_total[:, width_ff : 2 * width_ff], dec_ffn_total[:, width_ff:]]),
        small_total[:, head_at : head_at + joints],
        small_total[:, :n_query],
        jnp.concatenate(
            [small_total[:, n_small + 128 : n_small + 130], small_total[:, vec_at + 2 : vec_at + n_vec]], axis=1
        ),
        small_total[:, n_small : n_small + 128].reshape(1, -1)[:, :bias_part],
    )

    def views(mats, expand, reduce, head, query, vector, bias):
        return (mats, expand, jnp.swapaxes(reduce, 1, 2), head, query.T, vector.T, bias.reshape(1, -1))

    weights = views(attention_mats, expand_mats, reduce_mats, action_head, query_pos, vectors, expand_bias)
    firsts, seconds = views(*moments[:7]), views(*moments[7:])
    rates = (rate_matrix,) * 4 + (rate_vector,) * 3
    for i, results in enumerate(update(list(zip(weights, gradients, firsts, seconds)), rates)):
        if i == 2:
            results = [jnp.swapaxes(value, 1, 2) for value in results]
        if i in (4, 5):
            results = [value.T for value in results]
        if i == 6:
            results = [value.reshape(-1) for value in results]
        outputs.extend(results)
    return tuple(outputs)


def solution(mesh):
    rows = P("dp", "seq", None)
    weight_specs = (
        P(None, ALL, None),
        P(None, ALL, None),
        P(None, None, ALL),
        P(ALL, None),
        P(None, ALL),
        P(None, ALL),
        P(ALL),
    )
    in_specs = (rows, rows, rows, P("dp")) + weight_specs * 3
    out_specs = (rows, rows) + tuple(spec for spec in weight_specs for unused in range(4))
    return jax.shard_map(
        per_device, mesh=mesh, in_specs=in_specs, out_specs=out_specs, check_vma=False
    )
```

```python
import functools
import math

import jax
import jax.numpy as jnp
import numpy as np
from jax import lax
from jax.experimental import pallas as pl
from jax.experimental.pallas import tpu as pltpu
from jax.sharding import PartitionSpec as P

HEADS = 8
HDIM = 64
PAIR = 2 * HDIM
STEP = 10
ALL = ("dp", "seq")

beta_first = 0.9
beta_second = 0.999
epsilon = 1e-08
decay_rate = 0.1
rate_matrix = 0.08
rate_vector = 0.2

BF = jnp.bfloat16
F32 = jnp.float32
MB = 1 << 20
SCALE = HDIM ** (-0.5)


def to_half(values):
    return values.astype(BF)


def mm(a, b):
    return lax.dot_general(a, b, (((1,), (0,)), ((), ())), preferred_element_type=F32)


def mm_t(a, b):
    return lax.dot_general(a, b, (((1,), (1,)), ((), ())), preferred_element_type=F32)


def column_sum(values):
    return jnp.sum(values.astype(F32), axis=0, keepdims=True)


def norm_parts(values):
    center = values - jnp.mean(values, axis=-1, keepdims=True)
    scale = lax.rsqrt(jnp.mean(center * center, axis=-1, keepdims=True) + 1e-05)
    return center * scale, scale


def layer_norm(values, gain, shift):
    return norm_parts(values)[0] * gain + shift


def norm_back(values, gain, gradient):
    unit, scale = norm_parts(values)
    inner = gradient * gain
    mean_inner = jnp.mean(inner, axis=-1, keepdims=True)
    mean_cross = jnp.mean(inner * unit, axis=-1, keepdims=True)
    back = scale * (inner - mean_inner - unit * mean_cross)
    return back, column_sum(gradient * unit), column_sum(gradient)


GELU_A = math.sqrt(2.0 / math.pi)
GELU_B = 0.044715


def gelu_parts(u):
    square = u * u
    bend = jnp.tanh(u * (GELU_A + GELU_A * GELU_B * square))
    half = 0.5 + 0.5 * bend
    slope = half + (0.5 * u) * (1.0 - bend * bend) * (GELU_A + 3.0 * GELU_A * GELU_B * square)
    return u * half, slope


def gelu(u):
    return u * (0.5 + 0.5 * jnp.tanh(u * (GELU_A + GELU_A * GELU_B * (u * u))))


def sine_table(count, width):
    halves = np.arange(width // 2, dtype=np.float64)
    frequency = np.exp(halves * (-2.0 * math.log(10000.0) / width))
    angles = np.arange(count)[:, None] * frequency[None, :]
    table = np.stack([np.sin(angles), np.cos(angles)], axis=-1).reshape(count, width)
    return table.astype(np.float32)


def own_lanes(values, h):
    lane = lax.broadcasted_iota(jnp.int32, values.shape, 1)
    return jnp.where((lane < HDIM) == (h == 0), values, jnp.zeros_like(values))


def join_rows(first, second):
    row = lax.broadcasted_iota(jnp.int32, first.shape, 0)
    return jnp.where(row < HDIM, first, second)


def attend_kernel(
    x_ref, pos_ref, wq_ref, wk_ref, wv_ref, vec_ref, q_ref, k_ref, v_ref, o_ref, log_ref, in_ref, vt_ref, *, chunk
):
    @pl.when(pl.program_id(0) == 0)
    def _():
        in_ref[...] = to_half(x_ref[...].astype(F32) + pos_ref[...])

    q_ref[...] = to_half(mm(in_ref[...], wq_ref[...]) + vec_ref[0:1, :])
    k_ref[...] = to_half(mm(in_ref[...], wk_ref[...]))
    values = to_half(mm(x_ref[...], wv_ref[...]) + vec_ref[1:2, :])
    v_ref[...] = values
    vt_ref[...] = values.T

    def step(i, carry):
        at = pl.ds(i * chunk, chunk)
        query = q_ref[at, :] * BF(SCALE)
        mixed = []
        for h in range(2):
            scores = mm_t(k_ref[...], own_lanes(query, h))
            peak = jnp.max(scores, axis=0, keepdims=True)
            weights = jnp.exp(scores - peak)
            total = jnp.sum(weights, axis=0, keepdims=True)
            mixed.append(mm(vt_ref[...], to_half(weights)) / total)
            log_ref[0, pl.ds(h, 1), at] = peak + jnp.log(total)
        o_ref[at, :] = to_half(join_rows(*mixed).T)
        return carry

    lax.fori_loop(0, q_ref.shape[0] // chunk, step, 0)


def attend(x, positions, weights, vec):
    rows, width = x.shape
    pairs = width // PAIR
    whole = pl.BlockSpec((rows, width), lambda i: (0, 0))
    own = pl.BlockSpec((rows, PAIR), lambda i: (0, i))
    mats = [pl.BlockSpec((width, PAIR), lambda i, j=j: (0, i + j * pairs)) for j in range(3)]
    half = jax.ShapeDtypeStruct((rows, width), BF)
    return pl.pallas_call(
        functools.partial(attend_kernel, chunk=256),
        grid=(pairs,),
        in_specs=[whole, whole] + mats + [pl.BlockSpec((vec.shape[0], PAIR), lambda i: (0, i))],
        out_specs=[own] * 4 + [pl.BlockSpec((1, 2, rows), lambda i: (i, 0, 0))],
        out_shape=[half] * 4 + [jax.ShapeDtypeStruct((pairs, 2, rows), F32)],
        scratch_shapes=[pltpu.VMEM((rows, width), BF), pltpu.VMEM((PAIR, rows), BF)],
        compiler_params=pltpu.CompilerParams(vmem_limit_bytes=56 * MB),
        cost_estimate=pl.CostEstimate(
            flops=16 * rows * rows * width, bytes_accessed=12 * rows * width, transcendentals=8 * rows * rows
        ),
        name="attend",
    )(x, positions, weights, weights, weights, vec)


def forward_kernel(
    mixed_ref, x_ref, out_ref, vec_ref, e_top_ref, e_bottom_ref, r_top_ref, r_bottom_ref, turn_ref, bias_ref,
    sum_one_ref, hidden_ref, u_ref, sum_two_ref, memory_ref, e_ref, r_ref, *, tile
):
    step = pl.program_id(0)
    count = x_ref.shape[0] // tile

    def rows_of(i):
        return pl.ds(pl.multiple_of(i * tile, tile), tile)

    @pl.when(step == 0)
    def _():
        def body(i, carry):
            at = rows_of(i)
            total = x_ref[at, :].astype(F32) + mm(mixed_ref[at, :], out_ref[...]) + vec_ref[2:3, :]
            sum_one_ref[at, :] = total
            hidden = layer_norm(total, vec_ref[3:4, :], vec_ref[4:5, :])
            hidden_ref[at, :] = to_half(hidden)
            sum_two_ref[at, :] = hidden + vec_ref[5:6, :]
            return carry

        lax.fori_loop(0, count, body, 0)

    cut = e_top_ref.shape[0]
    for top_ref, bottom_ref, to_ref in ((e_top_ref, e_bottom_ref, e_ref), (r_top_ref, r_bottom_ref, r_ref)):
        to_ref[...] = to_half(mm(turn_ref[:, :cut], top_ref[...]) + mm(turn_ref[:, cut:], bottom_ref[...]))

    def body(i, carry):
        at = rows_of(i)
        u = mm(hidden_ref[at, :], e_ref[...]) + bias_ref[...]
        u_ref[at, :] = u
        sum_two_ref[at, :] += mm_t(to_half(gelu(u)), r_ref[...])
        return carry

    lax.fori_loop(0, count, body, 0)

    @pl.when(step == pl.num_programs(0) - 1)
    def _():
        def body(i, carry):
            at = rows_of(i)
            memory_ref[at, :] = layer_norm(sum_two_ref[at, :], vec_ref[6:7, :], vec_ref[7:8, :])
            return carry

        lax.fori_loop(0, count, body, 0)


def feed_forward(mixed, x, enc_mats, vec, top, bottom, turn_back, bias):
    rows, width = x.shape
    width_ff = bias.shape[1]
    block = 640 if width_ff % 640 == 0 else width_ff
    steps = width_ff // block
    whole = pl.BlockSpec((rows, width), lambda i: (0, 0))
    column = pl.BlockSpec((width // 2, block), lambda i: (0, i))
    other = pl.BlockSpec((width // 2, block), lambda i: (0, i + steps))
    float_rows = jax.ShapeDtypeStruct((rows, width), F32)
    return pl.pallas_call(
        functools.partial(forward_kernel, tile=256),
        grid=(steps,),
        in_specs=[
            whole,
            whole,
            pl.BlockSpec((width, width), lambda i: (0, 3)),
            pl.BlockSpec(vec.shape, lambda i: (0, 0)),
            column,
            column,
            other,
            other,
            pl.BlockSpec((width, width), lambda i: (0, 0)),
            pl.BlockSpec((1, block), lambda i: (0, i)),
        ],
        out_specs=[whole, whole, pl.BlockSpec((rows, block), lambda i: (0, i)), whole, whole]
        + [pl.BlockSpec((width, block), lambda i: (0, i))] * 2,
        out_shape=[
            float_rows,
            jax.ShapeDtypeStruct((rows, width), BF),
            jax.ShapeDtypeStruct((rows, width_ff), F32),
            float_rows,
            float_rows,
        ]
        + [jax.ShapeDtypeStruct((width, width_ff), BF)] * 2,
        compiler_params=pltpu.CompilerParams(vmem_limit_bytes=56 * MB),
        cost_estimate=pl.CostEstimate(
            flops=4 * rows * width * width_ff, bytes_accessed=4 * rows * width_ff, transcendentals=rows * width_ff
        ),
        name="feed_forward",
    )(mixed, x, enc_mats, vec, top, bottom, top, bottom, turn_back, bias)


def turned(turn, values):
    return to_half(mm_t(turn, values))


def lefts_kernel(x_ref, pos_ref, mixed_ref, hidden_ref, turn_ref, in_t_ref, x_t_ref, mixed_t_ref, hidden_t_ref):
    in_t_ref[...] = turned(turn_ref[...], to_half(x_ref[...].astype(F32) + pos_ref[...]))
    x_t_ref[...] = turned(turn_ref[...], x_ref[...])
    mixed_t_ref[...] = turned(turn_ref[...], mixed_ref[...])
    hidden_t_ref[...] = turned(turn_ref[...], hidden_ref[...])


def lefts(x, positions, mixed, hidden, turn):
    rows, width = x.shape
    return pl.pallas_call(
        lefts_kernel,
        out_shape=[jax.ShapeDtypeStruct((width, rows), BF)] * 4,
        compiler_params=pltpu.CompilerParams(vmem_limit_bytes=40 * MB),
        cost_estimate=pl.CostEstimate(flops=8 * rows * width * width, bytes_accessed=20 * rows * width, transcendentals=0),
        name="lefts",
    )(x, positions, mixed, hidden, turn)


def norm_kernel(grad_ref, sum_two_ref, vec_ref, turn_ref, two_ref, half_t_ref, vec_grad_ref, half_ref, *, tile):
    vec_grad_ref[...] = jnp.zeros_like(vec_grad_ref)

    def body(i, carry):
        at = pl.ds(pl.multiple_of(i * tile, tile), tile)
        back, gain, shift = norm_back(sum_two_ref[at, :], vec_ref[6:7, :], grad_ref[at, :])
        two_ref[at, :] = back
        half_ref[at, :] = to_half(back)
        vec_grad_ref[0:1, :] += column_sum(back)
        vec_grad_ref[1:2, :] += gain
        vec_grad_ref[2:3, :] += shift
        return carry

    lax.fori_loop(0, grad_ref.shape[0] // tile, body, 0)
    half_t_ref[...] = turned(turn_ref[...], half_ref[...])


def last_norm_back(grad, sum_two, vec, turn):
    rows, width = grad.shape
    return pl.pallas_call(
        functools.partial(norm_kernel, tile=256),
        out_shape=[
            jax.ShapeDtypeStruct((rows, width), F32),
            jax.ShapeDtypeStruct((width, rows), BF),
            jax.ShapeDtypeStruct((8, width), F32),
        ],
        scratch_shapes=[pltpu.VMEM((rows, width), BF)],
        compiler_params=pltpu.CompilerParams(vmem_limit_bytes=40 * MB),
        cost_estimate=pl.CostEstimate(flops=2 * rows * width * width, bytes_accessed=14 * rows * width, transcendentals=0),
        name="last_norm_back",
    )(grad, sum_two, vec, turn)


def backward_kernel(
    grad_ref, half_t_ref, sum_one_ref, hidden_t_ref, mixed_t_ref, u_ref, e_ref, r_ref, out_ref, vec_ref,
    keep_ref, send_ref, one_ref, mixed_grad_ref, vec_grad_ref, bias_ref,
    two_ref, half_ref, act_ref, inner_ref, *, tile
):
    step = pl.program_id(0)
    rows, width = sum_one_ref.shape
    count = rows // tile
    cut = width // 2

    def rows_of(i):
        return pl.ds(pl.multiple_of(i * tile, tile), tile)

    @pl.when(step == 0)
    def _():
        two_ref[...] = grad_ref[...]
        half_ref[...] = to_half(grad_ref[...])

    bias_ref[...] = jnp.zeros_like(bias_ref)

    def body(i, carry):
        at = rows_of(i)
        act, slope = gelu_parts(u_ref[at, :])
        act_ref[at, :] = to_half(act)
        inner = to_half(mm(half_ref[at, :], r_ref[...]) * slope)
        inner_ref[at, :] = inner
        bias_ref[...] += column_sum(inner)
        two_ref[at, :] += mm_t(inner, e_ref[...])
        return carry

    lax.fori_loop(0, count, body, 0)
    block = u_ref.shape[1]
    steps = pl.num_programs(0)

    def set_grad(at, grad):
        at = pl.ds(pl.multiple_of(at, 128), grad.shape[1])
        keep_ref[:, at] = to_half(grad[:cut])
        send_ref[:, at] = to_half(grad[cut:])

    set_grad(step * block, mm(hidden_t_ref[...], inner_ref[...]))
    set_grad((step + steps) * block, mm(half_t_ref[...], act_ref[...]))

    @pl.when(step == pl.num_programs(0) - 1)
    def _():
        vec_grad_ref[...] = jnp.zeros_like(vec_grad_ref)

        def body(i, carry):
            at = rows_of(i)
            back, gain, shift = norm_back(sum_one_ref[at, :], vec_ref[3:4, :], two_ref[at, :])
            one_ref[at, :] = back
            half = to_half(back)
            half_ref[at, :] = half
            mixed_grad_ref[at, :] = to_half(mm_t(half, out_ref[...]))
            vec_grad_ref[0:1, :] += column_sum(back)
            vec_grad_ref[1:2, :] += gain
            vec_grad_ref[2:3, :] += shift
            return carry

        lax.fori_loop(0, count, body, 0)
        set_grad(2 * steps * block, mm(mixed_t_ref[...], half_ref[...]))


def feed_back(grad, half_t, sum_one, hidden_t, mixed_t, u, enc_mats, expand, reduce_t, vec):
    rows, width = sum_one.shape
    width_ff = u.shape[1]
    block = 640 if width_ff % 640 == 0 else width_ff
    steps = width_ff // block
    cut = width // 2
    whole = pl.BlockSpec((rows, width), lambda i: (0, 0))
    whole_t = pl.BlockSpec((width, rows), lambda i: (0, 0))
    grads = (cut, 2 * width_ff + width)
    return pl.pallas_call(
        functools.partial(backward_kernel, tile=256),
        grid=(steps,),
        in_specs=[
            whole,
            whole_t,
            whole,
            whole_t,
            whole_t,
            pl.BlockSpec((rows, block), lambda i: (0, i)),
            pl.BlockSpec((width, block), lambda i: (0, i)),
            pl.BlockSpec((width, block), lambda i: (0, i)),
            pl.BlockSpec((width, width), lambda i: (0, 3)),
            pl.BlockSpec(vec.shape, lambda i: (0, 0)),
        ],
        out_specs=[pl.BlockSpec(grads, lambda i: (0, 0))] * 2
        + [
            whole,
            whole,
            pl.BlockSpec((8, width), lambda i: (0, 0)),
            pl.BlockSpec((1, block), lambda i: (0, i)),
        ],
        out_shape=[jax.ShapeDtypeStruct(grads, BF)] * 2
        + [
            jax.ShapeDtypeStruct((rows, width), F32),
            jax.ShapeDtypeStruct((rows, width), BF),
            jax.ShapeDtypeStruct((8, width), F32),
            jax.ShapeDtypeStruct((1, width_ff), F32),
        ],
        scratch_shapes=[
            pltpu.VMEM((rows, width), F32),
            pltpu.VMEM((rows, width), BF),
            pltpu.VMEM((rows, block), BF),
            pltpu.VMEM((rows, block), BF),
        ],
        compiler_params=pltpu.CompilerParams(vmem_limit_bytes=60 * MB),
        cost_estimate=pl.CostEstimate(
            flops=8 * rows * width * width_ff, bytes_accessed=6 * rows * width_ff, transcendentals=rows * width_ff
        ),
        name="feed_back",
    )(grad, half_t, sum_one, hidden_t, mixed_t, u, expand, reduce_t, enc_mats, vec)


def attend_back_kernel(
    q_ref, k_ref, v_ref, o_ref, g_ref, log_ref, in_t_ref, x_t_ref, one_ref, wq_ref, wk_ref, wv_ref, *refs, chunk, first
):
    keep_ref, send_ref, grad_ref, vec_ref, kt_ref, dx_ref, dq_ref, dk_ref, dv_ref = refs[-9:]
    step_at = pl.program_id(0)
    width = x_t_ref.shape[0]
    cut = width // 2

    @pl.when(step_at == 0)
    def _():
        dx_ref[...] = one_ref[...]
        if first:
            keep_ref[...] = refs[0][...]
            send_ref[...] = refs[1][...]

    kt_ref[...] = k_ref[...].T
    dk_ref[...] = jnp.zeros_like(dk_ref)
    dv_ref[...] = jnp.zeros_like(dv_ref)

    def step(i, carry):
        at = pl.ds(i * chunk, chunk)
        query = q_ref[at, :] * BF(SCALE)
        grad = g_ref[at, :]
        cross = (grad.astype(F32) * o_ref[at, :].astype(F32)).T
        back = []
        for h in range(2):
            own, own_grad = own_lanes(query, h), own_lanes(grad, h)
            weighted = jnp.sum(cross[h * HDIM : (h + 1) * HDIM], axis=0, keepdims=True)
            probs = jnp.exp(mm_t(k_ref[...], own) - log_ref[0, pl.ds(h, 1), at])
            score_grad = to_half(probs * (mm_t(v_ref[...], own_grad) - weighted))
            dv_ref[...] += mm(to_half(probs), own_grad)
            dk_ref[...] += mm(score_grad, own)
            back.append(mm(kt_ref[...], score_grad))
        dq_ref[at, :] = to_half((join_rows(*back) * SCALE).T)
        return carry

    lax.fori_loop(0, q_ref.shape[0] // chunk, step, 0)
    dq = dq_ref[...]
    dk = to_half(dk_ref[...])
    dv = to_half(dv_ref[...])
    dx_ref[...] += mm_t(dq, wq_ref[...]) + mm_t(dk, wk_ref[...]) + mm_t(dv, wv_ref[...])
    for j, (left_ref, right) in enumerate(((in_t_ref, dq), (in_t_ref, dk), (x_t_ref, dv))):
        wgrad = to_half(mm(left_ref[...], right))
        at = pl.ds(pl.multiple_of(j * width + (first + step_at) * PAIR, PAIR), PAIR)
        keep_ref[:, at] = wgrad[:cut]
        send_ref[:, at] = wgrad[cut:]
    vec_ref[...] = jnp.zeros_like(vec_ref)
    vec_ref[0:1, :] = column_sum(dq)
    vec_ref[1:2, :] = column_sum(dv)

    @pl.when(step_at == pl.num_programs(0) - 1)
    def _():
        grad_ref[...] = dx_ref[...].astype(grad_ref.dtype)


def attend_back(query, keys, values, mixed, grad, log_total, in_t, x_t, so_far, enc_mats, first, count, grads):
    rows, width = query.shape
    pairs = width // PAIR
    cut = width // 2
    own = pl.BlockSpec((rows, PAIR), lambda i: (0, i + first))
    whole = pl.BlockSpec((rows, width), lambda i: (0, 0))
    whole_t = pl.BlockSpec((width, rows), lambda i: (0, 0))
    mats = [pl.BlockSpec((width, PAIR), lambda i, j=j: (0, i + first + j * pairs)) for j in range(3)]
    three = pl.BlockSpec((cut, 3 * width), lambda i: (0, 0))
    return pl.pallas_call(
        functools.partial(attend_back_kernel, chunk=256, first=first),
        grid=(count,),
        in_specs=[own] * 5
        + [pl.BlockSpec((1, 2, rows), lambda i: (i + first, 0, 0)), whole_t, whole_t, whole]
        + mats
        + [three] * len(grads),
        out_specs=[three, three, whole, pl.BlockSpec((8, PAIR), lambda i: (0, i))],
        out_shape=[jax.ShapeDtypeStruct((cut, 3 * width), BF)] * 2
        + [
            jax.ShapeDtypeStruct((rows, width), BF if first + count == pairs else F32),
            jax.ShapeDtypeStruct((8, count * PAIR), F32),
        ],
        scratch_shapes=[
            pltpu.VMEM((PAIR, rows), BF),
            pltpu.VMEM((rows, width), F32),
            pltpu.VMEM((rows, PAIR), BF),
            pltpu.VMEM((rows, PAIR), F32),
            pltpu.VMEM((rows, PAIR), F32),
        ],
        compiler_params=pltpu.CompilerParams(vmem_limit_bytes=60 * MB),
        cost_estimate=pl.CostEstimate(
            flops=10 * rows * rows * width * count, bytes_accessed=16 * rows * width, transcendentals=4 * rows * rows
        ),
        name="attend_back",
    )(query, keys, values, mixed, grad, log_total, in_t, x_t, so_far, enc_mats, enc_mats, enc_mats, *grads)


def heads_forward(query, key_ref, value_ref, prob_ref, n_keys):
    outs = []
    for pair in range(HEADS // 2):
        lanes = slice(pair * PAIR, (pair + 1) * PAIR)
        keys = key_ref[:, lanes]
        values_t = value_ref[:, lanes].T
        scaled = query[:, lanes] * BF(SCALE)
        mixed = []
        for h in range(2):
            scores = mm_t(keys, own_lanes(scaled, h))
            if n_keys < keys.shape[0]:
                row = lax.broadcasted_iota(jnp.int32, scores.shape, 0)
                scores = jnp.where(row < n_keys, scores, -jnp.inf)
            weights = jnp.exp(scores - jnp.max(scores, axis=0, keepdims=True))
            probs = weights * (1.0 / jnp.sum(weights, axis=0, keepdims=True))
            prob_ref[2 * pair + h] = probs
            mixed.append(mm(values_t, to_half(probs)))
        outs.append(to_half(join_rows(*mixed).T))
    return jnp.concatenate(outs, axis=1)


def heads_back(query, key_ref, value_ref, prob_ref, grad, dk_ref, dv_ref):
    outs = []
    for pair in range(HEADS // 2):
        lanes = slice(pair * PAIR, (pair + 1) * PAIR)
        keys_t = key_ref[:, lanes].T
        values = value_ref[:, lanes]
        scaled = query[:, lanes] * BF(SCALE)
        dk = dv = None
        back = []
        for h in range(2):
            own, own_grad = own_lanes(scaled, h), own_lanes(grad[:, lanes], h)
            probs = prob_ref[2 * pair + h]
            prob_grad = mm_t(values, own_grad)
            weighted = jnp.sum(probs * prob_grad, axis=0, keepdims=True)
            score_grad = to_half(probs * (prob_grad - weighted))
            back.append(mm(keys_t, score_grad))
            k_part, v_part = mm(score_grad, own), mm(to_half(probs), own_grad)
            dk = k_part if h == 0 else dk + k_part
            dv = v_part if h == 0 else dv + v_part
        dk_ref[:, lanes] = to_half(dk)
        dv_ref[:, lanes] = to_half(dv)
        outs.append(to_half((join_rows(*back) * SCALE).T))
    return jnp.concatenate(outs, axis=1)


def decode_kernel(
    x_ref, query_ref, target_ref, valid_ref, w_ref, head_ref, vec_ref, bias_ref, mem_ref, pos_ref, turn_ref,
    w_keep_ref, w_send_ref, f_keep_ref, f_send_ref, in_grad_ref, query_grad_ref, mem_grad_ref, vec_grad_ref, head_grad_ref, bias_grad_ref,
    mem_in, mem_half, cross_k, cross_v, cross_dk, cross_dv, cross_p,
    self_k, self_v, self_dk, self_dv, self_p, u_ref, act_ref, acc_ref, left_ref, *, n_steps, joints, block
):
    width = x_ref.shape[1]
    width_ff = u_ref.shape[1]
    blocks = width_ff // block
    first = 8 * width
    second = first + width_ff

    def mat(i):
        return w_ref[:, i * width : (i + 1) * width]

    cut = width // 2

    def left_of(values):
        return turned(turn_ref[...], values)

    def set_mat(i, left_t, right):
        grad = to_half(mm(left_t, right))
        w_keep_ref[:, i * width : (i + 1) * width] = grad[:cut]
        w_send_ref[:, i * width : (i + 1) * width] = grad[cut:]

    def set_ffn(at, left_t, right):
        grad = to_half(mm(left_t, right))
        f_keep_ref[:, at] = grad[:cut]
        f_send_ref[:, at] = grad[cut:]

    def vec(i):
        return vec_ref[i : i + 1, :]

    def set_vec(i, value):
        vec_grad_ref[i - 8 : i - 7, :] = value

    def lanes(i, start=0):
        return pl.ds(pl.multiple_of(start + i * block, 128), block)

    vec_grad_ref[...] = jnp.zeros_like(vec_grad_ref)
    x = x_ref[...]
    x_float = x.astype(F32)
    places = query_ref[...]
    self_in = to_half(x_float + places)
    self_q = to_half(mm(self_in, mat(0)) + vec(8))
    self_k[...] = to_half(mm(self_in, mat(1)))
    self_v[...] = to_half(mm(x, mat(2)) + vec(9))
    self_mixed = heads_forward(self_q, self_k, self_v, self_p, n_steps)
    sum_one = x_float + mm(self_mixed, mat(3)) + vec(10)
    one = layer_norm(sum_one, vec(11), vec(12))
    cross_in = to_half(one + places)
    cross_q = to_half(mm(cross_in, mat(4)) + vec(13))
    mem_in[...] = to_half(mem_ref[...] + pos_ref[...])
    mem_half[...] = to_half(mem_ref[...])
    cross_k[...] = to_half(mm(mem_in[...], mat(5)))
    cross_v[...] = to_half(mm(mem_half[...], mat(6)) + vec(14))
    cross_mixed = heads_forward(cross_q, cross_k, cross_v, cross_p, cross_k.shape[0])
    sum_two = one + mm(cross_mixed, mat(7)) + vec(15)
    two = layer_norm(sum_two, vec(16), vec(17))
    two_half = to_half(two)
    acc_ref[...] = two + vec(18)

    def forward(i, carry):
        u = mm(two_half, w_ref[:, lanes(i, first)]) + bias_ref[:, lanes(i)]
        u_ref[:, lanes(i)] = u
        acc_ref[...] += mm_t(to_half(gelu(u)), w_ref[:, lanes(i, second)])
        return carry

    lax.fori_loop(0, blocks, forward, 0)
    sum_three = acc_ref[...]
    three_half = to_half(layer_norm(sum_three, vec(19), vec(20)))
    error = mm_t(three_half, head_ref[...]) - target_ref[...]
    pred_grad = to_half(error * lax.rsqrt(error * error + 1.0) * valid_ref[...] / joints)
    head_grad_ref[...] = mm(pred_grad.T, three_half)
    sum_three_grad, gain, shift = norm_back(sum_three, vec(19), mm(pred_grad, head_ref[...]))
    set_vec(18, column_sum(sum_three_grad))
    set_vec(19, gain)
    set_vec(20, shift)
    out_grad = to_half(sum_three_grad)
    left_ref[0] = left_of(out_grad)
    left_ref[1] = left_of(two_half)
    acc_ref[...] = sum_three_grad

    def backward(i, carry):
        act, slope = gelu_parts(u_ref[:, lanes(i)])
        inner = to_half(mm(out_grad, w_ref[:, lanes(i, second)]) * slope)
        bias_grad_ref[:, lanes(i)] = column_sum(inner)
        acc_ref[...] += mm_t(inner, w_ref[:, lanes(i, first)])
        set_ffn(lanes(i), left_ref[1], inner)
        set_ffn(lanes(i, width_ff), left_ref[0], to_half(act))
        return carry

    lax.fori_loop(0, blocks, backward, 0)
    sum_two_grad, gain, shift = norm_back(sum_two, vec(16), acc_ref[...])
    set_vec(15, column_sum(sum_two_grad))
    set_vec(16, gain)
    set_vec(17, shift)
    out_grad = to_half(sum_two_grad)
    set_mat(7, left_of(cross_mixed), out_grad)
    mixed_grad = to_half(mm_t(out_grad, mat(7)))
    cross_dq = heads_back(cross_q, cross_k, cross_v, cross_p, mixed_grad, cross_dk, cross_dv)
    set_vec(13, column_sum(cross_dq))
    set_vec(14, column_sum(cross_dv[...]))
    mem_grad_ref[...] = mm_t(cross_dk[...], mat(5)) + mm_t(cross_dv[...], mat(6))
    set_mat(4, left_of(cross_in), cross_dq)
    set_mat(5, left_of(mem_in[...]), cross_dk[...])
    set_mat(6, left_of(mem_half[...]), cross_dv[...])
    cross_in_grad = mm_t(cross_dq, mat(4))
    sum_one_grad, gain, shift = norm_back(sum_one, vec(11), sum_two_grad + cross_in_grad)
    set_vec(10, column_sum(sum_one_grad))
    set_vec(11, gain)
    set_vec(12, shift)
    out_grad = to_half(sum_one_grad)
    set_mat(3, left_of(self_mixed), out_grad)
    mixed_grad = to_half(mm_t(out_grad, mat(3)))
    self_dq = heads_back(self_q, self_k, self_v, self_p, mixed_grad, self_dk, self_dv)
    set_vec(8, column_sum(self_dq))
    set_vec(9, column_sum(self_dv[...]))
    in_t = left_of(self_in)
    set_mat(0, in_t, self_dq)
    set_mat(1, in_t, self_dk[...])
    set_mat(2, left_of(x), self_dv[...])
    self_in_grad = mm_t(self_dq, mat(0)) + mm_t(self_dk[...], mat(1))
    in_grad_ref[...] = to_half(sum_one_grad + self_in_grad + mm_t(self_dv[...], mat(2)))
    query_grad_ref[...] = self_in_grad + cross_in_grad


def decode(x, places, target, valid, weights, head_t, vec, bias, memory, positions, turn, n_steps, joints):
    rows, width = x.shape
    mem_rows = memory.shape[0]
    width_ff = bias.shape[1]
    half = lambda n: pltpu.VMEM((n, width), BF)
    return pl.pallas_call(
        functools.partial(
            decode_kernel, n_steps=n_steps, joints=joints, block=640 if width_ff % 640 == 0 else width_ff
        ),
        out_shape=[
            jax.ShapeDtypeStruct((width // 2, 8 * width), BF),
            jax.ShapeDtypeStruct((width // 2, 8 * width), BF),
            jax.ShapeDtypeStruct((width // 2, 2 * width_ff), BF),
            jax.ShapeDtypeStruct((width // 2, 2 * width_ff), BF),
            jax.ShapeDtypeStruct((rows, width), BF),
            jax.ShapeDtypeStruct((rows, width), F32),
            jax.ShapeDtypeStruct((mem_rows, width), F32),
            jax.ShapeDtypeStruct((16, width), F32),
            jax.ShapeDtypeStruct(head_t.shape, F32),
            jax.ShapeDtypeStruct((1, width_ff), F32),
        ],
        scratch_shapes=[half(mem_rows)] * 6
        + [pltpu.VMEM((HEADS, mem_rows, rows), F32)]
        + [half(rows)] * 4
        + [
            pltpu.VMEM((HEADS, rows, rows), F32),
            pltpu.VMEM((rows, width_ff), F32),
            pltpu.VMEM((rows, width_ff), BF),
            pltpu.VMEM((rows, width), F32),
            pltpu.VMEM((2, width, rows), BF),
        ],
        compiler_params=pltpu.CompilerParams(vmem_limit_bytes=60 * MB),
        cost_estimate=pl.CostEstimate(
            flops=12 * mem_rows * width * width, bytes_accessed=4 * weights.size, transcendentals=rows * width_ff
        ),
        name="decode",
    )(x, places, target, valid, weights, head_t, vec, bias, memory, positions, turn)


def adamw(weight, gradient, moment_one, moment_two, step_rate):
    moment_one = beta_first * moment_one + (1.0 - beta_first) * gradient
    moment_two = beta_second * moment_two + (1.0 - beta_second) * gradient * gradient
    mean_hat = moment_one / (1.0 - beta_first**STEP)
    square_hat = moment_two / (1.0 - beta_second**STEP)
    updated = weight - step_rate * (
        mean_hat / (jnp.sqrt(square_hat) + epsilon) + decay_rate * weight
    )
    return (moment_one, moment_two, updated, updated.astype(BF))


def update_kernel(*refs, rates):
    count = len(rates)
    ins, outs = refs[: 4 * count], refs[4 * count :]
    for i, rate in enumerate(rates):
        values = adamw(*(ref[...] for ref in ins[4 * i : 4 * i + 4]), rate)
        for ref, value in zip(outs[4 * i : 4 * i + 4], values):
            ref[...] = value


def update(groups, rates):
    shapes = []
    for group in groups:
        shapes += [jax.ShapeDtypeStruct(group[0].shape, F32)] * 3
        shapes.append(jax.ShapeDtypeStruct(group[0].shape, BF))
    outs = pl.pallas_call(
        functools.partial(update_kernel, rates=rates),
        out_shape=shapes,
        compiler_params=pltpu.CompilerParams(vmem_limit_bytes=56 * MB),
        name="update",
    )(*(array for group in groups for array in group))
    return [outs[4 * i : 4 * i + 4] for i in range(len(groups))]


def pad_to(values, rows, columns):
    return jnp.pad(values, ((0, rows - values.shape[0]), (0, columns - values.shape[1])))


def side_by_side(mats):
    return jnp.concatenate([mats[i] for i in range(mats.shape[0])], axis=1)


def gather(columns):
    return lax.all_gather(columns, ALL, axis=0, tiled=True)


def width_bits(axis):
    return (lax.axis_size(axis) - 1).bit_length()


def bit_groups(one_by_one=False):
    low = width_bits("seq")
    others = list(range(low + width_bits("dp") - 1, low, -1))
    groups = [[low]]
    for bits, most in ((others, 2), (list(range(low)), 1 if one_by_one else 2)):
        groups += [bits[i : i + most] for i in range(0, len(bits), most)]
    return groups


def spread(bits, place):
    return sum(((place >> k) & 1) << bit for k, bit in enumerate(reversed(bits)))


def turn_matrices(width):
    order = [bit for bits in bit_groups() for bit in bits]
    devices = 1 << len(order)
    relative = np.array([spread(order, j) for j in range(devices)], np.int32)
    shard = width // devices
    source = jnp.bitwise_xor(jnp.asarray(relative), lax.axis_index(ALL).astype(jnp.int32))
    source = (source[:, None] * shard + jnp.arange(shard, dtype=jnp.int32)[None, :]).reshape(width)
    places = jnp.arange(width, dtype=jnp.int32)
    return (source[:, None] == places[None, :]).astype(BF), (source[None, :] == places[:, None]).astype(BF)


def exchange(values, distance):
    low = width_bits("seq")
    axis, distance = ("dp", distance >> low) if distance >> low else ("seq", distance)
    pairs = [(i, i ^ distance) for i in range(lax.axis_size(axis))]
    return lax.ppermute(values, axis, pairs)


class Sum:
    def __init__(self, blocks, one_by_one=False):
        self.blocks = list(blocks)
        self.groups = bit_groups(one_by_one)
        self.arrived = None

    def start(self):
        bits = self.groups.pop(0)
        self.arrived = [exchange(block, spread(bits, j)) for j, block in enumerate(self.blocks) if j]

    def add(self):
        arrays = [self.blocks[0]] + self.arrived
        count = 1 << len(self.groups[0]) if self.groups else 1
        rows = arrays[0].shape[-2] // count
        totals = []
        for j in range(count):
            parts = [array[..., j * rows : (j + 1) * rows, :].astype(F32) for array in arrays]
            total = functools.reduce(jnp.add, parts)
            totals.append(to_half(total) if self.groups else total)
        self.blocks = totals
        self.arrived = None

    def step(self):
        self.add()
        if self.groups:
            self.start()

    def finish(self):
        while self.groups or self.arrived is not None:
            if self.arrived is None:
                self.start()
            self.step()
        return self.blocks[0]


class Gather:
    def __init__(self, value):
        self.value = value
        self.groups = bit_groups()
        self.arrived = None

    def start(self):
        bits = self.groups.pop()
        self.arrived = [exchange(self.value, spread(bits, j)) for j in range(1, 1 << len(bits))]

    def step(self):
        if not self.groups:
            return self.value, self.arrived[0]
        self.value = jnp.concatenate([self.value] + self.arrived)
        self.start()

    def up_to_last(self):
        while len(self.groups) > 1:
            self.step()

    def finish(self):
        halves = self.step()
        while halves is None:
            halves = self.step()
        return halves


def swap(pieces):
    return lax.all_to_all(pieces, "seq", 0, 0, tiled=True)


def tie(values, *sums):
    values, arrived = lax.optimization_barrier((values, [s.arrived for s in sums]))
    for s, a in zip(sums, arrived):
        s.arrived = a
    return values


def per_device(
    enc_input,
    dec_input,
    targets,
    lengths,
    attention_mats,
    expand_mats,
    reduce_mats,
    action_head,
    query_pos,
    vectors,
    expand_bias,
    *moments,
):
    ranks = lax.axis_size("seq")
    seq_index = lax.axis_index("seq")
    items, enc_part, width = enc_input.shape
    dec_part = dec_input.shape[1]
    joints = targets.shape[2]
    width_ff = expand_mats.shape[2]
    shard = attention_mats.shape[1]
    bias_part = expand_bias.shape[0]
    n_query, n_vec = query_pos.shape[0], vectors.shape[0]
    vec_at = (n_query + 7) // 8 * 8
    head_at = (vec_at + n_vec + 7) // 8 * 8
    n_small = (head_at + joints + 127) // 128 * 128
    devices = width // shard
    dec_rows = (n_query + 127) // 128 * 128

    reduce_t = jnp.swapaxes(reduce_mats, 1, 2)
    half_mats = to_half(attention_mats)
    half_expand = to_half(expand_mats)
    half_reduce = to_half(reduce_t)
    small_local = to_half(
        jnp.concatenate(
            [
                pad_to(query_pos.T, shard, vec_at),
                pad_to(vectors.T, shard, head_at - vec_at),
                pad_to(action_head, shard, n_small - head_at),
            ],
            axis=1,
        )
    )
    bias_local = to_half(jnp.pad(expand_bias, (0, shard * 128 - bias_part)).reshape(shard, 128))
    ffn_all = Gather(jnp.concatenate([half_expand[0], half_reduce[0]], axis=1))
    ffn_all.start()
    enc_att = gather(jnp.concatenate([side_by_side(half_mats[0:4]), small_local, bias_local], axis=1))
    dec_all = gather(
        jnp.concatenate([side_by_side(half_mats[4:12]), half_expand[1], half_reduce[1]], axis=1)
    )

    assert items == ranks
    enc_x = swap(enc_input).reshape(ranks * enc_part, width)
    dec_x = pad_to(swap(dec_input).reshape(ranks * dec_part, width), dec_rows, width)
    target = pad_to(swap(targets).reshape(ranks * dec_part, joints), dec_rows, 128)
    turn, turn_back = turn_matrices(width)
    positions = jnp.asarray(sine_table(ranks * enc_part, width))
    ffn_all.up_to_last()
    enc_x = tie(enc_x, ffn_all)
    ffn_all.step()
    length = lengths[seq_index]
    valid = jnp.broadcast_to((jnp.arange(dec_rows) < length).astype(F32)[:, None], (dec_rows, 128))

    at = 4 * width
    small = enc_att[:, at : at + n_small].T
    bias_all = enc_att[:, at + n_small :].reshape(devices, shard * 128)
    bias_all = bias_all[:, :bias_part].reshape(1, 2 * width_ff).astype(F32)
    query_whole = pad_to(small[:n_query].astype(F32), dec_rows, width)
    vec = pad_to(small[vec_at : vec_at + n_vec].astype(F32), (n_vec + 7) // 8 * 8, width)
    head_t = pad_to(small[head_at : head_at + joints], 128, width)
    query, keys, values, mixed, log_total = attend(enc_x, positions, enc_att, vec)
    mixed = tie(mixed, ffn_all)
    sum_one, hidden, u, sum_two, memory, expand, reduce_t_all = feed_forward(
        mixed, enc_x, enc_att, vec, *ffn_all.finish(), turn_back, bias_all[:, :width_ff]
    )
    memory, in_t, x_t, mixed_t, hidden_t = lax.optimization_barrier(
        (memory, *lefts(enc_x, positions, mixed, hidden, turn))
    )
    (
        w_keep, w_send, f_keep, f_send,
        dec_in_grad, query_grad, memory_grad, dec_vec_grads, head_grad_t, dec_bias_grad,
    ) = decode(
        dec_x, query_whole, target, valid, dec_all, head_t, vec, bias_all[:, width_ff:], memory, positions, turn,
        n_query, joints,
    )
    dec_ffn, dec_att = Sum([f_keep, f_send], True), Sum([w_keep, w_send], True)
    dec_ffn.start()
    dec_att.start()
    two_grad, half_t, vec_grads_c = tie(last_norm_back(memory_grad, sum_two, vec, turn), dec_ffn, dec_att)
    dec_ffn.step()
    keep, send, one_grad, mixed_grad, vec_grads_b, enc_bias_grad, att_held = tie(
        [
            *feed_back(two_grad, half_t, sum_one, hidden_t, mixed_t, u, enc_att, expand, reduce_t_all, vec),
            (dec_att.blocks, dec_att.arrived),
        ],
        dec_ffn,
    )
    dec_att.blocks, dec_att.arrived = att_held
    enc_ffn_sum = Sum([keep, send], True)
    enc_ffn_sum.start()
    dec_ffn.step()
    dec_att.step()

    def back(so_far, first, count, grads):
        return attend_back(
            query, keys, values, mixed, mixed_grad, log_total, in_t, x_t, so_far, enc_att, first, count, grads
        )

    pairs = HEADS // 2
    keep, send, so_far, vec_grads_d = tie(back(one_grad, 0, 1, ()), dec_ffn, dec_att, enc_ffn_sum)
    dec_ffn.step()
    dec_att.step()
    enc_ffn_sum.step()
    keep, send, so_far, vec_grads_e = tie(back(so_far, 1, pairs - 2, (keep, send)), dec_ffn, dec_att)
    dec_ffn_total = dec_ffn.finish()
    dec_att.step()
    dec_grad = swap(dec_in_grad[:n_query].reshape(ranks, dec_part, width))
    vec_grads = jnp.concatenate([vec_grads_b[:3], vec_grads_c[:3], dec_vec_grads[: n_vec - 8]])
    small_rows = jnp.concatenate(
        [
            pad_to(query_grad[:n_query], vec_at + 2, width),
            pad_to(vec_grads, head_at - vec_at - 2, width),
            pad_to(head_grad_t[:joints], n_small - head_at, width),
        ]
    )
    bias_grad = jnp.concatenate([enc_bias_grad, dec_bias_grad], axis=1).reshape(devices, bias_part)
    bias_grad = pad_to(bias_grad, devices, shard * 128).reshape(width, 128)
    small_grad = to_half(
        jnp.concatenate([mm_t(turn, to_half(small_rows)), mm(turn, to_half(bias_grad))], axis=1)
    )
    keep, send, enc_grad, vec_grads_f, small_grad, dec_grad = tie(
        [*back(so_far, pairs - 1, 1, (keep, send)), small_grad, dec_grad], dec_att, enc_ffn_sum
    )
    dec_att_total = dec_att.finish()
    enc_grad = swap(enc_grad.reshape(ranks, enc_part, width))
    enc_ffn_sum.step()
    late_rows = jnp.concatenate([vec_grads_d[:2], vec_grads_e[:2], vec_grads_f[:2]], axis=1)
    late_grad = to_half(mm_t(turn, to_half(pad_to(late_rows, 128, width))))
    half = width // 2
    last = Sum(
        [
            jnp.concatenate([keep, small_grad[:half], late_grad[:half]], axis=1),
            jnp.concatenate([send, small_grad[half:], late_grad[half:]], axis=1),
        ]
    )
    last.start()
    dec_att_total = tie(dec_att_total, last, enc_ffn_sum)
    last.step()
    enc_ffn_sum.step()
    dec_ffn_total = tie(dec_ffn_total, last, enc_ffn_sum)
    enc_ffn_total, last_total = enc_ffn_sum.finish(), last.finish()
    outputs = [enc_grad, dec_grad]

    small_total = last_total[:, 3 * width :]
    gradients = (
        jnp.stack(
            [last_total[:, i * width : (i + 1) * width] for i in range(3)]
            + [enc_ffn_total[:, 2 * width_ff :]]
            + [dec_att_total[:, i * width : (i + 1) * width] for i in range(8)]
        ),
        jnp.stack([enc_ffn_total[:, :width_ff], dec_ffn_total[:, :width_ff]]),
        jnp.stack([enc_ffn_total[:, width_ff : 2 * width_ff], dec_ffn_total[:, width_ff:]]),
        small_total[:, head_at : head_at + joints],
        small_total[:, :n_query],
        jnp.concatenate(
            [small_total[:, n_small + 128 : n_small + 130], small_total[:, vec_at + 2 : vec_at + n_vec]], axis=1
        ),
        small_total[:, n_small : n_small + 128].reshape(1, -1)[:, :bias_part],
    )

    def views(mats, expand, reduce, head, query, vector, bias):
        return (mats, expand, jnp.swapaxes(reduce, 1, 2), head, query.T, vector.T, bias.reshape(1, -1))

    weights = views(attention_mats, expand_mats, reduce_mats, action_head, query_pos, vectors, expand_bias)
    firsts, seconds = views(*moments[:7]), views(*moments[7:])
    rates = (rate_matrix,) * 4 + (rate_vector,) * 3
    for i, results in enumerate(update(list(zip(weights, gradients, firsts, seconds)), rates)):
        if i == 2:
            results = [jnp.swapaxes(value, 1, 2) for value in results]
        if i in (4, 5):
            results = [value.T for value in results]
        if i == 6:
            results = [value.reshape(-1) for value in results]
        outputs.extend(results)
    return tuple(outputs)


def solution(mesh):
    rows = P("dp", "seq", None)
    weight_specs = (
        P(None, ALL, None),
        P(None, ALL, None),
        P(None, None, ALL),
        P(ALL, None),
        P(None, ALL),
        P(None, ALL),
        P(ALL),
    )
    in_specs = (rows, rows, rows, P("dp")) + weight_specs * 3
    out_specs = (rows, rows) + tuple(spec for spec in weight_specs for unused in range(4))
    return jax.shard_map(
        per_device, mesh=mesh, in_specs=in_specs, out_specs=out_specs, check_vma=False
    )
```

```python
import functools
import math

import jax
import jax.numpy as jnp
import numpy as np
from jax import lax
from jax.experimental import pallas as pl
from jax.experimental.pallas import tpu as pltpu
from jax.sharding import PartitionSpec as P

HEADS = 8
HDIM = 64
PAIR = 2 * HDIM
STEP = 10
ALL = ("dp", "seq")

beta_first = 0.9
beta_second = 0.999
epsilon = 1e-08
decay_rate = 0.1
rate_matrix = 0.08
rate_vector = 0.2

BF = jnp.bfloat16
F32 = jnp.float32
MB = 1 << 20
SCALE = HDIM ** (-0.5)


def to_half(values):
    return values.astype(BF)


def mm(a, b):
    return lax.dot_general(a, b, (((1,), (0,)), ((), ())), preferred_element_type=F32)


def mm_t(a, b):
    return lax.dot_general(a, b, (((1,), (1,)), ((), ())), preferred_element_type=F32)


def column_sum(values):
    return jnp.sum(values.astype(F32), axis=0, keepdims=True)


def norm_parts(values):
    center = values - jnp.mean(values, axis=-1, keepdims=True)
    scale = lax.rsqrt(jnp.mean(center * center, axis=-1, keepdims=True) + 1e-05)
    return center * scale, scale


def layer_norm(values, gain, shift):
    return norm_parts(values)[0] * gain + shift


def norm_back(values, gain, gradient):
    unit, scale = norm_parts(values)
    inner = gradient * gain
    mean_inner = jnp.mean(inner, axis=-1, keepdims=True)
    mean_cross = jnp.mean(inner * unit, axis=-1, keepdims=True)
    back = scale * (inner - mean_inner - unit * mean_cross)
    return back, column_sum(gradient * unit), column_sum(gradient)


GELU_A = math.sqrt(2.0 / math.pi)
GELU_B = 0.044715


def gelu_parts(u):
    square = u * u
    bend = jnp.tanh(u * (GELU_A + GELU_A * GELU_B * square))
    half = 0.5 + 0.5 * bend
    slope = half + (0.5 * u) * (1.0 - bend * bend) * (GELU_A + 3.0 * GELU_A * GELU_B * square)
    return u * half, slope


def gelu(u):
    return u * (0.5 + 0.5 * jnp.tanh(u * (GELU_A + GELU_A * GELU_B * (u * u))))


def sine_table(count, width):
    halves = np.arange(width // 2, dtype=np.float64)
    frequency = np.exp(halves * (-2.0 * math.log(10000.0) / width))
    angles = np.arange(count)[:, None] * frequency[None, :]
    table = np.stack([np.sin(angles), np.cos(angles)], axis=-1).reshape(count, width)
    return table.astype(np.float32)


def own_lanes(values, h):
    lane = lax.broadcasted_iota(jnp.int32, values.shape, 1)
    return jnp.where((lane < HDIM) == (h == 0), values, jnp.zeros_like(values))


def join_rows(first, second):
    row = lax.broadcasted_iota(jnp.int32, first.shape, 0)
    return jnp.where(row < HDIM, first, second)


def settle_kernel(top_ref, bottom_ref, turn_ref, out_ref):
    cut = top_ref.shape[0]
    out_ref[...] = to_half(mm(turn_ref[:, :cut], top_ref[...]) + mm(turn_ref[:, cut:], bottom_ref[...]))


def settle(top, bottom, turn, block):
    cut, columns = top.shape
    part = pl.BlockSpec((cut, block), lambda i: (0, i))
    return pl.pallas_call(
        settle_kernel,
        grid=(columns // block,),
        in_specs=[part, part, pl.BlockSpec(turn.shape, lambda i: (0, 0))],
        out_specs=pl.BlockSpec((2 * cut, block), lambda i: (0, i)),
        out_shape=jax.ShapeDtypeStruct((2 * cut, columns), BF),
        compiler_params=pltpu.CompilerParams(vmem_limit_bytes=40 * MB),
        cost_estimate=pl.CostEstimate(flops=8 * cut * cut * columns, bytes_accessed=8 * cut * columns, transcendentals=0),
        name="settle",
    )(top, bottom, turn)


def attend_kernel(
    x_ref, pos_ref, wq_ref, wk_ref, wv_ref, vec_ref, q_ref, k_ref, v_ref, o_ref, log_ref, in_ref, vt_ref, *, chunk
):
    @pl.when(pl.program_id(0) == 0)
    def _():
        in_ref[...] = to_half(x_ref[...].astype(F32) + pos_ref[...])

    q_ref[...] = to_half(mm(in_ref[...], wq_ref[...]) + vec_ref[0:1, :])
    k_ref[...] = to_half(mm(in_ref[...], wk_ref[...]))
    values = to_half(mm(x_ref[...], wv_ref[...]) + vec_ref[1:2, :])
    v_ref[...] = values
    vt_ref[...] = values.T

    def step(i, carry):
        at = pl.ds(i * chunk, chunk)
        query = q_ref[at, :] * BF(SCALE)
        mixed = []
        for h in range(2):
            scores = mm_t(k_ref[...], own_lanes(query, h))
            peak = jnp.max(scores, axis=0, keepdims=True)
            weights = jnp.exp(scores - peak)
            total = jnp.sum(weights, axis=0, keepdims=True)
            mixed.append(mm(vt_ref[...], to_half(weights)) / total)
            log_ref[0, pl.ds(h, 1), at] = peak + jnp.log(total)
        o_ref[at, :] = to_half(join_rows(*mixed).T)
        return carry

    lax.fori_loop(0, q_ref.shape[0] // chunk, step, 0)


def attend(x, positions, weights, vec):
    rows, width = x.shape
    pairs = width // PAIR
    whole = pl.BlockSpec((rows, width), lambda i: (0, 0))
    own = pl.BlockSpec((rows, PAIR), lambda i: (0, i))
    mats = [pl.BlockSpec((width, PAIR), lambda i, j=j: (0, i + j * pairs)) for j in range(3)]
    half = jax.ShapeDtypeStruct((rows, width), BF)
    return pl.pallas_call(
        functools.partial(attend_kernel, chunk=256),
        grid=(pairs,),
        in_specs=[whole, whole] + mats + [pl.BlockSpec((vec.shape[0], PAIR), lambda i: (0, i))],
        out_specs=[own] * 4 + [pl.BlockSpec((1, 2, rows), lambda i: (i, 0, 0))],
        out_shape=[half] * 4 + [jax.ShapeDtypeStruct((pairs, 2, rows), F32)],
        scratch_shapes=[pltpu.VMEM((rows, width), BF), pltpu.VMEM((PAIR, rows), BF)],
        compiler_params=pltpu.CompilerParams(vmem_limit_bytes=56 * MB),
        cost_estimate=pl.CostEstimate(
            flops=16 * rows * rows * width, bytes_accessed=12 * rows * width, transcendentals=8 * rows * rows
        ),
        name="attend",
    )(x, positions, weights, weights, weights, vec)


def forward_kernel(
    mixed_ref, x_ref, out_ref, vec_ref, e_ref, r_ref, bias_ref,
    sum_one_ref, hidden_ref, u_ref, sum_two_ref, memory_ref, *, tile
):
    step = pl.program_id(0)
    count = x_ref.shape[0] // tile

    def rows_of(i):
        return pl.ds(pl.multiple_of(i * tile, tile), tile)

    @pl.when(step == 0)
    def _():
        def body(i, carry):
            at = rows_of(i)
            total = x_ref[at, :].astype(F32) + mm(mixed_ref[at, :], out_ref[...]) + vec_ref[2:3, :]
            sum_one_ref[at, :] = total
            hidden = layer_norm(total, vec_ref[3:4, :], vec_ref[4:5, :])
            hidden_ref[at, :] = to_half(hidden)
            sum_two_ref[at, :] = hidden + vec_ref[5:6, :]
            return carry

        lax.fori_loop(0, count, body, 0)

    def body(i, carry):
        at = rows_of(i)
        u = mm(hidden_ref[at, :], e_ref[...]) + bias_ref[...]
        u_ref[at, :] = u
        sum_two_ref[at, :] += mm_t(to_half(gelu(u)), r_ref[...])
        return carry

    lax.fori_loop(0, count, body, 0)

    @pl.when(step == pl.num_programs(0) - 1)
    def _():
        def body(i, carry):
            at = rows_of(i)
            memory_ref[at, :] = layer_norm(sum_two_ref[at, :], vec_ref[6:7, :], vec_ref[7:8, :])
            return carry

        lax.fori_loop(0, count, body, 0)


def feed_forward(mixed, x, enc_mats, vec, enc_ffn, bias):
    rows, width = x.shape
    width_ff = bias.shape[1]
    block = 640 if width_ff % 640 == 0 else width_ff
    steps = width_ff // block
    whole = pl.BlockSpec((rows, width), lambda i: (0, 0))
    float_rows = jax.ShapeDtypeStruct((rows, width), F32)
    return pl.pallas_call(
        functools.partial(forward_kernel, tile=256),
        grid=(steps,),
        in_specs=[
            whole,
            whole,
            pl.BlockSpec((width, width), lambda i: (0, 3)),
            pl.BlockSpec(vec.shape, lambda i: (0, 0)),
            pl.BlockSpec((width, block), lambda i: (0, i)),
            pl.BlockSpec((width, block), lambda i: (0, i + steps)),
            pl.BlockSpec((1, block), lambda i: (0, i)),
        ],
        out_specs=[whole, whole, pl.BlockSpec((rows, block), lambda i: (0, i)), whole, whole],
        out_shape=[
            float_rows,
            jax.ShapeDtypeStruct((rows, width), BF),
            jax.ShapeDtypeStruct((rows, width_ff), F32),
            float_rows,
            float_rows,
        ],
        compiler_params=pltpu.CompilerParams(vmem_limit_bytes=56 * MB),
        cost_estimate=pl.CostEstimate(
            flops=4 * rows * width * width_ff, bytes_accessed=4 * rows * width_ff, transcendentals=rows * width_ff
        ),
        name="feed_forward",
    )(mixed, x, enc_mats, vec, enc_ffn, enc_ffn, bias)


def turned(turn, values):
    return to_half(mm_t(turn, values))


def lefts_kernel(x_ref, pos_ref, mixed_ref, hidden_ref, turn_ref, in_t_ref, x_t_ref, mixed_t_ref, hidden_t_ref):
    in_t_ref[...] = turned(turn_ref[...], to_half(x_ref[...].astype(F32) + pos_ref[...]))
    x_t_ref[...] = turned(turn_ref[...], x_ref[...])
    mixed_t_ref[...] = turned(turn_ref[...], mixed_ref[...])
    hidden_t_ref[...] = turned(turn_ref[...], hidden_ref[...])


def lefts(x, positions, mixed, hidden, turn):
    rows, width = x.shape
    return pl.pallas_call(
        lefts_kernel,
        out_shape=[jax.ShapeDtypeStruct((width, rows), BF)] * 4,
        compiler_params=pltpu.CompilerParams(vmem_limit_bytes=40 * MB),
        cost_estimate=pl.CostEstimate(flops=8 * rows * width * width, bytes_accessed=20 * rows * width, transcendentals=0),
        name="lefts",
    )(x, positions, mixed, hidden, turn)


def norm_kernel(grad_ref, sum_two_ref, vec_ref, turn_ref, two_ref, half_t_ref, vec_grad_ref, half_ref, *, tile):
    vec_grad_ref[...] = jnp.zeros_like(vec_grad_ref)

    def body(i, carry):
        at = pl.ds(pl.multiple_of(i * tile, tile), tile)
        back, gain, shift = norm_back(sum_two_ref[at, :], vec_ref[6:7, :], grad_ref[at, :])
        two_ref[at, :] = back
        half_ref[at, :] = to_half(back)
        vec_grad_ref[0:1, :] += column_sum(back)
        vec_grad_ref[1:2, :] += gain
        vec_grad_ref[2:3, :] += shift
        return carry

    lax.fori_loop(0, grad_ref.shape[0] // tile, body, 0)
    half_t_ref[...] = turned(turn_ref[...], half_ref[...])


def last_norm_back(grad, sum_two, vec, turn):
    rows, width = grad.shape
    return pl.pallas_call(
        functools.partial(norm_kernel, tile=256),
        out_shape=[
            jax.ShapeDtypeStruct((rows, width), F32),
            jax.ShapeDtypeStruct((width, rows), BF),
            jax.ShapeDtypeStruct((8, width), F32),
        ],
        scratch_shapes=[pltpu.VMEM((rows, width), BF)],
        compiler_params=pltpu.CompilerParams(vmem_limit_bytes=40 * MB),
        cost_estimate=pl.CostEstimate(flops=2 * rows * width * width, bytes_accessed=14 * rows * width, transcendentals=0),
        name="last_norm_back",
    )(grad, sum_two, vec, turn)


def backward_kernel(
    grad_ref, half_t_ref, sum_one_ref, hidden_t_ref, mixed_t_ref, u_ref, e_ref, r_ref, out_ref, vec_ref,
    keep_ref, send_ref, one_ref, mixed_grad_ref, vec_grad_ref, bias_ref,
    two_ref, half_ref, act_ref, inner_ref, *, tile
):
    step = pl.program_id(0)
    rows, width = sum_one_ref.shape
    count = rows // tile
    cut = width // 2

    def rows_of(i):
        return pl.ds(pl.multiple_of(i * tile, tile), tile)

    @pl.when(step == 0)
    def _():
        two_ref[...] = grad_ref[...]
        half_ref[...] = to_half(grad_ref[...])

    bias_ref[...] = jnp.zeros_like(bias_ref)

    def body(i, carry):
        at = rows_of(i)
        act, slope = gelu_parts(u_ref[at, :])
        act_ref[at, :] = to_half(act)
        inner = to_half(mm(half_ref[at, :], r_ref[...]) * slope)
        inner_ref[at, :] = inner
        bias_ref[...] += column_sum(inner)
        two_ref[at, :] += mm_t(inner, e_ref[...])
        return carry

    lax.fori_loop(0, count, body, 0)
    block = u_ref.shape[1]
    steps = pl.num_programs(0)

    def set_grad(at, grad):
        at = pl.ds(pl.multiple_of(at, 128), grad.shape[1])
        keep_ref[:, at] = to_half(grad[:cut])
        send_ref[:, at] = to_half(grad[cut:])

    set_grad(step * block, mm(hidden_t_ref[...], inner_ref[...]))
    set_grad((step + steps) * block, mm(half_t_ref[...], act_ref[...]))

    @pl.when(step == pl.num_programs(0) - 1)
    def _():
        vec_grad_ref[...] = jnp.zeros_like(vec_grad_ref)

        def body(i, carry):
            at = rows_of(i)
            back, gain, shift = norm_back(sum_one_ref[at, :], vec_ref[3:4, :], two_ref[at, :])
            one_ref[at, :] = back
            half = to_half(back)
            half_ref[at, :] = half
            mixed_grad_ref[at, :] = to_half(mm_t(half, out_ref[...]))
            vec_grad_ref[0:1, :] += column_sum(back)
            vec_grad_ref[1:2, :] += gain
            vec_grad_ref[2:3, :] += shift
            return carry

        lax.fori_loop(0, count, body, 0)
        set_grad(2 * steps * block, mm(mixed_t_ref[...], half_ref[...]))


def feed_back(grad, half_t, sum_one, hidden_t, mixed_t, u, enc_mats, enc_ffn, vec):
    rows, width = sum_one.shape
    width_ff = u.shape[1]
    block = 640 if width_ff % 640 == 0 else width_ff
    steps = width_ff // block
    cut = width // 2
    whole = pl.BlockSpec((rows, width), lambda i: (0, 0))
    whole_t = pl.BlockSpec((width, rows), lambda i: (0, 0))
    grads = (cut, 2 * width_ff + width)
    return pl.pallas_call(
        functools.partial(backward_kernel, tile=256),
        grid=(steps,),
        in_specs=[
            whole,
            whole_t,
            whole,
            whole_t,
            whole_t,
            pl.BlockSpec((rows, block), lambda i: (0, i)),
            pl.BlockSpec((width, block), lambda i: (0, i)),
            pl.BlockSpec((width, block), lambda i: (0, i + steps)),
            pl.BlockSpec((width, width), lambda i: (0, 3)),
            pl.BlockSpec(vec.shape, lambda i: (0, 0)),
        ],
        out_specs=[pl.BlockSpec(grads, lambda i: (0, 0))] * 2
        + [
            whole,
            whole,
            pl.BlockSpec((8, width), lambda i: (0, 0)),
            pl.BlockSpec((1, block), lambda i: (0, i)),
        ],
        out_shape=[jax.ShapeDtypeStruct(grads, BF)] * 2
        + [
            jax.ShapeDtypeStruct((rows, width), F32),
            jax.ShapeDtypeStruct((rows, width), BF),
            jax.ShapeDtypeStruct((8, width), F32),
            jax.ShapeDtypeStruct((1, width_ff), F32),
        ],
        scratch_shapes=[
            pltpu.VMEM((rows, width), F32),
            pltpu.VMEM((rows, width), BF),
            pltpu.VMEM((rows, block), BF),
            pltpu.VMEM((rows, block), BF),
        ],
        compiler_params=pltpu.CompilerParams(vmem_limit_bytes=60 * MB),
        cost_estimate=pl.CostEstimate(
            flops=8 * rows * width * width_ff, bytes_accessed=6 * rows * width_ff, transcendentals=rows * width_ff
        ),
        name="feed_back",
    )(grad, half_t, sum_one, hidden_t, mixed_t, u, enc_ffn, enc_ffn, enc_mats, vec)


def attend_back_kernel(
    q_ref, k_ref, v_ref, o_ref, g_ref, log_ref, in_t_ref, x_t_ref, one_ref, wq_ref, wk_ref, wv_ref, *refs, chunk, first
):
    keep_ref, send_ref, grad_ref, vec_ref, kt_ref, dx_ref, dq_ref, dk_ref, dv_ref = refs[-9:]
    step_at = pl.program_id(0)
    width = x_t_ref.shape[0]
    cut = width // 2

    @pl.when(step_at == 0)
    def _():
        dx_ref[...] = one_ref[...]
        if first:
            keep_ref[...] = refs[0][...]
            send_ref[...] = refs[1][...]

    kt_ref[...] = k_ref[...].T
    dk_ref[...] = jnp.zeros_like(dk_ref)
    dv_ref[...] = jnp.zeros_like(dv_ref)

    def step(i, carry):
        at = pl.ds(i * chunk, chunk)
        query = q_ref[at, :] * BF(SCALE)
        grad = g_ref[at, :]
        cross = (grad.astype(F32) * o_ref[at, :].astype(F32)).T
        back = []
        for h in range(2):
            own, own_grad = own_lanes(query, h), own_lanes(grad, h)
            weighted = jnp.sum(cross[h * HDIM : (h + 1) * HDIM], axis=0, keepdims=True)
            probs = jnp.exp(mm_t(k_ref[...], own) - log_ref[0, pl.ds(h, 1), at])
            score_grad = to_half(probs * (mm_t(v_ref[...], own_grad) - weighted))
            dv_ref[...] += mm(to_half(probs), own_grad)
            dk_ref[...] += mm(score_grad, own)
            back.append(mm(kt_ref[...], score_grad))
        dq_ref[at, :] = to_half((join_rows(*back) * SCALE).T)
        return carry

    lax.fori_loop(0, q_ref.shape[0] // chunk, step, 0)
    dq = dq_ref[...]
    dk = to_half(dk_ref[...])
    dv = to_half(dv_ref[...])
    dx_ref[...] += mm_t(dq, wq_ref[...]) + mm_t(dk, wk_ref[...]) + mm_t(dv, wv_ref[...])
    for j, (left_ref, right) in enumerate(((in_t_ref, dq), (in_t_ref, dk), (x_t_ref, dv))):
        wgrad = to_half(mm(left_ref[...], right))
        at = pl.ds(pl.multiple_of(j * width + (first + step_at) * PAIR, PAIR), PAIR)
        keep_ref[:, at] = wgrad[:cut]
        send_ref[:, at] = wgrad[cut:]
    vec_ref[...] = jnp.zeros_like(vec_ref)
    vec_ref[0:1, :] = column_sum(dq)
    vec_ref[1:2, :] = column_sum(dv)

    @pl.when(step_at == pl.num_programs(0) - 1)
    def _():
        grad_ref[...] = dx_ref[...].astype(grad_ref.dtype)


def attend_back(query, keys, values, mixed, grad, log_total, in_t, x_t, so_far, enc_mats, first, count, grads):
    rows, width = query.shape
    pairs = width // PAIR
    cut = width // 2
    own = pl.BlockSpec((rows, PAIR), lambda i: (0, i + first))
    whole = pl.BlockSpec((rows, width), lambda i: (0, 0))
    whole_t = pl.BlockSpec((width, rows), lambda i: (0, 0))
    mats = [pl.BlockSpec((width, PAIR), lambda i, j=j: (0, i + first + j * pairs)) for j in range(3)]
    three = pl.BlockSpec((cut, 3 * width), lambda i: (0, 0))
    return pl.pallas_call(
        functools.partial(attend_back_kernel, chunk=256, first=first),
        grid=(count,),
        in_specs=[own] * 5
        + [pl.BlockSpec((1, 2, rows), lambda i: (i + first, 0, 0)), whole_t, whole_t, whole]
        + mats
        + [three] * len(grads),
        out_specs=[three, three, whole, pl.BlockSpec((8, PAIR), lambda i: (0, i))],
        out_shape=[jax.ShapeDtypeStruct((cut, 3 * width), BF)] * 2
        + [
            jax.ShapeDtypeStruct((rows, width), BF if first + count == pairs else F32),
            jax.ShapeDtypeStruct((8, count * PAIR), F32),
        ],
        scratch_shapes=[
            pltpu.VMEM((PAIR, rows), BF),
            pltpu.VMEM((rows, width), F32),
            pltpu.VMEM((rows, PAIR), BF),
            pltpu.VMEM((rows, PAIR), F32),
            pltpu.VMEM((rows, PAIR), F32),
        ],
        compiler_params=pltpu.CompilerParams(vmem_limit_bytes=60 * MB),
        cost_estimate=pl.CostEstimate(
            flops=10 * rows * rows * width * count, bytes_accessed=16 * rows * width, transcendentals=4 * rows * rows
        ),
        name="attend_back",
    )(query, keys, values, mixed, grad, log_total, in_t, x_t, so_far, enc_mats, enc_mats, enc_mats, *grads)


def heads_forward(query, key_ref, value_ref, prob_ref, spacing=None):
    outs = []
    for pair in range(HEADS // 2):
        lanes = slice(pair * PAIR, (pair + 1) * PAIR)
        keys = key_ref[:, lanes]
        values_t = value_ref[:, lanes].T
        scaled = query[:, lanes] * BF(SCALE)
        mixed = []
        for h in range(2):
            scores = mm_t(keys, own_lanes(scaled, h))
            if spacing is not None:
                row = lax.broadcasted_iota(jnp.int32, scores.shape, 0)
                scores = jnp.where(row % spacing[1] < spacing[0], scores, -jnp.inf)
            weights = jnp.exp(scores - jnp.max(scores, axis=0, keepdims=True))
            probs = weights * (1.0 / jnp.sum(weights, axis=0, keepdims=True))
            prob_ref[2 * pair + h] = probs
            mixed.append(mm(values_t, to_half(probs)))
        outs.append(to_half(join_rows(*mixed).T))
    return jnp.concatenate(outs, axis=1)


def heads_back(query, key_ref, value_ref, prob_ref, grad, dk_ref, dv_ref):
    outs = []
    for pair in range(HEADS // 2):
        lanes = slice(pair * PAIR, (pair + 1) * PAIR)
        keys_t = key_ref[:, lanes].T
        values = value_ref[:, lanes]
        scaled = query[:, lanes] * BF(SCALE)
        dk = dv = None
        back = []
        for h in range(2):
            own, own_grad = own_lanes(scaled, h), own_lanes(grad[:, lanes], h)
            probs = prob_ref[2 * pair + h]
            prob_grad = mm_t(values, own_grad)
            weighted = jnp.sum(probs * prob_grad, axis=0, keepdims=True)
            score_grad = to_half(probs * (prob_grad - weighted))
            back.append(mm(keys_t, score_grad))
            k_part, v_part = mm(score_grad, own), mm(to_half(probs), own_grad)
            dk = k_part if h == 0 else dk + k_part
            dv = v_part if h == 0 else dv + v_part
        dk_ref[:, lanes] = to_half(dk)
        dv_ref[:, lanes] = to_half(dv)
        outs.append(to_half((join_rows(*back) * SCALE).T))
    return jnp.concatenate(outs, axis=1)


def decode_kernel(
    x_ref, query_ref, target_ref, valid_ref, w_ref, f_ref, head_ref, vec_ref, bias_ref, mem_ref, pos_ref, turn_ref,
    w_keep_ref, w_send_ref, f_keep_ref, f_send_ref, in_grad_ref, query_grad_ref, mem_grad_ref, vec_grad_ref, head_grad_ref, bias_grad_ref,
    mem_in, mem_half, cross_k, cross_v, cross_dk, cross_dv, cross_p,
    self_k, self_v, self_dk, self_dv, self_p, u_ref, act_ref, acc_ref, left_ref, *, spacing, joints, block
):
    width = x_ref.shape[1]
    width_ff = u_ref.shape[1]
    blocks = width_ff // block

    def mat(i):
        return w_ref[:, i * width : (i + 1) * width]

    cut = width // 2

    def left_of(values):
        return turned(turn_ref[...], values)

    def set_mat(i, left_t, right):
        grad = to_half(mm(left_t, right))
        w_keep_ref[:, i * width : (i + 1) * width] = grad[:cut]
        w_send_ref[:, i * width : (i + 1) * width] = grad[cut:]

    def set_ffn(at, left_t, right):
        grad = to_half(mm(left_t, right))
        f_keep_ref[:, at] = grad[:cut]
        f_send_ref[:, at] = grad[cut:]

    def vec(i):
        return vec_ref[i : i + 1, :]

    def set_vec(i, value):
        vec_grad_ref[i - 8 : i - 7, :] = value

    def lanes(i, start=0):
        return pl.ds(pl.multiple_of(start + i * block, 128), block)

    vec_grad_ref[...] = jnp.zeros_like(vec_grad_ref)
    x = x_ref[...]
    x_float = x.astype(F32)
    places = query_ref[...]
    self_in = to_half(x_float + places)
    self_q = to_half(mm(self_in, mat(0)) + vec(8))
    self_k[...] = to_half(mm(self_in, mat(1)))
    self_v[...] = to_half(mm(x, mat(2)) + vec(9))
    self_mixed = heads_forward(self_q, self_k, self_v, self_p, spacing)
    sum_one = x_float + mm(self_mixed, mat(3)) + vec(10)
    one = layer_norm(sum_one, vec(11), vec(12))
    cross_in = to_half(one + places)
    cross_q = to_half(mm(cross_in, mat(4)) + vec(13))
    mem_in[...] = to_half(mem_ref[...] + pos_ref[...])
    mem_half[...] = to_half(mem_ref[...])
    cross_k[...] = to_half(mm(mem_in[...], mat(5)))
    cross_v[...] = to_half(mm(mem_half[...], mat(6)) + vec(14))
    cross_mixed = heads_forward(cross_q, cross_k, cross_v, cross_p)
    sum_two = one + mm(cross_mixed, mat(7)) + vec(15)
    two = layer_norm(sum_two, vec(16), vec(17))
    two_half = to_half(two)
    acc_ref[...] = two + vec(18)

    def forward(i, carry):
        u = mm(two_half, f_ref[:, lanes(i)]) + bias_ref[:, lanes(i)]
        u_ref[:, lanes(i)] = u
        acc_ref[...] += mm_t(to_half(gelu(u)), f_ref[:, lanes(i, width_ff)])
        return carry

    lax.fori_loop(0, blocks, forward, 0)
    sum_three = acc_ref[...]
    three_half = to_half(layer_norm(sum_three, vec(19), vec(20)))
    error = mm_t(three_half, head_ref[...]) - target_ref[...]
    pred_grad = to_half(error * lax.rsqrt(error * error + 1.0) * valid_ref[...] / joints)
    head_grad_ref[...] = mm(pred_grad.T, three_half)
    sum_three_grad, gain, shift = norm_back(sum_three, vec(19), mm(pred_grad, head_ref[...]))
    set_vec(18, column_sum(sum_three_grad))
    set_vec(19, gain)
    set_vec(20, shift)
    out_grad = to_half(sum_three_grad)
    left_ref[0] = left_of(out_grad)
    left_ref[1] = left_of(two_half)
    acc_ref[...] = sum_three_grad

    def backward(i, carry):
        act, slope = gelu_parts(u_ref[:, lanes(i)])
        inner = to_half(mm(out_grad, f_ref[:, lanes(i, width_ff)]) * slope)
        bias_grad_ref[:, lanes(i)] = column_sum(inner)
        acc_ref[...] += mm_t(inner, f_ref[:, lanes(i)])
        set_ffn(lanes(i), left_ref[1], inner)
        set_ffn(lanes(i, width_ff), left_ref[0], to_half(act))
        return carry

    lax.fori_loop(0, blocks, backward, 0)
    sum_two_grad, gain, shift = norm_back(sum_two, vec(16), acc_ref[...])
    set_vec(15, column_sum(sum_two_grad))
    set_vec(16, gain)
    set_vec(17, shift)
    out_grad = to_half(sum_two_grad)
    set_mat(7, left_of(cross_mixed), out_grad)
    mixed_grad = to_half(mm_t(out_grad, mat(7)))
    cross_dq = heads_back(cross_q, cross_k, cross_v, cross_p, mixed_grad, cross_dk, cross_dv)
    set_vec(13, column_sum(cross_dq))
    set_vec(14, column_sum(cross_dv[...]))
    mem_grad_ref[...] = mm_t(cross_dk[...], mat(5)) + mm_t(cross_dv[...], mat(6))
    set_mat(4, left_of(cross_in), cross_dq)
    set_mat(5, left_of(mem_in[...]), cross_dk[...])
    set_mat(6, left_of(mem_half[...]), cross_dv[...])
    cross_in_grad = mm_t(cross_dq, mat(4))
    sum_one_grad, gain, shift = norm_back(sum_one, vec(11), sum_two_grad + cross_in_grad)
    set_vec(10, column_sum(sum_one_grad))
    set_vec(11, gain)
    set_vec(12, shift)
    out_grad = to_half(sum_one_grad)
    set_mat(3, left_of(self_mixed), out_grad)
    mixed_grad = to_half(mm_t(out_grad, mat(3)))
    self_dq = heads_back(self_q, self_k, self_v, self_p, mixed_grad, self_dk, self_dv)
    set_vec(8, column_sum(self_dq))
    set_vec(9, column_sum(self_dv[...]))
    in_t = left_of(self_in)
    set_mat(0, in_t, self_dq)
    set_mat(1, in_t, self_dk[...])
    set_mat(2, left_of(x), self_dv[...])
    self_in_grad = mm_t(self_dq, mat(0)) + mm_t(self_dk[...], mat(1))
    in_grad_ref[...] = to_half(sum_one_grad + self_in_grad + mm_t(self_dv[...], mat(2)))
    query_grad_ref[...] = self_in_grad + cross_in_grad


def decode(x, places, target, valid, weights, ffn, head_t, vec, bias, memory, positions, turn, spacing, joints):
    rows, width = x.shape
    mem_rows = memory.shape[0]
    width_ff = bias.shape[1]
    half = lambda n: pltpu.VMEM((n, width), BF)
    return pl.pallas_call(
        functools.partial(
            decode_kernel, spacing=spacing, joints=joints, block=640 if width_ff % 640 == 0 else width_ff
        ),
        out_shape=[
            jax.ShapeDtypeStruct((width // 2, 8 * width), BF),
            jax.ShapeDtypeStruct((width // 2, 8 * width), BF),
            jax.ShapeDtypeStruct((width // 2, 2 * width_ff), BF),
            jax.ShapeDtypeStruct((width // 2, 2 * width_ff), BF),
            jax.ShapeDtypeStruct((rows, width), BF),
            jax.ShapeDtypeStruct((rows, width), F32),
            jax.ShapeDtypeStruct((mem_rows, width), F32),
            jax.ShapeDtypeStruct((16, width), F32),
            jax.ShapeDtypeStruct(head_t.shape, F32),
            jax.ShapeDtypeStruct((1, width_ff), F32),
        ],
        scratch_shapes=[half(mem_rows)] * 6
        + [pltpu.VMEM((HEADS, mem_rows, rows), F32)]
        + [half(rows)] * 4
        + [
            pltpu.VMEM((HEADS, rows, rows), F32),
            pltpu.VMEM((rows, width_ff), F32),
            pltpu.VMEM((rows, width_ff), BF),
            pltpu.VMEM((rows, width), F32),
            pltpu.VMEM((2, width, rows), BF),
        ],
        compiler_params=pltpu.CompilerParams(vmem_limit_bytes=60 * MB),
        cost_estimate=pl.CostEstimate(
            flops=12 * mem_rows * width * width, bytes_accessed=4 * weights.size, transcendentals=rows * width_ff
        ),
        name="decode",
    )(x, places, target, valid, weights, ffn, head_t, vec, bias, memory, positions, turn)


def adamw(weight, gradient, moment_one, moment_two, step_rate):
    moment_one = beta_first * moment_one + (1.0 - beta_first) * gradient
    moment_two = beta_second * moment_two + (1.0 - beta_second) * gradient * gradient
    mean_hat = moment_one / (1.0 - beta_first**STEP)
    square_hat = moment_two / (1.0 - beta_second**STEP)
    updated = weight - step_rate * (
        mean_hat / (jnp.sqrt(square_hat) + epsilon) + decay_rate * weight
    )
    return (moment_one, moment_two, updated, updated.astype(BF))


def update_kernel(*refs, rates):
    count = len(rates)
    ins, outs = refs[: 4 * count], refs[4 * count :]
    for i, rate in enumerate(rates):
        values = adamw(*(ref[...] for ref in ins[4 * i : 4 * i + 4]), rate)
        for ref, value in zip(outs[4 * i : 4 * i + 4], values):
            ref[...] = value


def update(groups, rates):
    shapes = []
    for group in groups:
        shapes += [jax.ShapeDtypeStruct(group[0].shape, F32)] * 3
        shapes.append(jax.ShapeDtypeStruct(group[0].shape, BF))
    outs = pl.pallas_call(
        functools.partial(update_kernel, rates=rates),
        out_shape=shapes,
        compiler_params=pltpu.CompilerParams(vmem_limit_bytes=56 * MB),
        name="update",
    )(*(array for group in groups for array in group))
    return [outs[4 * i : 4 * i + 4] for i in range(len(groups))]


def pad_to(values, rows, columns):
    return jnp.pad(values, ((0, rows - values.shape[0]), (0, columns - values.shape[1])))


def side_by_side(mats):
    return jnp.concatenate([mats[i] for i in range(mats.shape[0])], axis=1)


def gather(columns):
    return lax.all_gather(columns, ALL, axis=0, tiled=True)


def width_bits(axis):
    return (lax.axis_size(axis) - 1).bit_length()


def bit_groups(one_by_one=False):
    low = width_bits("seq")
    others = list(range(low + width_bits("dp") - 1, low, -1))
    groups = [[low]]
    for bits, most in ((others, 2), (list(range(low)), 1 if one_by_one else 2)):
        groups += [bits[i : i + most] for i in range(0, len(bits), most)]
    return groups


def spread(bits, place):
    return sum(((place >> k) & 1) << bit for k, bit in enumerate(reversed(bits)))


def turn_matrices(width):
    order = [bit for bits in bit_groups() for bit in bits]
    devices = 1 << len(order)
    relative = np.array([spread(order, j) for j in range(devices)], np.int32)
    shard = width // devices
    source = jnp.bitwise_xor(jnp.asarray(relative), lax.axis_index(ALL).astype(jnp.int32))
    source = (source[:, None] * shard + jnp.arange(shard, dtype=jnp.int32)[None, :]).reshape(width)
    places = jnp.arange(width, dtype=jnp.int32)
    return (source[:, None] == places[None, :]).astype(BF), (source[None, :] == places[:, None]).astype(BF)


def exchange(values, distance):
    low = width_bits("seq")
    axis, distance = ("dp", distance >> low) if distance >> low else ("seq", distance)
    pairs = [(i, i ^ distance) for i in range(lax.axis_size(axis))]
    return lax.ppermute(values, axis, pairs)


class Sum:
    def __init__(self, blocks, one_by_one=False):
        self.blocks = list(blocks)
        self.groups = bit_groups(one_by_one)
        self.arrived = None

    def start(self):
        bits = self.groups.pop(0)
        self.arrived = [exchange(block, spread(bits, j)) for j, block in enumerate(self.blocks) if j]

    def add(self):
        arrays = [self.blocks[0]] + self.arrived
        count = 1 << len(self.groups[0]) if self.groups else 1
        rows = arrays[0].shape[-2] // count
        totals = []
        for j in range(count):
            parts = [array[..., j * rows : (j + 1) * rows, :].astype(F32) for array in arrays]
            total = functools.reduce(jnp.add, parts)
            totals.append(to_half(total) if self.groups else total)
        self.blocks = totals
        self.arrived = None

    def step(self):
        self.add()
        if self.groups:
            self.start()

    def finish(self):
        while self.groups or self.arrived is not None:
            if self.arrived is None:
                self.start()
            self.step()
        return self.blocks[0]


class Gather:
    def __init__(self, value):
        self.value = value
        self.groups = bit_groups()
        self.arrived = None

    def start(self):
        bits = self.groups.pop()
        self.arrived = [exchange(self.value, spread(bits, j)) for j in range(1, 1 << len(bits))]

    def step(self):
        if not self.groups:
            return self.value, self.arrived[0]
        self.value = jnp.concatenate([self.value] + self.arrived)
        self.start()

    def up_to_last(self):
        while len(self.groups) > 1:
            self.step()

    def finish(self):
        halves = self.step()
        while halves is None:
            halves = self.step()
        return halves


def swap(pieces):
    return lax.all_to_all(pieces, "seq", 0, 0, tiled=True)


def tie(values, *sums):
    values, arrived = lax.optimization_barrier((values, [s.arrived for s in sums]))
    for s, a in zip(sums, arrived):
        s.arrived = a
    return values


def per_device(
    enc_input,
    dec_input,
    targets,
    lengths,
    attention_mats,
    expand_mats,
    reduce_mats,
    action_head,
    query_pos,
    vectors,
    expand_bias,
    *moments,
):
    ranks = lax.axis_size("seq")
    seq_index = lax.axis_index("seq")
    items, enc_part, width = enc_input.shape
    dec_part = dec_input.shape[1]
    joints = targets.shape[2]
    width_ff = expand_mats.shape[2]
    shard = attention_mats.shape[1]
    bias_part = expand_bias.shape[0]
    n_query, n_vec = query_pos.shape[0], vectors.shape[0]
    vec_at = (n_query + 7) // 8 * 8
    head_at = (vec_at + n_vec + 7) // 8 * 8
    n_small = (head_at + joints + 127) // 128 * 128
    devices = width // shard
    dec_block = (dec_part + 15) // 16 * 16
    dec_rows = ranks * dec_block

    reduce_t = jnp.swapaxes(reduce_mats, 1, 2)
    half_mats = to_half(attention_mats)
    half_expand = to_half(expand_mats)
    half_reduce = to_half(reduce_t)
    small_local = to_half(
        jnp.concatenate(
            [
                pad_to(query_pos.T, shard, vec_at),
                pad_to(vectors.T, shard, head_at - vec_at),
                pad_to(action_head, shard, n_small - head_at),
            ],
            axis=1,
        )
    )
    bias_local = to_half(jnp.pad(expand_bias, (0, shard * 128 - bias_part)).reshape(shard, 128))
    att_all = Gather(jnp.concatenate([side_by_side(half_mats[0:4]), small_local, bias_local], axis=1))
    ffn_all = Gather(jnp.concatenate([half_expand[1], half_reduce[1]], axis=1))
    att_all.start()
    enc_ffn = gather(jnp.concatenate([half_expand[0], half_reduce[0]], axis=1))
    dec_mats = gather(side_by_side(half_mats[4:12]))

    assert items == ranks
    def spaced(values):
        parts = values.reshape(ranks, dec_part, values.shape[-1])
        return jnp.pad(parts, ((0, 0), (0, dec_block - dec_part), (0, 0)))

    rows_in = swap(jnp.concatenate([enc_input, spaced(dec_input)], axis=1))
    enc_x = rows_in[:, :enc_part].reshape(ranks * enc_part, width)
    dec_x = rows_in[:, enc_part:].reshape(dec_rows, width)
    target = swap(jnp.pad(spaced(targets), ((0, 0), (0, 0), (0, 128 - joints)))).reshape(dec_rows, 128)
    turn, turn_back = turn_matrices(width)
    positions = jnp.asarray(sine_table(ranks * enc_part, width))
    att_all.up_to_last()
    ffn_all.value = tie(ffn_all.value, att_all)
    enc_att = settle(*att_all.finish(), turn_back, 4 * width + n_small + 128)
    ffn_all.start()
    length = lengths[seq_index]
    row = jnp.arange(dec_rows)
    place = row % dec_block
    valid = (place < dec_part) & (row // dec_block * dec_part + place < length)
    valid = jnp.broadcast_to(valid.astype(F32)[:, None], (dec_rows, 128))

    at = 4 * width
    small = enc_att[:, at : at + n_small].T
    bias_all = enc_att[:, at + n_small :].reshape(devices, shard * 128)
    bias_all = bias_all[:, :bias_part].reshape(1, 2 * width_ff).astype(F32)
    query_whole = spaced(small[:n_query].astype(F32)).reshape(dec_rows, width)
    vec = pad_to(small[vec_at : vec_at + n_vec].astype(F32), (n_vec + 7) // 8 * 8, width)
    head_t = pad_to(small[head_at : head_at + joints], 128, width)
    query, keys, values, mixed, log_total = attend(enc_x, positions, enc_att, vec)
    block = 640 if width_ff % 640 == 0 else width_ff
    query, keys, values, mixed, log_total, target, valid, query_whole, head_t, dec_x = tie(
        (query, keys, values, mixed, log_total, target, valid, query_whole, head_t, dec_x), ffn_all
    )
    ffn_all.step()
    sum_one, hidden, u, sum_two, memory = tie(
        feed_forward(mixed, enc_x, enc_att, vec, enc_ffn, bias_all[:, :width_ff]), ffn_all
    )
    ffn_all.up_to_last()
    memory, in_t, x_t, mixed_t, hidden_t = tie((memory, *lefts(enc_x, positions, mixed, hidden, turn)), ffn_all)
    dec_ffn = settle(*ffn_all.finish(), turn_back, block)
    (
        w_keep, w_send, f_keep, f_send,
        dec_in_grad, query_grad, memory_grad, dec_vec_grads, head_grad_t, dec_bias_grad,
    ) = decode(
        dec_x, query_whole, target, valid, dec_mats, dec_ffn, head_t, vec, bias_all[:, width_ff:], memory, positions, turn,
        (dec_part, dec_block), joints,
    )
    dec_f, dec_att = Sum([f_keep, f_send], True), Sum([w_keep, w_send], True)
    dec_f.start()
    dec_att.start()
    two_grad, half_t, vec_grads_c = tie(last_norm_back(memory_grad, sum_two, vec, turn), dec_f, dec_att)
    dec_f.step()
    keep, send, one_grad, mixed_grad, vec_grads_b, enc_bias_grad, att_held = tie(
        [
            *feed_back(two_grad, half_t, sum_one, hidden_t, mixed_t, u, enc_att, enc_ffn, vec),
            (dec_att.blocks, dec_att.arrived),
        ],
        dec_f,
    )
    dec_att.blocks, dec_att.arrived = att_held
    enc_ffn_sum = Sum([keep, send], True)
    enc_ffn_sum.start()
    dec_f.step()
    dec_att.step()

    def back(so_far, first, count, grads):
        return attend_back(
            query, keys, values, mixed, mixed_grad, log_total, in_t, x_t, so_far, enc_att, first, count, grads
        )

    pairs = HEADS // 2
    keep, send, so_far, vec_grads_d = tie(back(one_grad, 0, 1, ()), enc_ffn_sum)
    enc_ffn_sum.add()
    so_far, enc_ffn_sum.blocks = tie((so_far, enc_ffn_sum.blocks), dec_f, dec_att)
    enc_ffn_sum.start()
    dec_f.step()
    dec_att.step()
    keep, send, so_far, vec_grads_e = tie(back(so_far, 1, pairs - 2, (keep, send)), dec_f, dec_att)
    dec_ffn_total = dec_f.finish()
    dec_att.step()
    dec_grad = swap(dec_in_grad.reshape(ranks, dec_block, width))[:, :dec_part]
    vec_grads = jnp.concatenate([vec_grads_b[:3], vec_grads_c[:3], dec_vec_grads[: n_vec - 8]])
    small_rows = jnp.concatenate(
        [
            pad_to(query_grad.reshape(ranks, dec_block, width)[:, :dec_part].reshape(n_query, width), vec_at + 2, width),
            pad_to(vec_grads, head_at - vec_at - 2, width),
            pad_to(head_grad_t[:joints], n_small - head_at, width),
        ]
    )
    bias_grad = jnp.concatenate([enc_bias_grad, dec_bias_grad], axis=1).reshape(devices, bias_part)
    bias_grad = pad_to(bias_grad, devices, shard * 128).reshape(width, 128)
    small_grad = to_half(
        jnp.concatenate([mm_t(turn, to_half(small_rows)), mm(turn, to_half(bias_grad))], axis=1)
    )
    keep, send, enc_grad, vec_grads_f, small_grad, dec_grad = tie(
        [*back(so_far, pairs - 1, 1, (keep, send)), small_grad, dec_grad], dec_att, enc_ffn_sum
    )
    dec_att_total = dec_att.finish()
    enc_grad = swap(enc_grad.reshape(ranks, enc_part, width))
    enc_ffn_sum.step()
    late_rows = jnp.concatenate([vec_grads_d[:2], vec_grads_e[:2], vec_grads_f[:2]], axis=1)
    late_grad = to_half(mm_t(turn, to_half(pad_to(late_rows, 128, width))))
    half = width // 2
    last = Sum(
        [
            jnp.concatenate([keep, small_grad[:half], late_grad[:half]], axis=1),
            jnp.concatenate([send, small_grad[half:], late_grad[half:]], axis=1),
        ]
    )
    last.start()
    dec_att_total = tie(dec_att_total, last)
    last.step()
    dec_ffn_total = tie(dec_ffn_total, enc_ffn_sum)
    enc_ffn_sum.step()
    dec_ffn_total, enc_grad = tie((dec_ffn_total, enc_grad), last, enc_ffn_sum)
    enc_ffn_total, last_total = enc_ffn_sum.finish(), last.finish()
    outputs = [enc_grad, dec_grad]

    small_total = last_total[:, 3 * width :]
    gradients = (
        jnp.stack(
            [last_total[:, i * width : (i + 1) * width] for i in range(3)]
            + [enc_ffn_total[:, 2 * width_ff :]]
            + [dec_att_total[:, i * width : (i + 1) * width] for i in range(8)]
        ),
        jnp.stack([enc_ffn_total[:, :width_ff], dec_ffn_total[:, :width_ff]]),
        jnp.stack([enc_ffn_total[:, width_ff : 2 * width_ff], dec_ffn_total[:, width_ff:]]),
        small_total[:, head_at : head_at + joints],
        small_total[:, :n_query],
        jnp.concatenate(
            [small_total[:, n_small + 128 : n_small + 130], small_total[:, vec_at + 2 : vec_at + n_vec]], axis=1
        ),
        small_total[:, n_small : n_small + 128].reshape(1, -1)[:, :bias_part],
    )

    def views(mats, expand, reduce, head, query, vector, bias):
        return (mats, expand, jnp.swapaxes(reduce, 1, 2), head, query.T, vector.T, bias.reshape(1, -1))

    weights = views(attention_mats, expand_mats, reduce_mats, action_head, query_pos, vectors, expand_bias)
    firsts, seconds = views(*moments[:7]), views(*moments[7:])
    rates = (rate_matrix,) * 4 + (rate_vector,) * 3
    for i, results in enumerate(update(list(zip(weights, gradients, firsts, seconds)), rates)):
        if i == 2:
            results = [jnp.swapaxes(value, 1, 2) for value in results]
        if i in (4, 5):
            results = [value.T for value in results]
        if i == 6:
            results = [value.reshape(-1) for value in results]
        outputs.extend(results)
    return tuple(outputs)


def solution(mesh):
    rows = P("dp", "seq", None)
    weight_specs = (
        P(None, ALL, None),
        P(None, ALL, None),
        P(None, None, ALL),
        P(ALL, None),
        P(None, ALL),
        P(None, ALL),
        P(ALL),
    )
    in_specs = (rows, rows, rows, P("dp")) + weight_specs * 3
    out_specs = (rows, rows) + tuple(spec for spec in weight_specs for unused in range(4))
    return jax.shard_map(
        per_device, mesh=mesh, in_specs=in_specs, out_specs=out_specs, check_vma=False
    )
```

```python
import functools
import math

import jax
import jax.numpy as jnp
import numpy as np
from jax import lax
from jax.experimental import pallas as pl
from jax.experimental.pallas import tpu as pltpu
from jax.sharding import PartitionSpec as P

HEADS = 8
HDIM = 64
PAIR = 2 * HDIM
STEP = 10
ALL = ("dp", "seq")

beta_first = 0.9
beta_second = 0.999
epsilon = 1e-08
decay_rate = 0.1
rate_matrix = 0.08
rate_vector = 0.2

BF = jnp.bfloat16
F32 = jnp.float32
MB = 1 << 20
SCALE = HDIM ** (-0.5)


def to_half(values):
    return values.astype(BF)


def mm(a, b):
    return lax.dot_general(a, b, (((1,), (0,)), ((), ())), preferred_element_type=F32)


def mm_t(a, b):
    return lax.dot_general(a, b, (((1,), (1,)), ((), ())), preferred_element_type=F32)


def column_sum(values):
    return jnp.sum(values.astype(F32), axis=0, keepdims=True)


def norm_parts(values):
    center = values - jnp.mean(values, axis=-1, keepdims=True)
    scale = lax.rsqrt(jnp.mean(center * center, axis=-1, keepdims=True) + 1e-05)
    return center * scale, scale


def layer_norm(values, gain, shift):
    return norm_parts(values)[0] * gain + shift


def norm_back(values, gain, gradient):
    unit, scale = norm_parts(values)
    inner = gradient * gain
    mean_inner = jnp.mean(inner, axis=-1, keepdims=True)
    mean_cross = jnp.mean(inner * unit, axis=-1, keepdims=True)
    back = scale * (inner - mean_inner - unit * mean_cross)
    return back, column_sum(gradient * unit), column_sum(gradient)


GELU_A = math.sqrt(2.0 / math.pi)
GELU_B = 0.044715


def gelu_parts(u):
    square = u * u
    bend = jnp.tanh(u * (GELU_A + GELU_A * GELU_B * square))
    half = 0.5 + 0.5 * bend
    slope = half + (0.5 * u) * (1.0 - bend * bend) * (GELU_A + 3.0 * GELU_A * GELU_B * square)
    return u * half, slope


def gelu(u):
    return u * (0.5 + 0.5 * jnp.tanh(u * (GELU_A + GELU_A * GELU_B * (u * u))))


def sine_table(count, width):
    halves = np.arange(width // 2, dtype=np.float64)
    frequency = np.exp(halves * (-2.0 * math.log(10000.0) / width))
    angles = np.arange(count)[:, None] * frequency[None, :]
    table = np.stack([np.sin(angles), np.cos(angles)], axis=-1).reshape(count, width)
    return table.astype(np.float32)


def own_lanes(values, h):
    lane = lax.broadcasted_iota(jnp.int32, values.shape, 1)
    return jnp.where((lane < HDIM) == (h == 0), values, jnp.zeros_like(values))


def join_rows(first, second):
    row = lax.broadcasted_iota(jnp.int32, first.shape, 0)
    return jnp.where(row < HDIM, first, second)


def settle_kernel(top_ref, bottom_ref, turn_ref, out_ref):
    cut = top_ref.shape[0]
    out_ref[...] = to_half(mm(turn_ref[:, :cut], top_ref[...]) + mm(turn_ref[:, cut:], bottom_ref[...]))


def settle(top, bottom, turn, block):
    cut, columns = top.shape
    part = pl.BlockSpec((cut, block), lambda i: (0, i))
    return pl.pallas_call(
        settle_kernel,
        grid=(columns // block,),
        in_specs=[part, part, pl.BlockSpec(turn.shape, lambda i: (0, 0))],
        out_specs=pl.BlockSpec((2 * cut, block), lambda i: (0, i)),
        out_shape=jax.ShapeDtypeStruct((2 * cut, columns), BF),
        compiler_params=pltpu.CompilerParams(vmem_limit_bytes=40 * MB),
        cost_estimate=pl.CostEstimate(flops=8 * cut * cut * columns, bytes_accessed=8 * cut * columns, transcendentals=0),
        name="settle",
    )(top, bottom, turn)


def attend_kernel(
    x_ref, pos_ref, wq_ref, wk_ref, wv_ref, vec_ref, q_ref, k_ref, v_ref, o_ref, log_ref, in_ref, vt_ref, *, chunk
):
    @pl.when(pl.program_id(0) == 0)
    def _():
        in_ref[...] = to_half(x_ref[...].astype(F32) + pos_ref[...])

    q_ref[...] = to_half(mm(in_ref[...], wq_ref[...]) + vec_ref[0:1, :])
    k_ref[...] = to_half(mm(in_ref[...], wk_ref[...]))
    values = to_half(mm(x_ref[...], wv_ref[...]) + vec_ref[1:2, :])
    v_ref[...] = values
    vt_ref[...] = values.T

    def step(i, carry):
        at = pl.ds(i * chunk, chunk)
        query = q_ref[at, :] * BF(SCALE)
        mixed = []
        for h in range(2):
            scores = mm_t(k_ref[...], own_lanes(query, h))
            peak = jnp.max(scores, axis=0, keepdims=True)
            weights = jnp.exp(scores - peak)
            total = jnp.sum(weights, axis=0, keepdims=True)
            mixed.append(mm(vt_ref[...], to_half(weights)) / total)
            log_ref[0, pl.ds(h, 1), at] = peak + jnp.log(total)
        o_ref[at, :] = to_half(join_rows(*mixed).T)
        return carry

    lax.fori_loop(0, q_ref.shape[0] // chunk, step, 0)


def attend(x, positions, weights, vec):
    rows, width = x.shape
    pairs = width // PAIR
    whole = pl.BlockSpec((rows, width), lambda i: (0, 0))
    own = pl.BlockSpec((rows, PAIR), lambda i: (0, i))
    mats = [pl.BlockSpec((width, PAIR), lambda i, j=j: (0, i + j * pairs)) for j in range(3)]
    half = jax.ShapeDtypeStruct((rows, width), BF)
    return pl.pallas_call(
        functools.partial(attend_kernel, chunk=512),
        grid=(pairs,),
        in_specs=[whole, whole] + mats + [pl.BlockSpec((vec.shape[0], PAIR), lambda i: (0, i))],
        out_specs=[own] * 4 + [pl.BlockSpec((1, 2, rows), lambda i: (i, 0, 0))],
        out_shape=[half] * 4 + [jax.ShapeDtypeStruct((pairs, 2, rows), F32)],
        scratch_shapes=[pltpu.VMEM((rows, width), BF), pltpu.VMEM((PAIR, rows), BF)],
        compiler_params=pltpu.CompilerParams(vmem_limit_bytes=56 * MB),
        cost_estimate=pl.CostEstimate(
            flops=16 * rows * rows * width, bytes_accessed=12 * rows * width, transcendentals=8 * rows * rows
        ),
        name="attend",
    )(x, positions, weights, weights, weights, vec)


def forward_kernel(
    mixed_ref, x_ref, out_ref, vec_ref, e_ref, r_ref, bias_ref,
    sum_one_ref, hidden_ref, u_ref, sum_two_ref, memory_ref, *, tile
):
    step = pl.program_id(0)
    count = x_ref.shape[0] // tile

    def rows_of(i):
        return pl.ds(pl.multiple_of(i * tile, tile), tile)

    @pl.when(step == 0)
    def _():
        def body(i, carry):
            at = rows_of(i)
            total = x_ref[at, :].astype(F32) + mm(mixed_ref[at, :], out_ref[...]) + vec_ref[2:3, :]
            sum_one_ref[at, :] = total
            hidden = layer_norm(total, vec_ref[3:4, :], vec_ref[4:5, :])
            hidden_ref[at, :] = to_half(hidden)
            sum_two_ref[at, :] = hidden + vec_ref[5:6, :]
            return carry

        lax.fori_loop(0, count, body, 0)

    def body(i, carry):
        at = rows_of(i)
        u = mm(hidden_ref[at, :], e_ref[...]) + bias_ref[...]
        u_ref[at, :] = u
        sum_two_ref[at, :] += mm_t(to_half(gelu(u)), r_ref[...])
        return carry

    lax.fori_loop(0, count, body, 0)

    @pl.when(step == pl.num_programs(0) - 1)
    def _():
        def body(i, carry):
            at = rows_of(i)
            memory_ref[at, :] = layer_norm(sum_two_ref[at, :], vec_ref[6:7, :], vec_ref[7:8, :])
            return carry

        lax.fori_loop(0, count, body, 0)


def feed_forward(mixed, x, enc_mats, vec, enc_ffn, bias):
    rows, width = x.shape
    width_ff = bias.shape[1]
    block = 640 if width_ff % 640 == 0 else width_ff
    steps = width_ff // block
    whole = pl.BlockSpec((rows, width), lambda i: (0, 0))
    float_rows = jax.ShapeDtypeStruct((rows, width), F32)
    return pl.pallas_call(
        functools.partial(forward_kernel, tile=256),
        grid=(steps,),
        in_specs=[
            whole,
            whole,
            pl.BlockSpec((width, width), lambda i: (0, 3)),
            pl.BlockSpec(vec.shape, lambda i: (0, 0)),
            pl.BlockSpec((width, block), lambda i: (0, i)),
            pl.BlockSpec((width, block), lambda i: (0, i + steps)),
            pl.BlockSpec((1, block), lambda i: (0, i)),
        ],
        out_specs=[whole, whole, pl.BlockSpec((rows, block), lambda i: (0, i)), whole, whole],
        out_shape=[
            float_rows,
            jax.ShapeDtypeStruct((rows, width), BF),
            jax.ShapeDtypeStruct((rows, width_ff), F32),
            float_rows,
            float_rows,
        ],
        compiler_params=pltpu.CompilerParams(vmem_limit_bytes=56 * MB),
        cost_estimate=pl.CostEstimate(
            flops=4 * rows * width * width_ff, bytes_accessed=4 * rows * width_ff, transcendentals=rows * width_ff
        ),
        name="feed_forward",
    )(mixed, x, enc_mats, vec, enc_ffn, enc_ffn, bias)


def turned(turn, values):
    return to_half(mm_t(turn, values))


def lefts_kernel(x_ref, pos_ref, mixed_ref, hidden_ref, turn_ref, in_t_ref, x_t_ref, mixed_t_ref, hidden_t_ref):
    in_t_ref[...] = turned(turn_ref[...], to_half(x_ref[...].astype(F32) + pos_ref[...]))
    x_t_ref[...] = turned(turn_ref[...], x_ref[...])
    mixed_t_ref[...] = turned(turn_ref[...], mixed_ref[...])
    hidden_t_ref[...] = turned(turn_ref[...], hidden_ref[...])


def lefts(x, positions, mixed, hidden, turn):
    rows, width = x.shape
    return pl.pallas_call(
        lefts_kernel,
        out_shape=[jax.ShapeDtypeStruct((width, rows), BF)] * 4,
        compiler_params=pltpu.CompilerParams(vmem_limit_bytes=40 * MB),
        cost_estimate=pl.CostEstimate(flops=8 * rows * width * width, bytes_accessed=20 * rows * width, transcendentals=0),
        name="lefts",
    )(x, positions, mixed, hidden, turn)


def norm_kernel(grad_ref, sum_two_ref, vec_ref, turn_ref, two_ref, half_t_ref, vec_grad_ref, half_ref, *, tile):
    vec_grad_ref[...] = jnp.zeros_like(vec_grad_ref)

    def body(i, carry):
        at = pl.ds(pl.multiple_of(i * tile, tile), tile)
        back, gain, shift = norm_back(sum_two_ref[at, :], vec_ref[6:7, :], grad_ref[at, :])
        two_ref[at, :] = back
        half_ref[at, :] = to_half(back)
        vec_grad_ref[0:1, :] += column_sum(back)
        vec_grad_ref[1:2, :] += gain
        vec_grad_ref[2:3, :] += shift
        return carry

    lax.fori_loop(0, grad_ref.shape[0] // tile, body, 0)
    half_t_ref[...] = turned(turn_ref[...], half_ref[...])


def last_norm_back(grad, sum_two, vec, turn):
    rows, width = grad.shape
    return pl.pallas_call(
        functools.partial(norm_kernel, tile=256),
        out_shape=[
            jax.ShapeDtypeStruct((rows, width), F32),
            jax.ShapeDtypeStruct((width, rows), BF),
            jax.ShapeDtypeStruct((8, width), F32),
        ],
        scratch_shapes=[pltpu.VMEM((rows, width), BF)],
        compiler_params=pltpu.CompilerParams(vmem_limit_bytes=40 * MB),
        cost_estimate=pl.CostEstimate(flops=2 * rows * width * width, bytes_accessed=14 * rows * width, transcendentals=0),
        name="last_norm_back",
    )(grad, sum_two, vec, turn)


def backward_kernel(
    grad_ref, half_t_ref, sum_one_ref, hidden_t_ref, mixed_t_ref, u_ref, e_ref, r_ref, out_ref, vec_ref,
    keep_ref, send_ref, one_ref, mixed_grad_ref, vec_grad_ref, bias_ref,
    two_ref, half_ref, act_ref, inner_ref, *, tile
):
    step = pl.program_id(0)
    rows, width = sum_one_ref.shape
    count = rows // tile
    cut = width // 2

    def rows_of(i):
        return pl.ds(pl.multiple_of(i * tile, tile), tile)

    @pl.when(step == 0)
    def _():
        two_ref[...] = grad_ref[...]
        half_ref[...] = to_half(grad_ref[...])

    bias_ref[...] = jnp.zeros_like(bias_ref)

    def body(i, carry):
        at = rows_of(i)
        act, slope = gelu_parts(u_ref[at, :])
        act_ref[at, :] = to_half(act)
        inner = to_half(mm(half_ref[at, :], r_ref[...]) * slope)
        inner_ref[at, :] = inner
        bias_ref[...] += column_sum(inner)
        two_ref[at, :] += mm_t(inner, e_ref[...])
        return carry

    lax.fori_loop(0, count, body, 0)
    block = u_ref.shape[1]
    steps = pl.num_programs(0)

    def set_grad(at, grad):
        at = pl.ds(pl.multiple_of(at, 128), grad.shape[1])
        keep_ref[:, at] = to_half(grad[:cut])
        send_ref[:, at] = to_half(grad[cut:])

    set_grad(step * block, mm(hidden_t_ref[...], inner_ref[...]))
    set_grad((step + steps) * block, mm(half_t_ref[...], act_ref[...]))

    @pl.when(step == pl.num_programs(0) - 1)
    def _():
        vec_grad_ref[...] = jnp.zeros_like(vec_grad_ref)

        def body(i, carry):
            at = rows_of(i)
            back, gain, shift = norm_back(sum_one_ref[at, :], vec_ref[3:4, :], two_ref[at, :])
            one_ref[at, :] = back
            half = to_half(back)
            half_ref[at, :] = half
            mixed_grad_ref[at, :] = to_half(mm_t(half, out_ref[...]))
            vec_grad_ref[0:1, :] += column_sum(back)
            vec_grad_ref[1:2, :] += gain
            vec_grad_ref[2:3, :] += shift
            return carry

        lax.fori_loop(0, count, body, 0)
        set_grad(2 * steps * block, mm(mixed_t_ref[...], half_ref[...]))


def feed_back(grad, half_t, sum_one, hidden_t, mixed_t, u, enc_mats, enc_ffn, vec):
    rows, width = sum_one.shape
    width_ff = u.shape[1]
    block = 640 if width_ff % 640 == 0 else width_ff
    steps = width_ff // block
    cut = width // 2
    whole = pl.BlockSpec((rows, width), lambda i: (0, 0))
    whole_t = pl.BlockSpec((width, rows), lambda i: (0, 0))
    grads = (cut, 2 * width_ff + width)
    return pl.pallas_call(
        functools.partial(backward_kernel, tile=256),
        grid=(steps,),
        in_specs=[
            whole,
            whole_t,
            whole,
            whole_t,
            whole_t,
            pl.BlockSpec((rows, block), lambda i: (0, i)),
            pl.BlockSpec((width, block), lambda i: (0, i)),
            pl.BlockSpec((width, block), lambda i: (0, i + steps)),
            pl.BlockSpec((width, width), lambda i: (0, 3)),
            pl.BlockSpec(vec.shape, lambda i: (0, 0)),
        ],
        out_specs=[pl.BlockSpec(grads, lambda i: (0, 0))] * 2
        + [
            whole,
            whole,
            pl.BlockSpec((8, width), lambda i: (0, 0)),
            pl.BlockSpec((1, block), lambda i: (0, i)),
        ],
        out_shape=[jax.ShapeDtypeStruct(grads, BF)] * 2
        + [
            jax.ShapeDtypeStruct((rows, width), F32),
            jax.ShapeDtypeStruct((rows, width), BF),
            jax.ShapeDtypeStruct((8, width), F32),
            jax.ShapeDtypeStruct((1, width_ff), F32),
        ],
        scratch_shapes=[
            pltpu.VMEM((rows, width), F32),
            pltpu.VMEM((rows, width), BF),
            pltpu.VMEM((rows, block), BF),
            pltpu.VMEM((rows, block), BF),
        ],
        compiler_params=pltpu.CompilerParams(vmem_limit_bytes=60 * MB),
        cost_estimate=pl.CostEstimate(
            flops=8 * rows * width * width_ff, bytes_accessed=6 * rows * width_ff, transcendentals=rows * width_ff
        ),
        name="feed_back",
    )(grad, half_t, sum_one, hidden_t, mixed_t, u, enc_ffn, enc_ffn, enc_mats, vec)


def attend_back_kernel(
    q_ref, k_ref, v_ref, o_ref, g_ref, log_ref, in_t_ref, x_t_ref, one_ref, wq_ref, wk_ref, wv_ref, *refs, chunk, first
):
    keep_ref, send_ref, grad_ref, vec_ref, kt_ref, dx_ref, dq_ref, dk_ref, dv_ref = refs[-9:]
    step_at = pl.program_id(0)
    width = x_t_ref.shape[0]
    cut = width // 2

    @pl.when(step_at == 0)
    def _():
        dx_ref[...] = one_ref[...]
        if first:
            keep_ref[...] = refs[0][...]
            send_ref[...] = refs[1][...]

    kt_ref[...] = k_ref[...].T
    dk_ref[...] = jnp.zeros_like(dk_ref)
    dv_ref[...] = jnp.zeros_like(dv_ref)

    def step(i, carry):
        at = pl.ds(i * chunk, chunk)
        query = q_ref[at, :] * BF(SCALE)
        grad = g_ref[at, :]
        cross = (grad.astype(F32) * o_ref[at, :].astype(F32)).T
        back = []
        for h in range(2):
            own, own_grad = own_lanes(query, h), own_lanes(grad, h)
            weighted = jnp.sum(cross[h * HDIM : (h + 1) * HDIM], axis=0, keepdims=True)
            probs = jnp.exp(mm_t(k_ref[...], own) - log_ref[0, pl.ds(h, 1), at])
            score_grad = to_half(probs * (mm_t(v_ref[...], own_grad) - weighted))
            dv_ref[...] += mm(to_half(probs), own_grad)
            dk_ref[...] += mm(score_grad, own)
            back.append(mm(kt_ref[...], score_grad))
        dq_ref[at, :] = to_half((join_rows(*back) * SCALE).T)
        return carry

    lax.fori_loop(0, q_ref.shape[0] // chunk, step, 0)
    dq = dq_ref[...]
    dk = to_half(dk_ref[...])
    dv = to_half(dv_ref[...])
    dx_ref[...] += mm_t(dq, wq_ref[...]) + mm_t(dk, wk_ref[...]) + mm_t(dv, wv_ref[...])
    for j, (left_ref, right) in enumerate(((in_t_ref, dq), (in_t_ref, dk), (x_t_ref, dv))):
        wgrad = to_half(mm(left_ref[...], right))
        at = pl.ds(pl.multiple_of(j * width + (first + step_at) * PAIR, PAIR), PAIR)
        keep_ref[:, at] = wgrad[:cut]
        send_ref[:, at] = wgrad[cut:]
    vec_ref[...] = jnp.zeros_like(vec_ref)
    vec_ref[0:1, :] = column_sum(dq)
    vec_ref[1:2, :] = column_sum(dv)

    @pl.when(step_at == pl.num_programs(0) - 1)
    def _():
        grad_ref[...] = dx_ref[...].astype(grad_ref.dtype)


def attend_back(query, keys, values, mixed, grad, log_total, in_t, x_t, so_far, enc_mats, first, count, grads):
    rows, width = query.shape
    pairs = width // PAIR
    cut = width // 2
    own = pl.BlockSpec((rows, PAIR), lambda i: (0, i + first))
    whole = pl.BlockSpec((rows, width), lambda i: (0, 0))
    whole_t = pl.BlockSpec((width, rows), lambda i: (0, 0))
    mats = [pl.BlockSpec((width, PAIR), lambda i, j=j: (0, i + first + j * pairs)) for j in range(3)]
    three = pl.BlockSpec((cut, 3 * width), lambda i: (0, 0))
    return pl.pallas_call(
        functools.partial(attend_back_kernel, chunk=256, first=first),
        grid=(count,),
        in_specs=[own] * 5
        + [pl.BlockSpec((1, 2, rows), lambda i: (i + first, 0, 0)), whole_t, whole_t, whole]
        + mats
        + [three] * len(grads),
        out_specs=[three, three, whole, pl.BlockSpec((8, PAIR), lambda i: (0, i))],
        out_shape=[jax.ShapeDtypeStruct((cut, 3 * width), BF)] * 2
        + [
            jax.ShapeDtypeStruct((rows, width), BF if first + count == pairs else F32),
            jax.ShapeDtypeStruct((8, count * PAIR), F32),
        ],
        scratch_shapes=[
            pltpu.VMEM((PAIR, rows), BF),
            pltpu.VMEM((rows, width), F32),
            pltpu.VMEM((rows, PAIR), BF),
            pltpu.VMEM((rows, PAIR), F32),
            pltpu.VMEM((rows, PAIR), F32),
        ],
        compiler_params=pltpu.CompilerParams(vmem_limit_bytes=60 * MB),
        cost_estimate=pl.CostEstimate(
            flops=10 * rows * rows * width * count, bytes_accessed=16 * rows * width, transcendentals=4 * rows * rows
        ),
        name="attend_back",
    )(query, keys, values, mixed, grad, log_total, in_t, x_t, so_far, enc_mats, enc_mats, enc_mats, *grads)


def heads_forward(query, key_ref, value_ref, prob_ref, spacing=None):
    outs = []
    for pair in range(HEADS // 2):
        lanes = slice(pair * PAIR, (pair + 1) * PAIR)
        keys = key_ref[:, lanes]
        values_t = value_ref[:, lanes].T
        scaled = query[:, lanes] * BF(SCALE)
        mixed = []
        for h in range(2):
            scores = mm_t(keys, own_lanes(scaled, h))
            if spacing is not None:
                row = lax.broadcasted_iota(jnp.int32, scores.shape, 0)
                scores = jnp.where(row % spacing[1] < spacing[0], scores, -jnp.inf)
            weights = jnp.exp(scores - jnp.max(scores, axis=0, keepdims=True))
            probs = weights * (1.0 / jnp.sum(weights, axis=0, keepdims=True))
            prob_ref[2 * pair + h] = probs
            mixed.append(mm(values_t, to_half(probs)))
        outs.append(to_half(join_rows(*mixed).T))
    return jnp.concatenate(outs, axis=1)


def heads_back(query, key_ref, value_ref, prob_ref, grad, dk_ref, dv_ref):
    outs = []
    for pair in range(HEADS // 2):
        lanes = slice(pair * PAIR, (pair + 1) * PAIR)
        keys_t = key_ref[:, lanes].T
        values = value_ref[:, lanes]
        scaled = query[:, lanes] * BF(SCALE)
        dk = dv = None
        back = []
        for h in range(2):
            own, own_grad = own_lanes(scaled, h), own_lanes(grad[:, lanes], h)
            probs = prob_ref[2 * pair + h]
            prob_grad = mm_t(values, own_grad)
            weighted = jnp.sum(probs * prob_grad, axis=0, keepdims=True)
            score_grad = to_half(probs * (prob_grad - weighted))
            back.append(mm(keys_t, score_grad))
            k_part, v_part = mm(score_grad, own), mm(to_half(probs), own_grad)
            dk = k_part if h == 0 else dk + k_part
            dv = v_part if h == 0 else dv + v_part
        dk_ref[:, lanes] = to_half(dk)
        dv_ref[:, lanes] = to_half(dv)
        outs.append(to_half((join_rows(*back) * SCALE).T))
    return jnp.concatenate(outs, axis=1)


def decode_kernel(
    x_ref, query_ref, target_ref, valid_ref, w_ref, f_ref, head_ref, vec_ref, bias_ref, mem_ref, pos_ref, turn_ref,
    w_keep_ref, w_send_ref, f_keep_ref, f_send_ref, in_grad_ref, query_grad_ref, mem_grad_ref, vec_grad_ref, head_grad_ref, bias_grad_ref,
    mem_in, mem_half, cross_k, cross_v, cross_dk, cross_dv, cross_p,
    self_k, self_v, self_dk, self_dv, self_p, u_ref, act_ref, acc_ref, left_ref, *, spacing, joints, block
):
    width = x_ref.shape[1]
    width_ff = u_ref.shape[1]
    blocks = width_ff // block

    def mat(i):
        return w_ref[:, i * width : (i + 1) * width]

    cut = width // 2

    def left_of(values):
        return turned(turn_ref[...], values)

    def set_mat(i, left_t, right):
        grad = to_half(mm(left_t, right))
        w_keep_ref[:, i * width : (i + 1) * width] = grad[:cut]
        w_send_ref[:, i * width : (i + 1) * width] = grad[cut:]

    def set_ffn(at, left_t, right):
        grad = to_half(mm(left_t, right))
        f_keep_ref[:, at] = grad[:cut]
        f_send_ref[:, at] = grad[cut:]

    def vec(i):
        return vec_ref[i : i + 1, :]

    def set_vec(i, value):
        vec_grad_ref[i - 8 : i - 7, :] = value

    def lanes(i, start=0):
        return pl.ds(pl.multiple_of(start + i * block, 128), block)

    vec_grad_ref[...] = jnp.zeros_like(vec_grad_ref)
    x = x_ref[...]
    x_float = x.astype(F32)
    places = query_ref[...]
    self_in = to_half(x_float + places)
    self_q = to_half(mm(self_in, mat(0)) + vec(8))
    self_k[...] = to_half(mm(self_in, mat(1)))
    self_v[...] = to_half(mm(x, mat(2)) + vec(9))
    self_mixed = heads_forward(self_q, self_k, self_v, self_p, spacing)
    sum_one = x_float + mm(self_mixed, mat(3)) + vec(10)
    one = layer_norm(sum_one, vec(11), vec(12))
    cross_in = to_half(one + places)
    cross_q = to_half(mm(cross_in, mat(4)) + vec(13))
    mem_in[...] = to_half(mem_ref[...] + pos_ref[...])
    mem_half[...] = to_half(mem_ref[...])
    cross_k[...] = to_half(mm(mem_in[...], mat(5)))
    cross_v[...] = to_half(mm(mem_half[...], mat(6)) + vec(14))
    cross_mixed = heads_forward(cross_q, cross_k, cross_v, cross_p)
    sum_two = one + mm(cross_mixed, mat(7)) + vec(15)
    two = layer_norm(sum_two, vec(16), vec(17))
    two_half = to_half(two)
    acc_ref[...] = two + vec(18)

    def forward(i, carry):
        u = mm(two_half, f_ref[:, lanes(i)]) + bias_ref[:, lanes(i)]
        u_ref[:, lanes(i)] = u
        acc_ref[...] += mm_t(to_half(gelu(u)), f_ref[:, lanes(i, width_ff)])
        return carry

    lax.fori_loop(0, blocks, forward, 0)
    sum_three = acc_ref[...]
    three_half = to_half(layer_norm(sum_three, vec(19), vec(20)))
    error = mm_t(three_half, head_ref[...]) - target_ref[...]
    pred_grad = to_half(error * lax.rsqrt(error * error + 1.0) * valid_ref[...] / joints)
    head_grad_ref[...] = mm(pred_grad.T, three_half)
    sum_three_grad, gain, shift = norm_back(sum_three, vec(19), mm(pred_grad, head_ref[...]))
    set_vec(18, column_sum(sum_three_grad))
    set_vec(19, gain)
    set_vec(20, shift)
    out_grad = to_half(sum_three_grad)
    left_ref[0] = left_of(out_grad)
    left_ref[1] = left_of(two_half)
    acc_ref[...] = sum_three_grad

    def backward(i, carry):
        act, slope = gelu_parts(u_ref[:, lanes(i)])
        inner = to_half(mm(out_grad, f_ref[:, lanes(i, width_ff)]) * slope)
        bias_grad_ref[:, lanes(i)] = column_sum(inner)
        acc_ref[...] += mm_t(inner, f_ref[:, lanes(i)])
        set_ffn(lanes(i), left_ref[1], inner)
        set_ffn(lanes(i, width_ff), left_ref[0], to_half(act))
        return carry

    lax.fori_loop(0, blocks, backward, 0)
    sum_two_grad, gain, shift = norm_back(sum_two, vec(16), acc_ref[...])
    set_vec(15, column_sum(sum_two_grad))
    set_vec(16, gain)
    set_vec(17, shift)
    out_grad = to_half(sum_two_grad)
    set_mat(7, left_of(cross_mixed), out_grad)
    mixed_grad = to_half(mm_t(out_grad, mat(7)))
    cross_dq = heads_back(cross_q, cross_k, cross_v, cross_p, mixed_grad, cross_dk, cross_dv)
    set_vec(13, column_sum(cross_dq))
    set_vec(14, column_sum(cross_dv[...]))
    mem_grad_ref[...] = mm_t(cross_dk[...], mat(5)) + mm_t(cross_dv[...], mat(6))
    set_mat(4, left_of(cross_in), cross_dq)
    set_mat(5, left_of(mem_in[...]), cross_dk[...])
    set_mat(6, left_of(mem_half[...]), cross_dv[...])
    cross_in_grad = mm_t(cross_dq, mat(4))
    sum_one_grad, gain, shift = norm_back(sum_one, vec(11), sum_two_grad + cross_in_grad)
    set_vec(10, column_sum(sum_one_grad))
    set_vec(11, gain)
    set_vec(12, shift)
    out_grad = to_half(sum_one_grad)
    set_mat(3, left_of(self_mixed), out_grad)
    mixed_grad = to_half(mm_t(out_grad, mat(3)))
    self_dq = heads_back(self_q, self_k, self_v, self_p, mixed_grad, self_dk, self_dv)
    set_vec(8, column_sum(self_dq))
    set_vec(9, column_sum(self_dv[...]))
    in_t = left_of(self_in)
    set_mat(0, in_t, self_dq)
    set_mat(1, in_t, self_dk[...])
    set_mat(2, left_of(x), self_dv[...])
    self_in_grad = mm_t(self_dq, mat(0)) + mm_t(self_dk[...], mat(1))
    in_grad_ref[...] = to_half(sum_one_grad + self_in_grad + mm_t(self_dv[...], mat(2)))
    query_grad_ref[...] = self_in_grad + cross_in_grad


def decode(x, places, target, valid, weights, ffn, head_t, vec, bias, memory, positions, turn, spacing, joints):
    rows, width = x.shape
    mem_rows = memory.shape[0]
    width_ff = bias.shape[1]
    half = lambda n: pltpu.VMEM((n, width), BF)
    return pl.pallas_call(
        functools.partial(
            decode_kernel, spacing=spacing, joints=joints, block=640 if width_ff % 640 == 0 else width_ff
        ),
        out_shape=[
            jax.ShapeDtypeStruct((width // 2, 8 * width), BF),
            jax.ShapeDtypeStruct((width // 2, 8 * width), BF),
            jax.ShapeDtypeStruct((width // 2, 2 * width_ff), BF),
            jax.ShapeDtypeStruct((width // 2, 2 * width_ff), BF),
            jax.ShapeDtypeStruct((rows, width), BF),
            jax.ShapeDtypeStruct((rows, width), F32),
            jax.ShapeDtypeStruct((mem_rows, width), F32),
            jax.ShapeDtypeStruct((16, width), F32),
            jax.ShapeDtypeStruct(head_t.shape, F32),
            jax.ShapeDtypeStruct((1, width_ff), F32),
        ],
        scratch_shapes=[half(mem_rows)] * 6
        + [pltpu.VMEM((HEADS, mem_rows, rows), F32)]
        + [half(rows)] * 4
        + [
            pltpu.VMEM((HEADS, rows, rows), F32),
            pltpu.VMEM((rows, width_ff), F32),
            pltpu.VMEM((rows, width_ff), BF),
            pltpu.VMEM((rows, width), F32),
            pltpu.VMEM((2, width, rows), BF),
        ],
        compiler_params=pltpu.CompilerParams(vmem_limit_bytes=60 * MB),
        cost_estimate=pl.CostEstimate(
            flops=12 * mem_rows * width * width, bytes_accessed=4 * weights.size, transcendentals=rows * width_ff
        ),
        name="decode",
    )(x, places, target, valid, weights, ffn, head_t, vec, bias, memory, positions, turn)


def adamw(weight, gradient, moment_one, moment_two, step_rate):
    moment_one = beta_first * moment_one + (1.0 - beta_first) * gradient
    moment_two = beta_second * moment_two + (1.0 - beta_second) * gradient * gradient
    mean_hat = moment_one / (1.0 - beta_first**STEP)
    square_hat = moment_two / (1.0 - beta_second**STEP)
    updated = weight - step_rate * (
        mean_hat / (jnp.sqrt(square_hat) + epsilon) + decay_rate * weight
    )
    return (moment_one, moment_two, updated, updated.astype(BF))


def update_kernel(*refs, rates):
    count = len(rates)
    ins, outs = refs[: 4 * count], refs[4 * count :]
    for i, rate in enumerate(rates):
        values = adamw(*(ref[...] for ref in ins[4 * i : 4 * i + 4]), rate)
        for ref, value in zip(outs[4 * i : 4 * i + 4], values):
            ref[...] = value


def update(groups, rates):
    shapes = []
    for group in groups:
        shapes += [jax.ShapeDtypeStruct(group[0].shape, F32)] * 3
        shapes.append(jax.ShapeDtypeStruct(group[0].shape, BF))
    outs = pl.pallas_call(
        functools.partial(update_kernel, rates=rates),
        out_shape=shapes,
        compiler_params=pltpu.CompilerParams(vmem_limit_bytes=56 * MB),
        name="update",
    )(*(array for group in groups for array in group))
    return [outs[4 * i : 4 * i + 4] for i in range(len(groups))]


def pad_to(values, rows, columns):
    return jnp.pad(values, ((0, rows - values.shape[0]), (0, columns - values.shape[1])))


def side_by_side(mats):
    return jnp.concatenate([mats[i] for i in range(mats.shape[0])], axis=1)


def gather(columns):
    return lax.all_gather(columns, ALL, axis=0, tiled=True)


def width_bits(axis):
    return (lax.axis_size(axis) - 1).bit_length()


def bit_groups(one_by_one=False):
    low = width_bits("seq")
    others = list(range(low + width_bits("dp") - 1, low, -1))
    groups = [[low]]
    for bits, most in ((others, 2), (list(range(low)), 1 if one_by_one else 2)):
        groups += [bits[i : i + most] for i in range(0, len(bits), most)]
    return groups


def spread(bits, place):
    return sum(((place >> k) & 1) << bit for k, bit in enumerate(reversed(bits)))


def turn_matrices(width):
    order = [bit for bits in bit_groups() for bit in bits]
    devices = 1 << len(order)
    relative = np.array([spread(order, j) for j in range(devices)], np.int32)
    shard = width // devices
    source = jnp.bitwise_xor(jnp.asarray(relative), lax.axis_index(ALL).astype(jnp.int32))
    source = (source[:, None] * shard + jnp.arange(shard, dtype=jnp.int32)[None, :]).reshape(width)
    places = jnp.arange(width, dtype=jnp.int32)
    return (source[:, None] == places[None, :]).astype(BF), (source[None, :] == places[:, None]).astype(BF)


def exchange(values, distance):
    low = width_bits("seq")
    axis, distance = ("dp", distance >> low) if distance >> low else ("seq", distance)
    pairs = [(i, i ^ distance) for i in range(lax.axis_size(axis))]
    return lax.ppermute(values, axis, pairs)


class Sum:
    def __init__(self, blocks, one_by_one=False):
        self.blocks = list(blocks)
        self.groups = bit_groups(one_by_one)
        self.arrived = None

    def start(self):
        bits = self.groups.pop(0)
        self.arrived = [exchange(block, spread(bits, j)) for j, block in enumerate(self.blocks) if j]

    def add(self):
        arrays = [self.blocks[0]] + self.arrived
        count = 1 << len(self.groups[0]) if self.groups else 1
        rows = arrays[0].shape[-2] // count
        totals = []
        for j in range(count):
            parts = [array[..., j * rows : (j + 1) * rows, :].astype(F32) for array in arrays]
            total = functools.reduce(jnp.add, parts)
            totals.append(to_half(total) if self.groups else total)
        self.blocks = totals
        self.arrived = None

    def step(self):
        self.add()
        if self.groups:
            self.start()

    def finish(self):
        while self.groups or self.arrived is not None:
            if self.arrived is None:
                self.start()
            self.step()
        return self.blocks[0]


class Gather:
    def __init__(self, value):
        self.value = value
        self.groups = bit_groups()
        self.arrived = None

    def start(self):
        bits = self.groups.pop()
        self.arrived = [exchange(self.value, spread(bits, j)) for j in range(1, 1 << len(bits))]

    def step(self):
        if not self.groups:
            return self.value, self.arrived[0]
        self.value = jnp.concatenate([self.value] + self.arrived)
        self.start()

    def up_to_last(self):
        while len(self.groups) > 1:
            self.step()

    def finish(self):
        halves = self.step()
        while halves is None:
            halves = self.step()
        return halves


def swap(pieces):
    return lax.all_to_all(pieces, "seq", 0, 0, tiled=True)


def tie(values, *sums):
    values, arrived = lax.optimization_barrier((values, [s.arrived for s in sums]))
    for s, a in zip(sums, arrived):
        s.arrived = a
    return values


def per_device(
    enc_input,
    dec_input,
    targets,
    lengths,
    attention_mats,
    expand_mats,
    reduce_mats,
    action_head,
    query_pos,
    vectors,
    expand_bias,
    *moments,
):
    ranks = lax.axis_size("seq")
    seq_index = lax.axis_index("seq")
    items, enc_part, width = enc_input.shape
    dec_part = dec_input.shape[1]
    joints = targets.shape[2]
    width_ff = expand_mats.shape[2]
    shard = attention_mats.shape[1]
    bias_part = expand_bias.shape[0]
    n_query, n_vec = query_pos.shape[0], vectors.shape[0]
    vec_at = (n_query + 7) // 8 * 8
    head_at = (vec_at + n_vec + 7) // 8 * 8
    n_small = (head_at + joints + 127) // 128 * 128
    devices = width // shard
    dec_block = (dec_part + 15) // 16 * 16
    dec_rows = ranks * dec_block

    reduce_t = jnp.swapaxes(reduce_mats, 1, 2)
    half_mats = to_half(attention_mats)
    half_expand = to_half(expand_mats)
    half_reduce = to_half(reduce_t)
    small_local = to_half(
        jnp.concatenate(
            [
                pad_to(query_pos.T, shard, vec_at),
                pad_to(vectors.T, shard, head_at - vec_at),
                pad_to(action_head, shard, n_small - head_at),
            ],
            axis=1,
        )
    )
    bias_local = to_half(jnp.pad(expand_bias, (0, shard * 128 - bias_part)).reshape(shard, 128))
    att_all = Gather(jnp.concatenate([side_by_side(half_mats[0:4]), small_local, bias_local], axis=1))
    ffn_all = Gather(jnp.concatenate([half_expand[1], half_reduce[1]], axis=1))
    att_all.start()
    enc_ffn = gather(jnp.concatenate([half_expand[0], half_reduce[0]], axis=1))
    dec_mats = gather(side_by_side(half_mats[4:12]))

    assert items == ranks
    def spaced(values):
        parts = values.reshape(ranks, dec_part, values.shape[-1])
        return jnp.pad(parts, ((0, 0), (0, dec_block - dec_part), (0, 0)))

    rows_in = swap(jnp.concatenate([enc_input, spaced(dec_input)], axis=1))
    enc_x = rows_in[:, :enc_part].reshape(ranks * enc_part, width)
    dec_x = rows_in[:, enc_part:].reshape(dec_rows, width)
    target = swap(jnp.pad(spaced(targets), ((0, 0), (0, 0), (0, 128 - joints)))).reshape(dec_rows, 128)
    turn, turn_back = turn_matrices(width)
    positions = jnp.asarray(sine_table(ranks * enc_part, width))
    att_all.up_to_last()
    ffn_all.value = tie(ffn_all.value, att_all)
    enc_att = settle(*att_all.finish(), turn_back, 4 * width + n_small + 128)
    ffn_all.start()
    length = lengths[seq_index]
    row = jnp.arange(dec_rows)
    place = row % dec_block
    valid = (place < dec_part) & (row // dec_block * dec_part + place < length)
    valid = jnp.broadcast_to(valid.astype(F32)[:, None], (dec_rows, 128))

    at = 4 * width
    small = enc_att[:, at : at + n_small].T
    bias_all = enc_att[:, at + n_small :].reshape(devices, shard * 128)
    bias_all = bias_all[:, :bias_part].reshape(1, 2 * width_ff).astype(F32)
    query_whole = spaced(small[:n_query].astype(F32)).reshape(dec_rows, width)
    vec = pad_to(small[vec_at : vec_at + n_vec].astype(F32), (n_vec + 7) // 8 * 8, width)
    head_t = pad_to(small[head_at : head_at + joints], 128, width)
    query, keys, values, mixed, log_total = attend(enc_x, positions, enc_att, vec)
    block = 640 if width_ff % 640 == 0 else width_ff
    query, keys, values, mixed, log_total, target, valid, query_whole, head_t, dec_x = tie(
        (query, keys, values, mixed, log_total, target, valid, query_whole, head_t, dec_x), ffn_all
    )
    ffn_all.step()
    sum_one, hidden, u, sum_two, memory = tie(
        feed_forward(mixed, enc_x, enc_att, vec, enc_ffn, bias_all[:, :width_ff]), ffn_all
    )
    ffn_all.up_to_last()
    memory, in_t, x_t, mixed_t, hidden_t = tie((memory, *lefts(enc_x, positions, mixed, hidden, turn)), ffn_all)
    dec_ffn = settle(*ffn_all.finish(), turn_back, block)
    (
        w_keep, w_send, f_keep, f_send,
        dec_in_grad, query_grad, memory_grad, dec_vec_grads, head_grad_t, dec_bias_grad,
    ) = decode(
        dec_x, query_whole, target, valid, dec_mats, dec_ffn, head_t, vec, bias_all[:, width_ff:], memory, positions, turn,
        (dec_part, dec_block), joints,
    )
    dec_f, dec_att = Sum([f_keep, f_send], True), Sum([w_keep, w_send], True)
    dec_f.start()
    dec_att.start()
    two_grad, half_t, vec_grads_c = tie(last_norm_back(memory_grad, sum_two, vec, turn), dec_f, dec_att)
    dec_f.step()
    keep, send, one_grad, mixed_grad, vec_grads_b, enc_bias_grad, att_held = tie(
        [
            *feed_back(two_grad, half_t, sum_one, hidden_t, mixed_t, u, enc_att, enc_ffn, vec),
            (dec_att.blocks, dec_att.arrived),
        ],
        dec_f,
    )
    dec_att.blocks, dec_att.arrived = att_held
    enc_ffn_sum = Sum([keep, send], True)
    enc_ffn_sum.start()
    dec_f.step()
    dec_att.step()

    def back(so_far, first, count, grads):
        return attend_back(
            query, keys, values, mixed, mixed_grad, log_total, in_t, x_t, so_far, enc_att, first, count, grads
        )

    pairs = HEADS // 2
    keep, send, so_far, vec_grads_d = tie(back(one_grad, 0, 1, ()), enc_ffn_sum)
    enc_ffn_sum.add()
    so_far, enc_ffn_sum.blocks = tie((so_far, enc_ffn_sum.blocks), dec_f, dec_att)
    enc_ffn_sum.start()
    dec_f.step()
    dec_att.step()
    keep, send, so_far, vec_grads_e = tie(back(so_far, 1, pairs - 2, (keep, send)), dec_f, dec_att)
    dec_ffn_total = dec_f.finish()
    dec_att.step()
    dec_grad = swap(dec_in_grad.reshape(ranks, dec_block, width))[:, :dec_part]
    vec_grads = jnp.concatenate([vec_grads_b[:3], vec_grads_c[:3], dec_vec_grads[: n_vec - 8]])
    small_rows = jnp.concatenate(
        [
            pad_to(query_grad.reshape(ranks, dec_block, width)[:, :dec_part].reshape(n_query, width), vec_at + 2, width),
            pad_to(vec_grads, head_at - vec_at - 2, width),
            pad_to(head_grad_t[:joints], n_small - head_at, width),
        ]
    )
    bias_grad = jnp.concatenate([enc_bias_grad, dec_bias_grad], axis=1).reshape(devices, bias_part)
    bias_grad = pad_to(bias_grad, devices, shard * 128).reshape(width, 128)
    small_grad = to_half(
        jnp.concatenate([mm_t(turn, to_half(small_rows)), mm(turn, to_half(bias_grad))], axis=1)
    )
    keep, send, enc_grad, vec_grads_f, small_grad, dec_grad = tie(
        [*back(so_far, pairs - 1, 1, (keep, send)), small_grad, dec_grad], dec_att, enc_ffn_sum
    )
    dec_att_total = dec_att.finish()
    enc_grad = swap(enc_grad.reshape(ranks, enc_part, width))
    enc_ffn_sum.step()
    late_rows = jnp.concatenate([vec_grads_d[:2], vec_grads_e[:2], vec_grads_f[:2]], axis=1)
    late_grad = to_half(mm_t(turn, to_half(pad_to(late_rows, 128, width))))
    half = width // 2
    last = Sum(
        [
            jnp.concatenate([keep, small_grad[:half], late_grad[:half]], axis=1),
            jnp.concatenate([send, small_grad[half:], late_grad[half:]], axis=1),
        ]
    )
    last.start()
    dec_att_total = tie(dec_att_total, last)
    last.step()
    dec_ffn_total = tie(dec_ffn_total, enc_ffn_sum)
    enc_ffn_sum.step()
    dec_ffn_total, enc_grad = tie((dec_ffn_total, enc_grad), last, enc_ffn_sum)
    enc_ffn_total, last_total = enc_ffn_sum.finish(), last.finish()
    outputs = [enc_grad, dec_grad]

    small_total = last_total[:, 3 * width :]
    gradients = (
        jnp.stack(
            [last_total[:, i * width : (i + 1) * width] for i in range(3)]
            + [enc_ffn_total[:, 2 * width_ff :]]
            + [dec_att_total[:, i * width : (i + 1) * width] for i in range(8)]
        ),
        jnp.stack([enc_ffn_total[:, :width_ff], dec_ffn_total[:, :width_ff]]),
        jnp.stack([enc_ffn_total[:, width_ff : 2 * width_ff], dec_ffn_total[:, width_ff:]]),
        small_total[:, head_at : head_at + joints],
        small_total[:, :n_query],
        jnp.concatenate(
            [small_total[:, n_small + 128 : n_small + 130], small_total[:, vec_at + 2 : vec_at + n_vec]], axis=1
        ),
        small_total[:, n_small : n_small + 128].reshape(1, -1)[:, :bias_part],
    )

    def views(mats, expand, reduce, head, query, vector, bias):
        return (mats, expand, jnp.swapaxes(reduce, 1, 2), head, query.T, vector.T, bias.reshape(1, -1))

    weights = views(attention_mats, expand_mats, reduce_mats, action_head, query_pos, vectors, expand_bias)
    firsts, seconds = views(*moments[:7]), views(*moments[7:])
    rates = (rate_matrix,) * 4 + (rate_vector,) * 3
    for i, results in enumerate(update(list(zip(weights, gradients, firsts, seconds)), rates)):
        if i == 2:
            results = [jnp.swapaxes(value, 1, 2) for value in results]
        if i in (4, 5):
            results = [value.T for value in results]
        if i == 6:
            results = [value.reshape(-1) for value in results]
        outputs.extend(results)
    return tuple(outputs)


def solution(mesh):
    rows = P("dp", "seq", None)
    weight_specs = (
        P(None, ALL, None),
        P(None, ALL, None),
        P(None, None, ALL),
        P(ALL, None),
        P(None, ALL),
        P(None, ALL),
        P(ALL),
    )
    in_specs = (rows, rows, rows, P("dp")) + weight_specs * 3
    out_specs = (rows, rows) + tuple(spec for spec in weight_specs for unused in range(4))
    return jax.shard_map(
        per_device, mesh=mesh, in_specs=in_specs, out_specs=out_specs, check_vma=False
    )
```
